32 devices in a mesh: dom: 4 (over y, core), head: 8 (over z, x).
Axes of the slice: x: 2, y: 2, z: 4, core: 2. Of those that a mesh axis runs over, the one named last changes fastest.
Arguments:
- atoms: bfloat16 [4, 8192, 1024], P('dom', 'head'), may hold values from -6 to 6
- bonds: int32 [4, 4, 8192], P('dom', None, 'head'), may hold values from 0 to 1279
- triplets: int32 [4, 4, 8192], P('dom', None, 'head'), may hold values from 0 to 1279
- halo_ids: int32 [4, 1024], P('dom', 'head'), may hold values from 0 to 1023
- counts: int32 [4, 64], P('dom', 'head'), may hold values from 0 to 256, as said below
- enc_weight: bfloat16 [1024, 1024], replicated, may hold values from -0.1875 to 0.1875
- gate_gain: float32 [1024], replicated, may hold values from -8 to 8
- head_weight: bfloat16 [8, 2, 1024, 1024], P('head', None, 'dom'), may hold values from -0.1875 to 0.1875
Outputs:
- row_grads: bfloat16 [4, 8192, 1024], P('dom', 'head')
- head_grads: float32 [8, 2, 1024, 1024], P('head', None, 'dom')
The draws below stay inside these ranges and needn't reach their ends.
Inputs may be any that keep to these rules, and one draw needn't show every extreme that they name: `counts`: each entry is a multiple of 128 and at most 256, reached on some device in every draw; the 8 entries of one device sum to 1024; within one partition the entries of one dataset sum to at most 2048, and some dataset reaches that in every partition. `bonds`: entry (b, i) names a row of atom i's device's extended rows: its own 1024 rows, then the cut-bond rows of the previous partition, then those of the next. `triplets`: indexed like bonds. `halo_ids`: rows of the device itself.
All inputs are finite; a program needn't handle non-finite values.
Results may differ from the reference program's by a relative error of at most 0.0095.
Values may be sent and summed in bfloat16 or wider, within the bound.
No kernel may reach another device: no remote copies, remote signals or barrier semaphores. Data moves between devices by JAX's collectives and lax.ppermute only.
A program may use at most 128 MiB of HBM per device.

```python
import math
import jax
import jax.numpy as jnp
from jax import lax

D = 1024
BLOCK = 128
BLOCKS_DEV = 8
LOADED = 8
NBOND = 4
HALO = 128
HEAD_LAYERS = 2
PARTS_SIZE = 4
GROUP = 8
DATASETS = 8
ROWS_DEV = 1024
PART_ROWS = 8192


def draw_counts(key, part):

    def one_partition(sub_key):
        order_key, heavy_key = jax.random.split(jax.random.fold_in(sub_key, 17))
        order = jax.random.permutation(order_key, GROUP).astype(jnp.int32)
        heavy = jax.random.randint(heavy_key, (), 0, DATASETS).astype(jnp.int32)
        position = jnp.argsort(order).astype(jnp.int32)
        loaded = (position < LOADED).astype(jnp.int32)
        remain = BLOCKS_DEV - 2 * loaded
        remain_ordered = remain[order]
        start_ordered = jnp.cumsum(remain_ordered) - remain_ordered
        start = start_ordered[position]
        steps_ahead = jnp.arange(BLOCKS_DEV, dtype=jnp.int32)
        sequence = start[:, None] + steps_ahead[None, :]
        live = steps_ahead[None, :] < remain[:, None]
        target = sequence % (DATASETS - 1)
        target = target + (target >= heavy).astype(jnp.int32)
        datasets = jnp.arange(DATASETS, dtype=jnp.int32)
        hits = jnp.logical_and(target[:, :, None] == datasets[None, None, :], live[:, :, None])
        blocks = jnp.sum(hits.astype(jnp.int32), axis=1)
        blocks = blocks + 2 * loaded[:, None] * (datasets[None, :] == heavy).astype(jnp.int32)
        return (blocks * BLOCK).astype(jnp.int32)
    part_keys = jax.random.split(key, PARTS_SIZE)
    table = jax.vmap(one_partition)(part_keys)
    return table.reshape(PARTS_SIZE, GROUP * DATASETS)


def plant(values, stream_key, least, high):
    spot = [jax.random.randint(jax.random.fold_in(stream_key, axis), (), 0, length) for axis, length in enumerate(values.shape)]
    main_axis = values.shape.index(max(values.shape))
    neighbour = spot[:main_axis] + [(spot[main_axis] + 1) % values.shape[main_axis]] + spot[main_axis + 1:]
    return values.at[tuple(spot)].set(least).at[tuple(neighbour)].set(high)


def levels(rng, shape, shards, least, high):
    def one(dim, shards_of):
        draws = jax.random.uniform(jax.random.fold_in(jax.random.fold_in(rng, 6), dim), (shards_of,), jnp.float32, least / len(shards), high / len(shards))
        return jnp.repeat(jnp.exp(draws), shape[dim] // shards_of).reshape((-1,) + (1,) * (len(shape) - dim - 1))

    factor_of = one(*shards[0])
    for cut in shards[1:]:
        factor_of = factor_of * one(*cut)
    return factor_of


def noise(key, extent, spread, most, cuts=(), kind=jnp.bfloat16):
    loudness = levels(key, extent, cuts, -0.22, 0.18) if cuts else 1.0
    result = jax.random.normal(key, extent, jnp.float32) * spread * loudness
    return jnp.minimum(jnp.maximum(result, -most), most).astype(kind)


def setup_inputs(seed: int = 0) -> dict:
    key_list = jax.random.split(jax.random.key(seed), 9)
    return {
        "atoms": noise(key_list[0], (PARTS_SIZE, PART_ROWS, D), 1.0, 6.0, ((0, 4), (1, 8))),
        "bonds": plant(jax.random.randint(key_list[1], (PARTS_SIZE, NBOND, PART_ROWS), 0, ROWS_DEV + 2 * HALO), jax.random.fold_in(key_list[1], 1), 0, (ROWS_DEV + 2 * HALO) - 1).astype(jnp.int32),
        "triplets": plant(jax.random.randint(key_list[2], (PARTS_SIZE, NBOND, PART_ROWS), 0, ROWS_DEV + 2 * HALO), jax.random.fold_in(key_list[2], 1), 0, (ROWS_DEV + 2 * HALO) - 1).astype(jnp.int32),
        "halo_ids": plant(jax.random.randint(key_list[3], (PARTS_SIZE, GROUP * HALO), 0, ROWS_DEV), jax.random.fold_in(key_list[3], 1), 0, ROWS_DEV - 1).astype(jnp.int32),
        "counts": draw_counts(jax.random.fold_in(key_list[8], 71), 0),
        "enc_weight": noise(key_list[5], (D, D), D ** -0.5, 0.1875),
        "gate_gain": noise(key_list[6], (D,), 2.0, 8.0, (), jnp.float32),
        "head_weight": noise(key_list[7], (DATASETS, HEAD_LAYERS, D, D), D ** -0.5, 0.1875, ((0, 8), (2, 4))),
    }


def encode_rows(extended, atom_rows, bond_ids, partner_ids, enc_weight, gate_gain):
    bonded = jnp.take(extended, bond_ids, axis=0)
    partner = jnp.take(extended, partner_ids, axis=0)
    logits = lax.optimization_barrier(jnp.sum(bonded.astype(jnp.float32) * partner.astype(jnp.float32) * gate_gain, axis=-1)) / math.sqrt(extended.shape[1])
    gates = jax.nn.sigmoid(logits)
    message = lax.optimization_barrier(jnp.sum(gates[..., None] * bonded.astype(jnp.float32), axis=0)).astype(jnp.bfloat16)
    update = jnp.dot(message, enc_weight, preferred_element_type=jnp.float32)
    return (atom_rows.astype(jnp.float32) + jax.nn.silu(update)).astype(jnp.bfloat16)

def silu_slope(preact):
    sigma = jax.nn.sigmoid(preact)
    return sigma * (1.0 + preact * (1.0 - sigma))

def head_block(block_rows, weights):
    activations = [block_rows]
    preacts = []
    current = block_rows
    for layer_id in range(HEAD_LAYERS):
        preact = jnp.dot(current, weights[layer_id], preferred_element_type=jnp.float32)
        preacts.append(preact)
        if layer_id < HEAD_LAYERS - 1:
            current = jax.nn.silu(preact).astype(jnp.bfloat16)
            activations.append(current)
    residue = preacts[-1] - block_rows.astype(jnp.float32)
    gradient = residue.astype(jnp.bfloat16)
    layer_terms = []
    upward = residue
    for layer_id in reversed(range(HEAD_LAYERS)):
        layer_terms.append(lax.dot_general(activations[layer_id], gradient, (((0,), (0,)), ((), ())), preferred_element_type=jnp.float32))
        upward = lax.dot_general(gradient, weights[layer_id], (((1,), (1,)), ((), ())), preferred_element_type=jnp.float32)
        if layer_id > 0:
            gradient = (upward * silu_slope(preacts[layer_id - 1])).astype(jnp.bfloat16)
    ordered_terms = layer_terms[::-1]
    return ((upward - residue).astype(jnp.bfloat16), jnp.stack(ordered_terms))

def reference(atoms, bonds, triplets, halo_ids, counts, enc_weight, gate_gain, head_weight):
    devices = PARTS_SIZE * GROUP
    per_device = atoms.reshape(PARTS_SIZE, GROUP, ROWS_DEV, D)
    chosen = halo_ids.reshape(PARTS_SIZE, GROUP, HALO)
    cut_rows = jnp.take_along_axis(per_device, chosen[..., None], axis=2)
    zero_part = jnp.zeros_like(cut_rows[:1])
    before = jnp.concatenate([zero_part, cut_rows[:-1]], axis=0).reshape(devices, HALO, D)
    after = jnp.concatenate([cut_rows[1:], zero_part], axis=0).reshape(devices, HALO, D)
    flat_rows = per_device.reshape(devices, ROWS_DEV, D)
    bond_flat = bonds.reshape(PARTS_SIZE, NBOND, GROUP, ROWS_DEV).transpose(0, 2, 1, 3).reshape(devices, NBOND, ROWS_DEV)
    angle_flat = triplets.reshape(PARTS_SIZE, NBOND, GROUP, ROWS_DEV).transpose(0, 2, 1, 3).reshape(devices, NBOND, ROWS_DEV)

    def one_device(items):
        own, prior, later, bond_ids, partner_ids = items
        extended = jnp.concatenate([own, prior, later], axis=0)
        return encode_rows(extended, own, bond_ids, partner_ids, enc_weight, gate_gain)
    features = lax.map(one_device, (flat_rows, before, after, bond_flat, angle_flat))
    block_counts = counts.reshape(devices, DATASETS) // BLOCK
    inclusive = jnp.cumsum(block_counts, axis=1)
    block_ids = jnp.arange(BLOCKS_DEV, dtype=jnp.int32)
    block_sets = lax.optimization_barrier(jnp.sum((inclusive[:, None, :] <= block_ids[None, :, None]).astype(jnp.int32), axis=-1)).astype(jnp.int32)
    blocks = features.reshape(devices * BLOCKS_DEV, BLOCK, D)

    def step(totals, items):
        block_rows, set_id = items
        row_part, layer_terms = head_block(block_rows, head_weight[set_id])
        return (totals.at[set_id].add(layer_terms), row_part)
    start = jnp.zeros((DATASETS, HEAD_LAYERS, D, D), jnp.float32)
    totals, row_parts = lax.scan(step, start, (blocks, block_sets.reshape(-1)))
    head_grads = totals * (1.0 / math.sqrt(PARTS_SIZE * ROWS_DEV))
    return (row_parts.reshape(PARTS_SIZE, PART_ROWS, D), head_grads)
```

```python
import functools
import math

import jax
import jax.numpy as jnp
from jax import lax
from jax.experimental import pallas as pl
from jax.experimental.pallas import tpu as pltpu
from jax.sharding import PartitionSpec as P

BLOCK = 128
PAIR = 2 * BLOCK
LANES = 128
MB = 1 << 20
F32 = jnp.float32
BF16 = jnp.bfloat16


def sigmoid(x):
    return 1.0 / (1.0 + jnp.exp(-x))


def resident(shape):
    return pl.BlockSpec(shape, lambda *_: (0,) * len(shape))


def pick_kernel(ids_ref, rows_ref, out_ref):
    count, total = out_ref.shape[0], rows_ref.shape[0]
    places = lax.broadcasted_iota(jnp.int32, (count, total), 1)
    ones = jnp.where(places == ids_ref[...], 1.0, 0.0).astype(BF16)
    out_ref[...] = jnp.dot(ones, rows_ref[...], preferred_element_type=F32).astype(BF16)


def pick_rows(rows, ids):
    return pl.pallas_call(
        pick_kernel,
        out_shape=jax.ShapeDtypeStruct((ids.shape[0], rows.shape[1]), rows.dtype),
        compiler_params=pltpu.CompilerParams(vmem_limit_bytes=24 * MB),
        name="pick_rows",
    )(ids[:, None], rows)


def step_source(counts_ref, step, extra, sets):
    zero = jnp.int32(0)

    def scan(dataset, carry):
        start, seen, source, live = carry
        blocks = counts_ref[0, dataset] // BLOCK
        double = blocks > 1
        is_second = jnp.logical_and(double, seen == step)
        is_first = jnp.logical_and(blocks > 0, dataset + extra == step)
        source = jnp.where(is_second, start + 1, jnp.where(is_first, start, source))
        live = jnp.where(jnp.logical_or(is_second, is_first), 1, live)
        return start + blocks, seen + jnp.where(double, 1, 0), source, live

    carry = (zero, zero, zero, zero)
    for dataset in range(sets):
        carry = scan(dataset, carry)
    return carry[2], carry[3]


def encode_kernel(
    extra, bond_count, unroll, counts_ref, codes_ref, atoms_ref, low_ref, high_ref, weight_ref,
    gain_ref, second_ref, first_ref, plain, gained, products, gates, mixed, message,
):
    step = pl.program_id(0)
    rows, width = atoms_ref.shape
    depth = low_ref.shape[0]
    tall = width // LANES
    sets = first_ref.shape[0] if False else counts_ref.shape[1]

    @pl.when(step == 0)
    def _():
        def spread(ref, at, base):
            for k in range(tall):
                lanes = slice(k * LANES, (k + 1) * LANES)
                value = ref[pl.ds(at, BLOCK), lanes].astype(F32)
                place = pl.ds(base * tall + k, BLOCK, stride=tall)
                plain[place, :] = value
                gained[place, :] = value * gain_ref[:, lanes]

        for at in range(0, rows, BLOCK):
            spread(atoms_ref, at, at)
        for at in range(0, depth, BLOCK):
            spread(low_ref, at, rows + at)
            spread(high_ref, at, rows + depth + at)

    source, live = step_source(counts_ref, step, extra, sets)
    base = pl.multiple_of(source * BLOCK, BLOCK)

    def row_of(ref, place):
        return ref[pl.ds(pl.multiple_of(place, tall), tall), :]

    def encode():
        def score(outer, carry):
            for inner in range(unroll):
                atom = outer * unroll + inner
                for bond in range(bond_count):
                    code = codes_ref[bond * rows + base + atom]
                    bonded = row_of(plain, code >> 16)
                    partner = row_of(gained, code & 0xFFFF)
                    place = pl.multiple_of((atom * bond_count + bond) * tall, tall)
                    products[pl.ds(place, tall), :] = bonded * partner
            return carry

        lax.fori_loop(0, BLOCK // unroll, score, 0)
        pairs = BLOCK * bond_count
        total = products[pl.ds(0, pairs, stride=tall), :]
        for k in range(1, tall):
            total = total + products[pl.ds(k, pairs, stride=tall), :]
        logits = jnp.sum(total, axis=1, keepdims=True) * (1.0 / math.sqrt(width))
        gates[...] = jnp.broadcast_to(sigmoid(logits), gates.shape)

        def mix(outer, carry):
            for inner in range(unroll):
                atom = outer * unroll + inner
                acc = None
                for bond in range(bond_count):
                    code = codes_ref[bond * rows + base + atom]
                    gate = gates[pl.ds(atom * bond_count + bond, 1), :]
                    term = row_of(plain, code >> 16) * gate
                    acc = term if acc is None else acc + term
                mixed[pl.ds(pl.multiple_of(atom * tall, tall), tall), :] = acc
            return carry

        lax.fori_loop(0, BLOCK // unroll, mix, 0)
        for k in range(tall):
            part = mixed[pl.ds(k, BLOCK, stride=tall), :]
            message[:, k * LANES : (k + 1) * LANES] = part.astype(BF16)
        update = jnp.dot(message[...], weight_ref[...], preferred_element_type=F32)
        own = atoms_ref[pl.ds(base, BLOCK), :].astype(F32)
        return (own + update * sigmoid(update)).astype(BF16)

    def emit(out_ref):
        @pl.when(live == 1)
        def _():
            out_ref[0] = encode()

        @pl.when(live == 0)
        def _():
            out_ref[...] = jnp.zeros_like(out_ref)

    pl.when(step < extra)(lambda: emit(second_ref))
    pl.when(step >= extra)(lambda: emit(first_ref))


def encode(counts, codes, atoms, low, high, weight, gain, bond_count):
    rows, width = atoms.shape
    depth = low.shape[0]
    sets = counts.shape[1]
    extra = rows // PAIR
    tall = width // LANES
    extended = rows + 2 * depth
    kernel = functools.partial(encode_kernel, extra, bond_count, 4)
    block = (1, BLOCK, width)
    return pl.pallas_call(
        kernel,
        grid_spec=pltpu.PrefetchScalarGridSpec(
            num_scalar_prefetch=2,
            grid=(extra + sets,),
            in_specs=[
                resident((rows, width)),
                resident((depth, width)),
                resident((depth, width)),
                resident((width, width)),
                resident((1, width)),
            ],
            out_specs=[
                pl.BlockSpec(block, lambda t, *_: (jnp.minimum(t, extra - 1), 0, 0)),
                pl.BlockSpec(block, lambda t, *_: (jnp.maximum(t - extra, 0), 0, 0)),
            ],
            scratch_shapes=[
                pltpu.VMEM((extended * tall, LANES), F32),
                pltpu.VMEM((extended * tall, LANES), F32),
                pltpu.VMEM((BLOCK * bond_count * tall, LANES), F32),
                pltpu.VMEM((BLOCK * bond_count, LANES), F32),
                pltpu.VMEM((BLOCK * tall, LANES), F32),
                pltpu.VMEM((BLOCK, width), BF16),
            ],
        ),
        out_shape=[
            jax.ShapeDtypeStruct((extra, BLOCK, width), BF16),
            jax.ShapeDtypeStruct((sets, BLOCK, width), BF16),
        ],
        compiler_params=pltpu.CompilerParams(vmem_limit_bytes=48 * MB),
        name="encode_rows",
    )(counts, codes, atoms, low, high, weight, gain)


def head_kernel(masked, keep_ref, rows_ref, weight_ref, *outs):
    step = pl.program_id(0)
    blocks, _, width = rows_ref.shape
    if masked:
        x_ref, back_ref, sent_ref, act_ref, low_grad_ref, high_grad_ref = outs
        for b in range(blocks):
            live = keep_ref[0, step * blocks + b] == 1
            x_ref[b] = jnp.where(live, rows_ref[b], jnp.zeros_like(rows_ref[b]))
    else:
        back_ref, act_ref, low_grad_ref, high_grad_ref = outs
        x_ref = rows_ref
    x = x_ref[...].reshape(blocks * BLOCK, width)
    shape = x_ref.shape
    low = weight_ref[:, 0].reshape(width, width)
    high = weight_ref[:, 1].reshape(width, width)
    transposed = (((1,), (1,)), ((), ()))
    z = jnp.dot(x, low, preferred_element_type=F32)
    s = sigmoid(z)
    act = (z * s).astype(BF16)
    act_ref[...] = act.reshape(shape)
    slope = s * (1.0 + z * (1.0 - s))
    err = jnp.dot(act, high, preferred_element_type=F32) - x.astype(F32)
    grad = err.astype(BF16)
    high_grad_ref[...] = grad.reshape(shape)
    up = lax.dot_general(grad, high, transposed, preferred_element_type=F32)
    grad = (up * slope).astype(BF16)
    low_grad_ref[...] = grad.reshape(shape)
    up = lax.dot_general(grad, low, transposed, preferred_element_type=F32)
    back = (up - err).astype(BF16).reshape(shape)
    back_ref[...] = back
    if masked:
        for b in range(blocks):
            live = keep_ref[1, step * blocks + b] == 1
            sent_ref[b] = jnp.where(live, back[b], jnp.zeros_like(back[b]))


def run_head(rows, weights, keep):
    count, _, width = rows.shape
    tile = 2 if count % 2 == 0 else 1
    masked = keep is not None
    if keep is None:
        keep = jnp.zeros((2, count), jnp.int32)
    block = pl.BlockSpec((tile, BLOCK, width), lambda t, *_: (t, 0, 0))
    total = count * BLOCK
    outs = 6 if masked else 4
    return pl.pallas_call(
        functools.partial(head_kernel, masked),
        grid_spec=pltpu.PrefetchScalarGridSpec(
            num_scalar_prefetch=1,
            grid=(count // tile,),
            in_specs=[block, resident(weights.shape)],
            out_specs=[block] * outs,
        ),
        out_shape=[jax.ShapeDtypeStruct(rows.shape, BF16)] * outs,
        compiler_params=pltpu.CompilerParams(vmem_limit_bytes=48 * MB),
        cost_estimate=pl.CostEstimate(
            flops=8 * total * width * width,
            bytes_accessed=(outs + 1) * total * width * 2 + weights.size * 2,
            transcendentals=total * width,
        ),
        name="head_rows",
    )(keep, rows, weights)


def place_kernel(counts_ref, first_ref, second_ref, others_ref, out_ref):
    sets = counts_ref.shape[1]
    dataset, rank, order = block_place(counts_ref, pl.program_id(0), sets)
    from_first = rank == 0
    from_second = order == 0
    rest = jnp.where(from_second, second_ref[0], others_ref[0])
    out_ref[0] = jnp.where(from_first, first_ref[0], rest)


def block_place(counts_ref, block, sets):
    zero = jnp.int32(0)
    start, seen, dataset, rank, order = zero, zero, zero, zero, zero
    for candidate in range(sets):
        blocks = counts_ref[0, candidate] // BLOCK
        inside = jnp.logical_and(block >= start, block < start + blocks)
        dataset = jnp.where(inside, candidate, dataset)
        rank = jnp.where(inside, block - start, rank)
        order = jnp.where(inside, seen, order)
        start = start + blocks
        seen = seen + jnp.where(blocks > 1, 1, 0)
    return dataset, rank, order


def place_rows(counts, first, second, others, row_blocks):
    sets, _, width = first.shape
    shape = (1, BLOCK, width)

    def first_index(block, counts_ref):
        return block_place(counts_ref, block, sets)[0], 0, 0

    def other_index(block, counts_ref):
        dataset, rank, order = block_place(counts_ref, block, sets)
        return jnp.where(jnp.logical_and(rank > 0, order > 0), dataset, 0), 0, 0

    return pl.pallas_call(
        place_kernel,
        grid_spec=pltpu.PrefetchScalarGridSpec(
            num_scalar_prefetch=1,
            grid=(row_blocks,),
            in_specs=[
                pl.BlockSpec(shape, first_index),
                resident(shape),
                pl.BlockSpec(shape, other_index),
            ],
            out_specs=pl.BlockSpec(shape, lambda block, *_: (block, 0, 0)),
        ),
        out_shape=jax.ShapeDtypeStruct((row_blocks, BLOCK, width), BF16),
        compiler_params=pltpu.CompilerParams(vmem_limit_bytes=24 * MB),
        name="place_rows",
    )(counts, first, second, others)


def halo(cut_rows):
    count = lax.axis_size("dom")
    forward = [(i, i + 1) for i in range(count - 1)]
    backward = [(target, source) for source, target in forward]
    low = lax.ppermute(cut_rows, "dom", forward)
    high = lax.ppermute(cut_rows, "dom", backward)
    return low, high


def exchange(blocks):
    return lax.all_to_all(blocks, "head", split_axis=0, concat_axis=0, tiled=True)


def body(atoms, bonds, triplets, halo_ids, counts, enc_weight, gate_gain, head_weight):
    atom_rows = atoms[0]
    row_count, width = atom_rows.shape
    row_blocks = row_count // BLOCK
    bond_count = bonds.shape[1]
    sets = counts.shape[1]
    group = lax.axis_size("head")
    tall = width // LANES
    layers = head_weight.shape[1]

    every = lax.all_gather(counts, ("dom", "head"), axis=0, tiled=True)
    weights = lax.all_gather(head_weight[0], "dom", axis=0, tiled=False)
    low, high = halo(pick_rows(atom_rows, halo_ids[0]))
    codes = ((bonds[0] * tall) * 65536 + triplets[0] * tall).reshape(-1)
    second, first = encode(
        counts, codes, atom_rows, low, high, enc_weight, gate_gain[None, :], bond_count
    )

    doubled = every == PAIR
    order = jnp.cumsum(doubled.astype(jnp.int32), axis=1)
    more = (jnp.max(order) > 1).astype(jnp.int32)
    mine = lax.dynamic_slice_in_dim(doubled, lax.axis_index("dom") * group, group, 0)
    mine_order = lax.dynamic_slice_in_dim(order, lax.axis_index("dom") * group, group, 0)
    here = jnp.arange(sets, dtype=jnp.int32)[None, :] == lax.axis_index("head")
    has_second = jnp.any(jnp.logical_and(mine, here), axis=1)
    is_lead = jnp.any(jnp.logical_and(jnp.logical_and(mine, here), mine_order == 1), axis=1)
    keep = jnp.stack([has_second, is_lead]).astype(jnp.int32)
    own_doubled = counts[0] == PAIR
    own_order = jnp.cumsum(own_doubled.astype(jnp.int32)) - 1

    lead = lax.all_gather(second[0], "head", axis=0, tiled=False)
    arrived = exchange(first)

    def send_rest(_, held):
        picked = jnp.take(second, jnp.clip(own_order, 0, second.shape[0] - 1), axis=0)
        rest = exchange(jnp.where(own_doubled[:, None, None], picked, jnp.zeros_like(picked)))
        return jnp.where(is_lead[:, None, None], held, rest)

    seconds = lax.fori_loop(0, more, send_rest, lead)

    x_b, back_b, sent_b, act_b, low_b, high_b = run_head(seconds, weights, keep)
    returned_second = lax.psum_scatter(sent_b, "head", scatter_dimension=0, tiled=True)
    back_a, act_a, low_a, high_a = run_head(arrived, weights, None)
    returned_first = exchange(back_a)
    returned_rest = lax.fori_loop(0, more, lambda _, held: exchange(held), back_b)

    scale = 1.0 / math.sqrt(lax.axis_size("dom") * row_count)

    def share(first_acts, first_grads, second_acts, second_grads):
        def product(acts, grads):
            return lax.dot_general(
                acts.reshape(-1, width),
                grads.reshape(-1, width),
                (((0,), (0,)), ((), ())),
                preferred_element_type=F32,
            )

        total = product(second_acts, second_grads) + product(first_acts, first_grads)
        return lax.psum_scatter(
            (total * scale).astype(BF16), "dom", scatter_dimension=0, tiled=True
        ).astype(F32)

    shares = [share(act_a, high_a, act_b, high_b), share(arrived, low_a, x_b, low_b)]
    head_part = jnp.stack(shares[::-1])
    row_part = place_rows(counts, returned_first, returned_second, returned_rest, row_blocks)
    return row_part.reshape(1, row_count, width), head_part[None]


def solution(mesh):
    return jax.shard_map(
        body,
        mesh=mesh,
        in_specs=(
            P("dom", "head", None),
            P("dom", None, "head"),
            P("dom", None, "head"),
            P("dom", "head"),
            P("dom", "head"),
            P(),
            P(),
            P("head", None, "dom", None),
        ),
        out_specs=(P("dom", "head", None), P("head", None, "dom", None)),
        check_vma=False,
    )
```

```python
import functools
import math

import jax
import jax.numpy as jnp
from jax import lax
from jax.experimental import pallas as pl
from jax.experimental.pallas import tpu as pltpu
from jax.sharding import PartitionSpec as P

BLOCK = 128
LANES = 128
MB = 1 << 20
F32 = jnp.float32
BF16 = jnp.bfloat16


def sigmoid(x):
    return 1.0 / (1.0 + jnp.exp(-x))


def resident(shape):
    return pl.BlockSpec(shape, lambda *_: (0,) * len(shape))


def pick_kernel(ids_ref, rows_ref, out_ref):
    count, total = out_ref.shape[0], rows_ref.shape[0]
    places = lax.broadcasted_iota(jnp.int32, (count, total), 1)
    ones = jnp.where(places == ids_ref[...], 1.0, 0.0).astype(BF16)
    out_ref[...] = jnp.dot(ones, rows_ref[...], preferred_element_type=F32).astype(BF16)


def pick_rows(rows, ids):
    return pl.pallas_call(
        pick_kernel,
        out_shape=jax.ShapeDtypeStruct((ids.shape[0], rows.shape[1]), rows.dtype),
        compiler_params=pltpu.CompilerParams(vmem_limit_bytes=24 * MB),
        name="pick_rows",
    )(ids[:, None], rows)


def step_source(info_ref, step, half, mirror):
    sets = info_ref.shape[1] - 1
    base = info_ref[0, sets] // half * half
    dataset = lax.rem(base + (half if mirror else 0) + step // 2, sets)
    rank = lax.rem(step, 2)
    start = jnp.int32(0)
    blocks = jnp.int32(0)
    for candidate in range(sets):
        here = info_ref[0, candidate] // BLOCK
        start = start + jnp.where(candidate < dataset, here, 0)
        blocks = jnp.where(candidate == dataset, here, blocks)
    live = rank < blocks
    return jnp.where(live, start + rank, 0), live


def encode_kernel(
    half, mirror, bond_count, unroll, info_ref, codes_ref, atoms_ref, low_ref, high_ref,
    weight_ref, gain_ref, out_ref, plain, gained, products, gates, mixed, message,
):
    step = pl.program_id(0)
    rows, width = atoms_ref.shape
    depth = low_ref.shape[0]
    tall = width // LANES
    @pl.when(step == 0)
    def _():
        def spread(ref, at, base):
            for k in range(tall):
                lanes = slice(k * LANES, (k + 1) * LANES)
                value = ref[pl.ds(at, BLOCK), lanes].astype(F32)
                place = pl.ds(base * tall + k, BLOCK, stride=tall)
                plain[place, :] = value
                gained[place, :] = value * gain_ref[:, lanes]

        for at in range(0, rows, BLOCK):
            spread(atoms_ref, at, at)
        for at in range(0, depth, BLOCK):
            spread(low_ref, at, rows + at)
            spread(high_ref, at, rows + depth + at)

    source, live = step_source(info_ref, step, half, mirror)
    base = pl.multiple_of(source * BLOCK, BLOCK)

    def row_of(ref, place):
        return ref[pl.ds(pl.multiple_of(place, tall), tall), :]

    def encode():
        def score(outer, carry):
            for inner in range(unroll):
                atom = outer * unroll + inner
                for bond in range(bond_count):
                    code = codes_ref[bond * rows + base + atom]
                    bonded = row_of(plain, code >> 16)
                    partner = row_of(gained, code & 0xFFFF)
                    place = pl.multiple_of((atom * bond_count + bond) * tall, tall)
                    products[pl.ds(place, tall), :] = bonded * partner
            return carry

        lax.fori_loop(0, BLOCK // unroll, score, 0)
        pairs = BLOCK * bond_count
        total = products[pl.ds(0, pairs, stride=tall), :]
        for k in range(1, tall):
            total = total + products[pl.ds(k, pairs, stride=tall), :]
        logits = jnp.sum(total, axis=1, keepdims=True) * (1.0 / math.sqrt(width))
        gates[...] = jnp.broadcast_to(sigmoid(logits), gates.shape)

        def mix(outer, carry):
            for inner in range(unroll):
                atom = outer * unroll + inner
                acc = None
                for bond in range(bond_count):
                    code = codes_ref[bond * rows + base + atom]
                    gate = gates[pl.ds(atom * bond_count + bond, 1), :]
                    term = row_of(plain, code >> 16) * gate
                    acc = term if acc is None else acc + term
                mixed[pl.ds(pl.multiple_of(atom * tall, tall), tall), :] = acc
            return carry

        lax.fori_loop(0, BLOCK // unroll, mix, 0)
        for k in range(tall):
            part = mixed[pl.ds(k, BLOCK, stride=tall), :]
            message[:, k * LANES : (k + 1) * LANES] = part.astype(BF16)
        update = jnp.dot(message[...], weight_ref[...], preferred_element_type=F32)
        own = atoms_ref[pl.ds(base, BLOCK), :].astype(F32)
        return (own + update * sigmoid(update)).astype(BF16)

    @pl.when(live)
    def _():
        out_ref[0] = encode()

    @pl.when(jnp.logical_not(live))
    def _():
        out_ref[...] = jnp.zeros_like(out_ref)


def encode(info, codes, atoms, low, high, weight, gain, bond_count, half, mirror):
    rows, width = atoms.shape
    depth = low.shape[0]
    tall = width // LANES
    extended = rows + 2 * depth
    blocks = pl.pallas_call(
        functools.partial(encode_kernel, half, mirror, bond_count, 4),
        grid_spec=pltpu.PrefetchScalarGridSpec(
            num_scalar_prefetch=2,
            grid=(2 * half,),
            in_specs=[
                resident((rows, width)),
                resident((depth, width)),
                resident((depth, width)),
                resident((width, width)),
                resident((1, width)),
            ],
            out_specs=pl.BlockSpec((1, BLOCK, width), lambda t, *_: (t, 0, 0)),
            scratch_shapes=[
                pltpu.VMEM((extended * tall, LANES), F32),
                pltpu.VMEM((extended * tall, LANES), F32),
                pltpu.VMEM((BLOCK * bond_count * tall, LANES), F32),
                pltpu.VMEM((BLOCK * bond_count, LANES), F32),
                pltpu.VMEM((BLOCK * tall, LANES), F32),
                pltpu.VMEM((BLOCK, width), BF16),
            ],
        ),
        out_shape=jax.ShapeDtypeStruct((2 * half, BLOCK, width), BF16),
        compiler_params=pltpu.CompilerParams(vmem_limit_bytes=48 * MB),
        cost_estimate=pl.CostEstimate(
            flops=rows * width * width,
            bytes_accessed=30 * MB,
            transcendentals=rows * width,
        ),
        name="encode_mirror" if mirror else "encode_own",
    )(info, codes, atoms, low, high, weight, gain)
    return blocks.reshape(half, 2, BLOCK, width)


def head_kernel(rows_ref, weight_ref, back_ref, act_ref, low_grad_ref, high_grad_ref):
    width = rows_ref.shape[-1]
    shape = rows_ref.shape
    x = rows_ref[...].reshape(-1, width)
    some = jnp.max(jnp.abs(x.astype(F32))) > 0

    @pl.when(some)
    def _():
        low = weight_ref[:, 0].reshape(width, width)
        high = weight_ref[:, 1].reshape(width, width)
        transposed = (((1,), (1,)), ((), ()))
        z = jnp.dot(x, low, preferred_element_type=F32)
        s = sigmoid(z)
        act = (z * s).astype(BF16)
        act_ref[...] = act.reshape(shape)
        slope = s * (1.0 + z * (1.0 - s))
        err = jnp.dot(act, high, preferred_element_type=F32) - x.astype(F32)
        grad = err.astype(BF16)
        high_grad_ref[...] = grad.reshape(shape)
        up = lax.dot_general(grad, high, transposed, preferred_element_type=F32)
        grad = (up * slope).astype(BF16)
        low_grad_ref[...] = grad.reshape(shape)
        up = lax.dot_general(grad, low, transposed, preferred_element_type=F32)
        back_ref[...] = (up - err).astype(BF16).reshape(shape)

    @pl.when(jnp.logical_not(some))
    def _():
        for ref in (back_ref, act_ref, low_grad_ref, high_grad_ref):
            ref[...] = jnp.zeros_like(ref)


def run_head(rows, weights, name):
    sources, ranks, _, width = rows.shape
    tile = 4 if sources % 4 == 0 else 1
    block = pl.BlockSpec((tile, 1, BLOCK, width), lambda r, t: (t, r, 0, 0))
    total = sources * ranks * BLOCK
    return pl.pallas_call(
        head_kernel,
        grid=(ranks, sources // tile),
        in_specs=[block, resident(weights.shape)],
        out_specs=[block] * 4,
        out_shape=[jax.ShapeDtypeStruct(rows.shape, BF16)] * 4,
        compiler_params=pltpu.CompilerParams(vmem_limit_bytes=48 * MB),
        cost_estimate=pl.CostEstimate(
            flops=8 * total * width * width,
            bytes_accessed=5 * total * width * 2 + weights.size * 2,
            transcendentals=total * width,
        ),
        name=name,
    )(rows, weights)


def block_place(info_ref, block):
    sets = info_ref.shape[1] - 1
    start, dataset, rank = jnp.int32(0), jnp.int32(0), jnp.int32(0)
    for candidate in range(sets):
        blocks = info_ref[0, candidate] // BLOCK
        inside = jnp.logical_and(block >= start, block < start + blocks)
        dataset = jnp.where(inside, candidate, dataset)
        rank = jnp.where(inside, block - start, rank)
        start = start + blocks
    return dataset, rank, info_ref[0, sets]


def place_kernel(half, info_ref, own_ref, mirror_ref, out_ref):
    dataset, _, place = block_place(info_ref, pl.program_id(0))
    is_own = dataset // half == place // half
    out_ref[0] = jnp.where(is_own, own_ref[0, 0], mirror_ref[0, 0])


def place_rows(info, own, mirror, row_blocks):
    half, _, _, width = own.shape
    shape = (1, 1, BLOCK, width)

    def index(of_own, block, info_ref):
        dataset, rank, place = block_place(info_ref, block)
        wanted = (dataset // half == place // half) == of_own
        return jnp.where(wanted, lax.rem(dataset, half), 0), jnp.where(wanted, rank, 0), 0, 0

    return pl.pallas_call(
        functools.partial(place_kernel, half),
        grid_spec=pltpu.PrefetchScalarGridSpec(
            num_scalar_prefetch=1,
            grid=(row_blocks,),
            in_specs=[
                pl.BlockSpec(shape, functools.partial(index, True)),
                pl.BlockSpec(shape, functools.partial(index, False)),
            ],
            out_specs=pl.BlockSpec((1, BLOCK, width), lambda block, *_: (block, 0, 0)),
        ),
        out_shape=jax.ShapeDtypeStruct((row_blocks, BLOCK, width), BF16),
        compiler_params=pltpu.CompilerParams(vmem_limit_bytes=24 * MB),
        name="place_rows",
    )(info, own, mirror)


def halo(cut_rows):
    count = lax.axis_size("dom")
    forward = [(i, i + 1) for i in range(count - 1)]
    backward = [(target, source) for source, target in forward]
    low = lax.ppermute(cut_rows, "dom", forward)
    high = lax.ppermute(cut_rows, "dom", backward)
    return low, high


def exchange(blocks, half):
    groups = [list(range(half)), list(range(half, 2 * half))]
    return lax.all_to_all(
        blocks, "head", split_axis=0, concat_axis=0, axis_index_groups=groups, tiled=True
    )


def across(array, half):
    return lax.ppermute(array, "head", [(i, (i + half) % (2 * half)) for i in range(2 * half)])


def sum_over_dom(share):
    count = lax.axis_size("dom")
    rows, width = share.shape
    if count & (count - 1):
        return lax.psum_scatter(share, "dom", scatter_dimension=0, tiled=True).astype(F32)
    bits = count.bit_length() - 1
    place = lax.axis_index("dom")
    total = share.reshape((2,) * bits + (rows // count, width))
    for bit in range(bits):
        axis = bits - 1 - bit
        mine = (place >> bit) & 1
        keep = lax.dynamic_index_in_dim(total, mine, axis, keepdims=False)
        send = lax.dynamic_index_in_dim(total, 1 - mine, axis, keepdims=False)
        got = lax.ppermute(send, "dom", [(i, i ^ (1 << bit)) for i in range(count)])
        total = keep.astype(F32) + got.astype(F32)
        if bit < bits - 1:
            total = total.astype(BF16)
    return total


def body(atoms, bonds, triplets, halo_ids, counts, enc_weight, gate_gain, head_weight):
    atom_rows = atoms[0]
    row_count, width = atom_rows.shape
    row_blocks = row_count // BLOCK
    bond_count = bonds.shape[1]
    half = lax.axis_size("head") // 2
    tall = width // LANES

    own_weights = lax.all_gather(head_weight[0], "dom", axis=0, tiled=False)
    mirror_weights = lax.all_gather(across(head_weight[0], half), "dom", axis=0, tiled=False)
    low, high = halo(pick_rows(atom_rows, halo_ids[0]))
    codes = ((bonds[0] * tall) * 65536 + triplets[0] * tall).reshape(-1)
    place = lax.axis_index("head").astype(jnp.int32).reshape(1, 1)
    info = jnp.concatenate([counts, place], axis=1)

    def encoded(mirror):
        return encode(
            info, codes, atom_rows, low, high, enc_weight, gate_gain[None, :], bond_count, half,
            mirror,
        )

    scale = 1.0 / math.sqrt(lax.axis_size("dom") * row_count)

    def share(acts, grads):
        product = lax.dot_general(
            acts.reshape(-1, width),
            grads.reshape(-1, width),
            (((0,), (0,)), ((), ())),
            preferred_element_type=F32,
        )
        return sum_over_dom((product * scale).astype(BF16))

    own_rows = exchange(encoded(False), half)
    mirror_rows = exchange(encoded(True), half)
    own_back, own_act, own_low, own_high = run_head(own_rows, own_weights, "head_own")
    own_back = exchange(own_back, half)
    mirror_back, act, low_grad, high_grad = run_head(mirror_rows, mirror_weights, "head_mirror")
    mirror_back = exchange(mirror_back, half)
    high_part = across(share(act, high_grad).astype(BF16), half)
    low_part = across(share(mirror_rows, low_grad).astype(BF16), half)
    head_part = jnp.stack(
        [
            share(own_rows, own_low) + low_part.astype(F32),
            share(own_act, own_high) + high_part.astype(F32),
        ]
    )
    row_part = place_rows(info, own_back, mirror_back, row_blocks)
    return row_part.reshape(1, row_count, width), head_part[None]


def solution(mesh):
    return jax.shard_map(
        body,
        mesh=mesh,
        in_specs=(
            P("dom", "head", None),
            P("dom", None, "head"),
            P("dom", None, "head"),
            P("dom", "head"),
            P("dom", "head"),
            P(),
            P(),
            P("head", None, "dom", None),
        ),
        out_specs=(P("dom", "head", None), P("head", None, "dom", None)),
        check_vma=False,
    )
```

```python
import functools
import math

import jax
import jax.numpy as jnp
from jax import lax
from jax.experimental import pallas as pl
from jax.experimental.pallas import tpu as pltpu
from jax.sharding import PartitionSpec as P

BLOCK = 128
LANES = 128
MB = 1 << 20
VMEM = 58 * MB
F32 = jnp.float32
BF16 = jnp.bfloat16


def sigmoid(x):
    return 1.0 / (1.0 + jnp.exp(-x))


def resident(shape):
    return pl.BlockSpec(shape, lambda *_: (0,) * len(shape))


def pick_kernel(ids_ref, rows_ref, out_ref):
    count, total = out_ref.shape[0], rows_ref.shape[0]
    places = lax.broadcasted_iota(jnp.int32, (count, total), 1)
    ones = jnp.where(places == ids_ref[...], 1.0, 0.0).astype(BF16)
    out_ref[...] = jnp.dot(ones, rows_ref[...], preferred_element_type=F32).astype(BF16)


def pick_rows(rows, ids):
    return pl.pallas_call(
        pick_kernel,
        out_shape=jax.ShapeDtypeStruct((ids.shape[0], rows.shape[1]), rows.dtype),
        compiler_params=pltpu.CompilerParams(vmem_limit_bytes=VMEM),
        name="pick_rows",
    )(ids[:, None], rows)


def step_source(info_ref, step, half, mirror):
    sets = info_ref.shape[1] - 1
    base = info_ref[0, sets] // half * half
    dataset = lax.rem(base + (half if mirror else 0) + step // 2, sets)
    rank = lax.rem(step, 2)
    start = jnp.int32(0)
    blocks = jnp.int32(0)
    for candidate in range(sets):
        here = info_ref[0, candidate] // BLOCK
        start = start + jnp.where(candidate < dataset, here, 0)
        blocks = jnp.where(candidate == dataset, here, blocks)
    live = rank < blocks
    return jnp.where(live, start + rank, 0), live


def fold(arrays):
    rows = lax.broadcasted_iota(jnp.int32, arrays[0].shape, 0)
    for shift in (1, 2, 4):
        first = (rows & shift) == 0
        arrays = [
            jnp.where(first, a, b) + pltpu.roll(jnp.where(first, b, a), 8 - shift, 0)
            for a, b in zip(arrays[::2], arrays[1::2])
        ]
    return arrays[0]


def encode_kernel(
    half, mirror, bond_count, info_ref, codes_ref, atoms_ref, low_ref, high_ref,
    weight_ref, gain_ref, ids_ref, out_ref, plain, gained, partial, gate_rows,
):
    step = pl.program_id(0)
    rows, width = atoms_ref.shape
    depth = low_ref.shape[0]
    tall = width // LANES

    @pl.when(step == 0)
    def _():
        def spread(ref, at, base):
            for k in range(tall):
                lanes = slice(k * LANES, (k + 1) * LANES)
                value = ref[pl.ds(at, BLOCK), lanes].astype(F32)
                place = pl.ds(base * tall + k, BLOCK, stride=tall)
                plain[place, :] = value
                gained[place, :] = value * gain_ref[:, lanes]

        for at in range(0, rows, BLOCK):
            spread(atoms_ref, at, at)
        for at in range(0, depth, BLOCK):
            spread(low_ref, at, rows + at)
            spread(high_ref, at, rows + depth + at)

    source, live = step_source(info_ref, step, half, mirror)
    base = pl.multiple_of(source * BLOCK, BLOCK)

    def row_of(ref, place):
        return ref[pl.ds(pl.multiple_of(place, tall), tall), :]

    def product(code):
        value = row_of(plain, code >> 16) * row_of(gained, code & 0xFFFF)
        return sum(value[k : k + 8] for k in range(0, tall, 8))

    @pl.when(live)
    def _():
        def score(group, carry):
            for bond in range(bond_count):
                at = bond * rows + base + group * 8
                place = pl.multiple_of(bond * BLOCK + group * 8, 8)
                partial[pl.ds(place, 8), :] = fold([product(codes_ref[at + j]) for j in range(8)])
            return carry

        lax.fori_loop(0, BLOCK // 8, score, 0)
        logits = jnp.sum(partial[...], axis=1, keepdims=True) * (1.0 / math.sqrt(width))
        gates = sigmoid(logits)
        ids = ids_ref[pl.ds(base, BLOCK), :]
        total = gate_rows.shape[1]
        for at in range(0, total, LANES):
            places = lax.broadcasted_iota(jnp.int32, (BLOCK, LANES), 1) + at
            acc = jnp.zeros((BLOCK, LANES), F32)
            for bond in range(bond_count):
                gate = gates[bond * BLOCK : (bond + 1) * BLOCK]
                acc = acc + jnp.where(places == ids[:, bond : bond + 1], gate, 0.0)
            gate_rows[:, at : at + LANES] = acc.astype(BF16)
        message = jnp.dot(gate_rows[:, :rows], atoms_ref[...], preferred_element_type=F32)
        for ref, at in ((low_ref, rows), (high_ref, rows + depth)):
            message += jnp.dot(
                gate_rows[:, at : at + depth], ref[...], preferred_element_type=F32
            )
        update = jnp.dot(message.astype(BF16), weight_ref[...], preferred_element_type=F32)
        own = atoms_ref[pl.ds(base, BLOCK), :].astype(F32)
        out_ref[0] = (own + update * sigmoid(update)).astype(BF16)

    @pl.when(jnp.logical_not(live))
    def _():
        out_ref[...] = jnp.zeros_like(out_ref)


def encode(info, codes, atoms, low, high, weight, gain, ids, half, mirror):
    rows, width = atoms.shape
    depth = low.shape[0]
    tall = width // LANES
    extended = rows + 2 * depth
    bond_count = ids.shape[1]
    blocks = pl.pallas_call(
        functools.partial(encode_kernel, half, mirror, bond_count),
        grid_spec=pltpu.PrefetchScalarGridSpec(
            num_scalar_prefetch=2,
            grid=(2 * half,),
            in_specs=[
                resident((rows, width)),
                resident((depth, width)),
                resident((depth, width)),
                resident((width, width)),
                resident((1, width)),
                resident((rows, bond_count)),
            ],
            out_specs=pl.BlockSpec((1, BLOCK, width), lambda t, *_: (t, 0, 0)),
            scratch_shapes=[
                pltpu.VMEM((extended * tall, LANES), F32),
                pltpu.VMEM((extended * tall, LANES), F32),
                pltpu.VMEM((BLOCK * bond_count, LANES), F32),
                pltpu.VMEM((BLOCK, extended), BF16),
            ],
        ),
        out_shape=jax.ShapeDtypeStruct((2 * half, BLOCK, width), BF16),
        compiler_params=pltpu.CompilerParams(vmem_limit_bytes=VMEM),
        cost_estimate=pl.CostEstimate(
            flops=rows * width * width,
            bytes_accessed=30 * MB,
            transcendentals=rows * width,
        ),
        name="encode_mirror" if mirror else "encode_own",
    )(info, codes, atoms, low, high, weight, gain, ids)
    return blocks.reshape(half, 2, BLOCK, width)


def head_kernel(rows_ref, low_ref, high_ref, back_ref, act_ref, low_grad_ref, high_grad_ref):
    width = rows_ref.shape[-1]
    shape = rows_ref.shape
    x = rows_ref[...].reshape(-1, width)
    some = jnp.max(jnp.abs(x.astype(F32))) > 0

    @pl.when(some)
    def _():
        low = low_ref[...].reshape(width, width)
        high = high_ref[...].reshape(width, width)
        transposed = (((1,), (1,)), ((), ()))
        z = jnp.dot(x, low, preferred_element_type=F32)
        s = sigmoid(z)
        act = (z * s).astype(BF16)
        act_ref[...] = act.reshape(shape)
        slope = s * (1.0 + z * (1.0 - s))
        err = jnp.dot(act, high, preferred_element_type=F32) - x.astype(F32)
        grad = err.astype(BF16)
        high_grad_ref[...] = grad.reshape(shape)
        up = lax.dot_general(grad, high, transposed, preferred_element_type=F32)
        grad = (up * slope).astype(BF16)
        low_grad_ref[...] = grad.reshape(shape)
        up = lax.dot_general(grad, low, transposed, preferred_element_type=F32)
        back_ref[...] = (up - err).astype(BF16).reshape(shape)

    @pl.when(jnp.logical_not(some))
    def _():
        for ref in (back_ref, act_ref, low_grad_ref, high_grad_ref):
            ref[...] = jnp.zeros_like(ref)


def run_head(rows, weights, name):
    sources, ranks, _, width = rows.shape
    tile = 4 if sources % 4 == 0 else 1
    block = pl.BlockSpec((tile, 1, BLOCK, width), lambda r, t: (t, r, 0, 0))
    total = sources * ranks * BLOCK
    return pl.pallas_call(
        head_kernel,
        grid=(ranks, sources // tile),
        in_specs=[block] + [resident(w.shape) for w in weights],
        out_specs=[block] * 4,
        out_shape=[jax.ShapeDtypeStruct(rows.shape, BF16)] * 4,
        compiler_params=pltpu.CompilerParams(vmem_limit_bytes=VMEM),
        cost_estimate=pl.CostEstimate(
            flops=8 * total * width * width,
            bytes_accessed=5 * total * width * 2 + width * width * 4,
            transcendentals=total * width,
        ),
        name=name,
    )(rows, *weights)


def block_place(info_ref, block):
    sets = info_ref.shape[1] - 1
    start, dataset, rank = jnp.int32(0), jnp.int32(0), jnp.int32(0)
    for candidate in range(sets):
        blocks = info_ref[0, candidate] // BLOCK
        inside = jnp.logical_and(block >= start, block < start + blocks)
        dataset = jnp.where(inside, candidate, dataset)
        rank = jnp.where(inside, block - start, rank)
        start = start + blocks
    return dataset, rank, info_ref[0, sets]


def place_kernel(half, info_ref, own_ref, mirror_ref, out_ref, sems):
    def moves(block, act):
        dataset, rank, place = block_place(info_ref, block)
        is_own = dataset // half == place // half

        def one(ref):
            source = ref.at[lax.rem(dataset, half), rank]
            act(pltpu.make_async_copy(source, out_ref.at[block], sems.at[block]))

        pl.when(is_own)(lambda: one(own_ref))
        pl.when(jnp.logical_not(is_own))(lambda: one(mirror_ref))

    for block in range(out_ref.shape[0]):
        moves(block, lambda copy: copy.start())
    for block in range(out_ref.shape[0]):
        moves(block, lambda copy: copy.wait())


def place_rows(info, own, mirror, row_blocks):
    half, _, _, width = own.shape
    anywhere = pl.BlockSpec(memory_space=pl.ANY)
    return pl.pallas_call(
        functools.partial(place_kernel, half),
        grid_spec=pltpu.PrefetchScalarGridSpec(
            num_scalar_prefetch=1,
            grid=(1,),
            in_specs=[anywhere, anywhere],
            out_specs=anywhere,
            scratch_shapes=[pltpu.SemaphoreType.DMA((row_blocks,))],
        ),
        out_shape=jax.ShapeDtypeStruct((row_blocks, BLOCK, width), BF16),
        compiler_params=pltpu.CompilerParams(vmem_limit_bytes=VMEM),
        name="place_rows",
    )(info, own, mirror)


def halo(cut_rows):
    count = lax.axis_size("dom")
    forward = [(i, i + 1) for i in range(count - 1)]
    backward = [(target, source) for source, target in forward]
    low = lax.ppermute(cut_rows, "dom", forward)
    high = lax.ppermute(cut_rows, "dom", backward)
    return low, high


def exchange(blocks, half):
    groups = [list(range(half)), list(range(half, 2 * half))]
    return lax.all_to_all(
        blocks, "head", split_axis=0, concat_axis=0, axis_index_groups=groups, tiled=True
    )


def across(array, half):
    return lax.ppermute(array, "head", [(i, (i + half) % (2 * half)) for i in range(2 * half)])


def after(value, *others):
    return lax.optimization_barrier((value,) + others)[0]


def sum_steps(share):
    count = lax.axis_size("dom")
    rows, width = share.shape
    bits = count.bit_length() - 1
    place = lax.axis_index("dom")
    total = share.reshape((2,) * bits + (rows // count, width))
    for bit in range(bits):
        axis = bits - 1 - bit
        mine = (place >> bit) & 1
        keep = lax.dynamic_index_in_dim(total, mine, axis, keepdims=False)
        send = lax.dynamic_index_in_dim(total, 1 - mine, axis, keepdims=False)
        yield send
        got = lax.ppermute(send, "dom", [(i, i ^ (1 << bit)) for i in range(count)])
        total = keep.astype(F32) + got.astype(F32)
        if bit < bits - 1:
            total = total.astype(BF16)
    yield total


def sum_over_dom(share):
    return list(sum_steps(share))


def body(atoms, bonds, triplets, halo_ids, counts, enc_weight, gate_gain, head_weight):
    atom_rows = atoms[0]
    row_count, width = atom_rows.shape
    row_blocks = row_count // BLOCK
    half = lax.axis_size("head") // 2
    tall = width // LANES

    def gather(shard):
        return lax.all_gather(shard, "dom", axis=0, tiled=False)

    shard = head_weight[0]
    own_weights = [gather(shard[0]), gather(shard[1])]
    low, high = halo(pick_rows(atom_rows, halo_ids[0]))
    far_low = across(shard[0], half)
    codes = ((bonds[0] * tall) * 65536 + triplets[0] * tall).reshape(-1)
    ids = bonds[0].T
    place = lax.axis_index("head").astype(jnp.int32).reshape(1, 1)
    info = jnp.concatenate([counts, place], axis=1)
    gain = gate_gain[None, :]

    def encoded(info, mirror):
        return encode(info, codes, atom_rows, low, high, enc_weight, gain, ids, half, mirror)

    scale = 1.0 / math.sqrt(lax.axis_size("dom") * row_count)

    def share(acts, grads):
        product = lax.dot_general(
            acts.reshape(-1, width),
            grads.reshape(-1, width),
            (((0,), (0,)), ((), ())),
            preferred_element_type=F32,
        )
        return (product * scale).astype(BF16)

    own_blocks = encoded(info, False)
    own_rows = exchange(own_blocks, half)
    far_high = across(after(shard[1], far_low, own_blocks), half)
    mirror_low = gather(after(far_low, own_blocks))
    mirror_blocks = encoded(after(info, own_blocks), True)
    mirror_rows = exchange(mirror_blocks, half)
    mirror_high = gather(after(far_high, mirror_blocks))

    back, act, low_grad, high_grad = run_head(own_rows, own_weights, "head_own")
    own_back = exchange(back, half)
    own_high_sum = sum_over_dom(share(act, high_grad))
    own_low_sum = sum_over_dom(share(own_rows, low_grad))

    mirror_rows = after(mirror_rows, own_high_sum[-2], own_low_sum[-2])
    back, act, low_grad, high_grad = run_head(
        mirror_rows, [mirror_low, mirror_high], "head_mirror"
    )
    high_share = share(act, high_grad)
    low_share = share(mirror_rows, low_grad)
    high_part = across(sum_over_dom(high_share)[-1].astype(BF16), half)
    low_part = across(sum_over_dom(low_share)[-1].astype(BF16), half)
    mirror_back = exchange(after(back, high_share), half)
    row_part = place_rows(info, own_back, mirror_back, row_blocks)
    low_part, high_part, row_part = lax.optimization_barrier((low_part, high_part, row_part))
    head_part = jnp.stack(
        [own_low_sum[-1] + low_part.astype(F32), own_high_sum[-1] + high_part.astype(F32)]
    )
    return row_part.reshape(1, row_count, width), head_part[None]


def solution(mesh):
    return jax.shard_map(
        body,
        mesh=mesh,
        in_specs=(
            P("dom", "head", None),
            P("dom", None, "head"),
            P("dom", None, "head"),
            P("dom", "head"),
            P("dom", "head"),
            P(),
            P(),
            P("head", None, "dom", None),
        ),
        out_specs=(P("dom", "head", None), P("head", None, "dom", None)),
        check_vma=False,
    )
```

```python
import functools
import math

import jax
import jax.numpy as jnp
from jax import lax
from jax.experimental import pallas as pl
from jax.experimental.pallas import tpu as pltpu
from jax.sharding import PartitionSpec as P

BLOCK = 128
LANES = 128
MB = 1 << 20
VMEM = 58 * MB
F32 = jnp.float32
BF16 = jnp.bfloat16


def sigmoid(x):
    return 1.0 / (1.0 + jnp.exp(-x))


def resident(shape):
    return pl.BlockSpec(shape, lambda *_: (0,) * len(shape))


def pick_kernel(ids_ref, rows_ref, out_ref):
    count, total = out_ref.shape[0], rows_ref.shape[0]
    places = lax.broadcasted_iota(jnp.int32, (count, total), 1)
    ones = jnp.where(places == ids_ref[...], 1.0, 0.0).astype(BF16)
    out_ref[...] = jnp.dot(ones, rows_ref[...], preferred_element_type=F32).astype(BF16)


def pick_rows(rows, ids):
    return pl.pallas_call(
        pick_kernel,
        out_shape=jax.ShapeDtypeStruct((ids.shape[0], rows.shape[1]), rows.dtype),
        compiler_params=pltpu.CompilerParams(vmem_limit_bytes=VMEM),
        name="pick_rows",
    )(ids[:, None], rows)


def block_source(info_ref, dataset, rank):
    start = jnp.int32(0)
    blocks = jnp.int32(0)
    for candidate in range(info_ref.shape[1] - 1):
        here = info_ref[0, candidate] // BLOCK
        start = start + jnp.where(candidate < dataset, here, 0)
        blocks = jnp.where(candidate == dataset, here, blocks)
    live = rank < blocks
    return jnp.where(live, start + rank, 0), live


def fold(arrays):
    rows = lax.broadcasted_iota(jnp.int32, arrays[0].shape, 0)
    for shift in (1, 2, 4):
        first = (rows & shift) == 0
        arrays = [
            jnp.where(first, a, b) + pltpu.roll(jnp.where(first, b, a), 8 - shift, 0)
            for a, b in zip(arrays[::2], arrays[1::2])
        ]
    return arrays[0]


def encode_kernel(
    half, info_ref, codes_ref, atoms_ref, low_ref, high_ref, weight_ref, gain_ref, ids_ref,
    own_ref, mirror_ref, plain, gained, partial, gate_rows, staged, sems,
):
    rows, width = atoms_ref.shape
    depth = low_ref.shape[0]
    tall = width // LANES
    bond_count = ids_ref.shape[1]
    sets = 2 * half
    home = info_ref[0, sets] // half * half

    def leave(slot, act):
        def one(ref, at):
            act(pltpu.make_async_copy(staged.at[slot], ref.at[at], sems.at[slot]))

        pl.when(slot < sets)(lambda: one(own_ref, slot))
        pl.when(slot >= sets)(lambda: one(mirror_ref, slot - sets))

    def spread(ref, at, base):
        for k in range(tall):
            lanes = slice(k * LANES, (k + 1) * LANES)
            value = ref[pl.ds(at, BLOCK), lanes].astype(F32)
            place = pl.ds(base * tall + k, BLOCK, stride=tall)
            plain[place, :] = value
            gained[place, :] = value * gain_ref[:, lanes]

    for at in range(0, rows, BLOCK):
        spread(atoms_ref, at, at)
    for at in range(0, depth, BLOCK):
        spread(low_ref, at, rows + at)
        spread(high_ref, at, rows + depth + at)

    def row_of(ref, place):
        return ref[pl.ds(pl.multiple_of(place, tall), tall), :]

    def product(code):
        value = row_of(plain, code >> 16) * row_of(gained, code & 0xFFFF)
        return sum(value[k : k + 8] for k in range(0, tall, 8))

    def encode_block(source, slot):
        base = pl.multiple_of(source * BLOCK, BLOCK)

        def score(group, carry):
            for bond in range(bond_count):
                at = bond * rows + base + group * 8
                place = pl.multiple_of(bond * BLOCK + group * 8, 8)
                partial[pl.ds(place, 8), :] = fold([product(codes_ref[at + j]) for j in range(8)])
            return carry

        lax.fori_loop(0, BLOCK // 8, score, 0)
        logits = jnp.sum(partial[...], axis=1, keepdims=True) * (1.0 / math.sqrt(width))
        gates = sigmoid(logits)
        ids = ids_ref[pl.ds(base, BLOCK), :]
        for at in range(0, gate_rows.shape[1], LANES):
            places = lax.broadcasted_iota(jnp.int32, (BLOCK, LANES), 1) + at
            acc = jnp.zeros((BLOCK, LANES), F32)
            for bond in range(bond_count):
                gate = gates[bond * BLOCK : (bond + 1) * BLOCK]
                acc = acc + jnp.where(places == ids[:, bond : bond + 1], gate, 0.0)
            gate_rows[:, at : at + LANES] = acc.astype(BF16)
        message = jnp.dot(gate_rows[:, :rows], atoms_ref[...], preferred_element_type=F32)
        for ref, at in ((low_ref, rows), (high_ref, rows + depth)):
            message += jnp.dot(
                gate_rows[:, at : at + depth], ref[...], preferred_element_type=F32
            )
        update = jnp.dot(message.astype(BF16), weight_ref[...], preferred_element_type=F32)
        own = atoms_ref[pl.ds(base, BLOCK), :].astype(F32)
        staged[slot] = (own + update * sigmoid(update)).astype(BF16)

    def one(slot, carry):
        dataset = lax.rem(home + slot // 2, sets)
        source, live = block_source(info_ref, dataset, lax.rem(slot, 2))
        pl.when(live)(lambda: encode_block(source, slot))

        @pl.when(jnp.logical_not(live))
        def _():
            staged[slot] = jnp.zeros(staged.shape[1:], BF16)

        leave(slot, lambda copy: copy.start())
        return carry

    def settle(slot, carry):
        leave(slot, lambda copy: copy.wait())
        return carry

    lax.fori_loop(0, 2 * sets, one, 0)
    lax.fori_loop(0, 2 * sets, settle, 0)


def encode(info, codes, atoms, low, high, weight, gain, ids, half):
    rows, width = atoms.shape
    depth = low.shape[0]
    tall = width // LANES
    extended = rows + 2 * depth
    bond_count = ids.shape[1]
    slots = 4 * half
    blocks = pl.pallas_call(
        functools.partial(encode_kernel, half),
        grid_spec=pltpu.PrefetchScalarGridSpec(
            num_scalar_prefetch=2,
            grid=(1,),
            in_specs=[
                resident((rows, width)),
                resident((depth, width)),
                resident((depth, width)),
                resident((width, width)),
                resident((1, width)),
                resident((rows, bond_count)),
            ],
            out_specs=[pl.BlockSpec(memory_space=pltpu.HBM)] * 2,
            scratch_shapes=[
                pltpu.VMEM((extended * tall, LANES), F32),
                pltpu.VMEM((extended * tall, LANES), F32),
                pltpu.VMEM((BLOCK * bond_count, LANES), F32),
                pltpu.VMEM((BLOCK, extended), BF16),
                pltpu.VMEM((slots, BLOCK, width), BF16),
                pltpu.SemaphoreType.DMA((slots,)),
            ],
        ),
        out_shape=[pltpu.HBM((2 * half, BLOCK, width), BF16)] * 2,
        compiler_params=pltpu.CompilerParams(vmem_limit_bytes=40 * MB),
        cost_estimate=pl.CostEstimate(
            flops=40 * rows * width * width,
            bytes_accessed=30 * MB,
            transcendentals=rows * width,
        ),
        name="encode_rows",
    )(info, codes, atoms, low, high, weight, gain, ids)
    return [rows.reshape(half, 2, BLOCK, width) for rows in blocks]


def head_kernel(sizes, scale, table_ref, rows_ref, *refs):
    pieces = refs[: len(sizes)]
    back_ref, send_ref, keep_ref, weights, totals, sems = refs[len(sizes) :]
    width = rows_ref.shape[-1]
    shape = rows_ref.shape
    count = weights.shape[1]
    first = jnp.logical_and(pl.program_id(0) == 0, pl.program_id(1) == 0)
    last = jnp.logical_and(
        pl.program_id(0) == pl.num_programs(0) - 1, pl.program_id(1) == pl.num_programs(1) - 1
    )

    def loads(act):
        shard = 0
        for ref, size in zip(pieces, sizes):
            for i in range(size):
                for layer in range(2):
                    place = weights.at[layer, table_ref[shard]]
                    act(pltpu.make_async_copy(ref.at[i, layer], place, sems.at[layer, shard]))
                shard += 1

    @pl.when(first)
    def _():
        loads(lambda copy: copy.start())
        loads(lambda copy: copy.wait())

    x = rows_ref[...].reshape(-1, width)
    some = jnp.logical_or(first, jnp.max(jnp.abs(x.astype(F32))) > 0)

    @pl.when(some)
    def _():
        low = weights[0].reshape(width, width)
        high = weights[1].reshape(width, width)
        transposed = (((1,), (1,)), ((), ()))
        over_rows = (((0,), (0,)), ((), ()))

        def add(layer, acts, grads):
            value = lax.dot_general(acts, grads, over_rows, preferred_element_type=F32)
            value = value.reshape(totals.shape[1:])

            @pl.when(first)
            def _():
                totals[layer] = value

            @pl.when(jnp.logical_not(first))
            def _():
                totals[layer] += value

        z = jnp.dot(x, low, preferred_element_type=F32)
        s = sigmoid(z)
        act = (z * s).astype(BF16)
        slope = s * (1.0 + z * (1.0 - s))
        err = jnp.dot(act, high, preferred_element_type=F32) - x.astype(F32)
        grad = err.astype(BF16)
        add(1, act, grad)
        up = lax.dot_general(grad, high, transposed, preferred_element_type=F32)
        grad = (up * slope).astype(BF16)
        add(0, x, grad)
        up = lax.dot_general(grad, low, transposed, preferred_element_type=F32)
        back_ref[...] = (up - err).astype(BF16).reshape(shape)

    @pl.when(jnp.logical_not(some))
    def _():
        back_ref[...] = jnp.zeros_like(back_ref)

    @pl.when(last)
    def _():
        bit = table_ref[count]
        for layer in range(2):
            for j in range(count // 2):
                keep_ref[layer, j] = (totals[layer, 2 * j + bit] * scale).astype(BF16)
                send_ref[layer, j] = (totals[layer, 2 * j + 1 - bit] * scale).astype(BF16)


def run_head(rows, pieces, places, scale, name):
    sources, ranks, _, width = rows.shape
    count = lax.axis_size("dom")
    depth = width // count
    tile = 4 if sources % 4 == 0 else 1
    block = pl.BlockSpec((tile, 1, BLOCK, width), lambda r, t, *_: (t, r, 0, 0))
    total = sources * ranks * BLOCK
    sizes = [piece.shape[0] for piece in pieces]
    part = (2, count // 2, depth, width)
    bit = lax.axis_index("dom").astype(jnp.int32) & 1
    return pl.pallas_call(
        functools.partial(head_kernel, sizes, scale),
        grid_spec=pltpu.PrefetchScalarGridSpec(
            num_scalar_prefetch=1,
            grid=(ranks, sources // tile),
            in_specs=[block] + [pl.BlockSpec(memory_space=pltpu.HBM)] * len(pieces),
            out_specs=[block, resident(part), resident(part)],
            scratch_shapes=[
                pltpu.VMEM((2, count, depth, width), BF16),
                pltpu.VMEM((2, count, depth, width), F32),
                pltpu.SemaphoreType.DMA((2, count)),
            ],
        ),
        out_shape=[
            jax.ShapeDtypeStruct(rows.shape, BF16),
            jax.ShapeDtypeStruct(part, BF16),
            jax.ShapeDtypeStruct(part, BF16),
        ],
        compiler_params=pltpu.CompilerParams(vmem_limit_bytes=VMEM),
        cost_estimate=pl.CostEstimate(
            flops=24 * total * width * width,
            bytes_accessed=5 * total * width * 2 + width * width * 4,
            transcendentals=total * width,
        ),
        name=name,
    )(jnp.stack(places + [bit]).astype(jnp.int32), rows, *pieces)


def block_place(info_ref, block):
    sets = info_ref.shape[1] - 1
    start, dataset, rank = jnp.int32(0), jnp.int32(0), jnp.int32(0)
    for candidate in range(sets):
        blocks = info_ref[0, candidate] // BLOCK
        inside = jnp.logical_and(block >= start, block < start + blocks)
        dataset = jnp.where(inside, candidate, dataset)
        rank = jnp.where(inside, block - start, rank)
        start = start + blocks
    return dataset, rank, info_ref[0, sets]


def place_kernel(half, info_ref, own_ref, mirror_ref, out_ref):
    dataset, _, place = block_place(info_ref, pl.program_id(0))
    is_own = dataset // half == place // half
    out_ref[0] = jnp.where(is_own, own_ref[0, 0], mirror_ref[0, 0])


def place_rows(info, own, mirror, row_blocks):
    half, _, _, width = own.shape
    shape = (1, 1, BLOCK, width)

    def index(of_own, block, info_ref):
        dataset, rank, place = block_place(info_ref, block)
        wanted = (dataset // half == place // half) == of_own
        return jnp.where(wanted, lax.rem(dataset, half), 0), jnp.where(wanted, rank, 0), 0, 0

    return pl.pallas_call(
        functools.partial(place_kernel, half),
        grid_spec=pltpu.PrefetchScalarGridSpec(
            num_scalar_prefetch=1,
            grid=(row_blocks,),
            in_specs=[
                pl.BlockSpec(shape, functools.partial(index, True)),
                pl.BlockSpec(shape, functools.partial(index, False)),
            ],
            out_specs=pl.BlockSpec((1, BLOCK, width), lambda block, *_: (block, 0, 0)),
        ),
        out_shape=jax.ShapeDtypeStruct((row_blocks, BLOCK, width), BF16),
        compiler_params=pltpu.CompilerParams(vmem_limit_bytes=16 * MB),
        name="place_rows",
    )(info, own, mirror)


def halo(cut_rows):
    count = lax.axis_size("dom")
    forward = [(i, i + 1) for i in range(count - 1)]
    backward = [(target, source) for source, target in forward]
    low = lax.ppermute(cut_rows, "dom", forward)
    high = lax.ppermute(cut_rows, "dom", backward)
    return low, high


def exchange(blocks, half):
    groups = [list(range(half)), list(range(half, 2 * half))]
    return lax.all_to_all(
        blocks, "head", split_axis=0, concat_axis=0, axis_index_groups=groups, tiled=True
    )


def across(array, half):
    return lax.ppermute(array, "head", [(i, (i + half) % (2 * half)) for i in range(2 * half)])


def after(value, *others):
    return lax.optimization_barrier((value,) + others)[0]


def swap(array, bit):
    count = lax.axis_size("dom")
    return lax.ppermute(array, "dom", [(i, i ^ (1 << bit)) for i in range(count)])


def spread_over_dom(shard):
    place = lax.axis_index("dom").astype(jnp.int32)
    pieces, places = [shard], [place]
    for bit in reversed(range(lax.axis_size("dom").bit_length() - 1)):
        pieces += [swap(piece, bit) for piece in pieces]
        places += [there ^ (1 << bit) for there in places]
    return pieces, places


def merge_kernel(bit_ref, keep_ref, got_ref, send_ref, kept_ref):
    bit = bit_ref[0]
    for layer in range(keep_ref.shape[0]):
        for j in range(kept_ref.shape[1]):
            for out_ref, at in ((kept_ref, 2 * j + bit), (send_ref, 2 * j + 1 - bit)):
                total = keep_ref[layer, at].astype(F32) + got_ref[layer, at].astype(F32)
                out_ref[layer, j] = total.astype(BF16)


def merge(keep, got, bit, first, layers):
    _, count, depth, width = keep.shape
    mine = (lax.axis_index("dom").astype(jnp.int32) >> bit) & 1
    part = pl.BlockSpec((layers, count, depth, width), lambda t, *_: (first // layers, 0, 0, 0))
    shape = (layers, count // 2, depth, width)
    return pl.pallas_call(
        merge_kernel,
        grid_spec=pltpu.PrefetchScalarGridSpec(
            num_scalar_prefetch=1,
            grid=(1,),
            in_specs=[part, part],
            out_specs=[resident(shape)] * 2,
        ),
        out_shape=[jax.ShapeDtypeStruct(shape, BF16)] * 2,
        compiler_params=pltpu.CompilerParams(vmem_limit_bytes=20 * MB),
        name="merge_shares",
    )(mine.reshape(1), keep, got)


def sum_over_dom(send, keep, got, first, layers):
    bits = lax.axis_size("dom").bit_length() - 1
    for bit in range(1, bits):
        send, keep = merge(keep, got, bit, first, layers)
        got = swap(send, bit)
        first = 0
    return keep[:, 0], got[:, 0], send


def total_kernel(*refs):
    *terms, out_ref = refs
    for layer in range(out_ref.shape[0]):
        acc = None
        for ref, at in terms_of(terms, layer):
            value = ref[at].astype(F32)
            acc = value if acc is None else acc + value
        out_ref[layer] = acc


def terms_of(terms, layer):
    keep, got, low, high = terms
    return [(keep, layer), (got, layer), ((low, high)[layer], 0)]


def total(keep, got, low, high):
    return pl.pallas_call(
        total_kernel,
        out_shape=jax.ShapeDtypeStruct(keep.shape, F32),
        compiler_params=pltpu.CompilerParams(vmem_limit_bytes=20 * MB),
        name="total_shares",
    )(keep, got, low, high)


def body(atoms, bonds, triplets, halo_ids, counts, enc_weight, gate_gain, head_weight):
    atom_rows = atoms[0]
    row_count, width = atom_rows.shape
    row_blocks = row_count // BLOCK
    half = lax.axis_size("head") // 2
    tall = width // LANES

    shard = head_weight[0]
    count = lax.axis_size("dom")
    own_weights = lax.all_gather(shard, "dom", axis=0, tiled=False)
    far = across(head_weight, half)
    low, high = halo(pick_rows(atom_rows, halo_ids[0]))
    codes = ((bonds[0] * tall) * 65536 + triplets[0] * tall).reshape(-1)
    place = lax.axis_index("head").astype(jnp.int32).reshape(1, 1)
    info = jnp.concatenate([counts, place], axis=1)
    own_blocks, mirror_blocks = encode(
        info, codes, atom_rows, low, high, enc_weight, gate_gain[None, :], bonds[0].T, half
    )
    own_rows = exchange(own_blocks, half)
    mirror_rows = exchange(mirror_blocks, half)
    far_pieces, far_places = spread_over_dom(far)

    scale = 1.0 / math.sqrt(count * row_count)
    orders = [jnp.int32(i) for i in range(count)]
    back, send, keep = run_head(own_rows, [own_weights], orders, scale, "head_own")
    own_back = exchange(back, half)
    own_keep, own_got, own_sent = sum_over_dom(send, keep, swap(send, 0), 0, 2)

    mirror_rows = after(mirror_rows, own_sent)
    back, send, keep = run_head(mirror_rows, far_pieces, far_places, scale, "head_mirror")
    got = swap(send, 0)
    high_keep, high_got, high_sent = sum_over_dom(send, keep, got, 1, 1)
    low_keep, low_got, low_sent = sum_over_dom(send, keep, got, 0, 1)
    mirror_back = exchange(after(back, high_sent, low_sent), half)
    high_part = across((high_keep.astype(F32) + high_got.astype(F32)).astype(BF16), half)
    low_part = across((low_keep.astype(F32) + low_got.astype(F32)).astype(BF16), half)
    row_part = place_rows(info, own_back, mirror_back, row_blocks)
    head_part = total(own_keep, own_got, low_part, after(high_part, row_part))
    return row_part.reshape(1, row_count, width), head_part[None]


def solution(mesh):
    return jax.shard_map(
        body,
        mesh=mesh,
        in_specs=(
            P("dom", "head", None),
            P("dom", None, "head"),
            P("dom", None, "head"),
            P("dom", "head"),
            P("dom", "head"),
            P(),
            P(),
            P("head", None, "dom", None),
        ),
        out_specs=(P("dom", "head", None), P("head", None, "dom", None)),
        check_vma=False,
    )
```

```python
import functools
import math

import jax
import jax.numpy as jnp
from jax import lax
from jax.experimental import pallas as pl
from jax.experimental.pallas import tpu as pltpu
from jax.sharding import PartitionSpec as P

BLOCK = 128
LANES = 128
MB = 1 << 20
VMEM = 58 * MB
F32 = jnp.float32
BF16 = jnp.bfloat16


def sigmoid(x):
    return 1.0 / (1.0 + jnp.exp(-x))


def resident(shape):
    return pl.BlockSpec(shape, lambda *_: (0,) * len(shape))


def pick_kernel(ids_ref, rows_ref, out_ref):
    count, total = out_ref.shape[0], rows_ref.shape[0]
    places = lax.broadcasted_iota(jnp.int32, (count, total), 1)
    ones = jnp.where(places == ids_ref[...], 1.0, 0.0).astype(BF16)
    out_ref[...] = jnp.dot(ones, rows_ref[...], preferred_element_type=F32).astype(BF16)


def pick_rows(rows, ids):
    return pl.pallas_call(
        pick_kernel,
        out_shape=jax.ShapeDtypeStruct((ids.shape[0], rows.shape[1]), rows.dtype),
        compiler_params=pltpu.CompilerParams(vmem_limit_bytes=VMEM),
        name="pick_rows",
    )(ids[:, None], rows)


def block_source(info_ref, dataset, rank):
    start = jnp.int32(0)
    blocks = jnp.int32(0)
    for candidate in range(info_ref.shape[1] - 1):
        here = info_ref[0, candidate] // BLOCK
        start = start + jnp.where(candidate < dataset, here, 0)
        blocks = jnp.where(candidate == dataset, here, blocks)
    live = rank < blocks
    return jnp.where(live, start + rank, 0), live


def fold(arrays):
    rows = lax.broadcasted_iota(jnp.int32, arrays[0].shape, 0)
    for shift in (1, 2, 4):
        first = (rows & shift) == 0
        arrays = [
            jnp.where(first, a, b) + pltpu.roll(jnp.where(first, b, a), 8 - shift, 0)
            for a, b in zip(arrays[::2], arrays[1::2])
        ]
    return arrays[0]


def encode_kernel(
    half, info_ref, codes_ref, atoms_ref, low_ref, high_ref, weight_ref, gain_ref, ids_ref,
    own_ref, mirror_ref, plain, gained, partial, gate_rows, staged, sems,
):
    rows, width = atoms_ref.shape
    depth = low_ref.shape[0]
    tall = width // LANES
    bond_count = ids_ref.shape[1]
    sets = 2 * half
    home = info_ref[0, sets] // half * half

    def leave(slot, act):
        def one(ref, at):
            act(pltpu.make_async_copy(staged.at[slot], ref.at[at], sems.at[slot]))

        pl.when(slot < sets)(lambda: one(own_ref, slot))
        pl.when(slot >= sets)(lambda: one(mirror_ref, slot - sets))

    def spread(ref, at, base):
        for k in range(tall):
            lanes = slice(k * LANES, (k + 1) * LANES)
            value = ref[pl.ds(at, BLOCK), lanes].astype(F32)
            place = pl.ds(base * tall + k, BLOCK, stride=tall)
            plain[place, :] = value
            gained[place, :] = value * gain_ref[:, lanes]

    for at in range(0, rows, BLOCK):
        spread(atoms_ref, at, at)
    for at in range(0, depth, BLOCK):
        spread(low_ref, at, rows + at)
        spread(high_ref, at, rows + depth + at)

    def row_of(ref, place):
        return ref[pl.ds(pl.multiple_of(place, tall), tall), :]

    def product(code):
        value = row_of(plain, code >> 16) * row_of(gained, code & 0xFFFF)
        return sum(value[k : k + 8] for k in range(0, tall, 8))

    def encode_block(source, slot):
        base = pl.multiple_of(source * BLOCK, BLOCK)

        def score(group, carry):
            for bond in range(bond_count):
                at = bond * rows + base + group * 8
                place = pl.multiple_of(bond * BLOCK + group * 8, 8)
                partial[pl.ds(place, 8), :] = fold([product(codes_ref[at + j]) for j in range(8)])
            return carry

        lax.fori_loop(0, BLOCK // 8, score, 0)
        logits = jnp.sum(partial[...], axis=1, keepdims=True) * (1.0 / math.sqrt(width))
        gates = sigmoid(logits)
        ids = ids_ref[pl.ds(base, BLOCK), :]
        for at in range(0, gate_rows.shape[1], LANES):
            places = lax.broadcasted_iota(jnp.int32, (BLOCK, LANES), 1) + at
            acc = jnp.zeros((BLOCK, LANES), F32)
            for bond in range(bond_count):
                gate = gates[bond * BLOCK : (bond + 1) * BLOCK]
                acc = acc + jnp.where(places == ids[:, bond : bond + 1], gate, 0.0)
            gate_rows[:, at : at + LANES] = acc.astype(BF16)
        message = jnp.dot(gate_rows[:, :rows], atoms_ref[...], preferred_element_type=F32)
        for ref, at in ((low_ref, rows), (high_ref, rows + depth)):
            message += jnp.dot(
                gate_rows[:, at : at + depth], ref[...], preferred_element_type=F32
            )
        update = jnp.dot(message.astype(BF16), weight_ref[...], preferred_element_type=F32)
        own = atoms_ref[pl.ds(base, BLOCK), :].astype(F32)
        staged[slot] = (own + update * sigmoid(update)).astype(BF16)

    def one(slot, carry):
        dataset = lax.rem(home + slot // 2, sets)
        source, live = block_source(info_ref, dataset, lax.rem(slot, 2))
        pl.when(live)(lambda: encode_block(source, slot))

        @pl.when(jnp.logical_not(live))
        def _():
            staged[slot] = jnp.zeros(staged.shape[1:], BF16)

        leave(slot, lambda copy: copy.start())
        return carry

    def settle(slot, carry):
        leave(slot, lambda copy: copy.wait())
        return carry

    lax.fori_loop(0, 2 * sets, one, 0)
    lax.fori_loop(0, 2 * sets, settle, 0)


def encode(info, codes, atoms, low, high, weight, gain, ids, half):
    rows, width = atoms.shape
    depth = low.shape[0]
    tall = width // LANES
    extended = rows + 2 * depth
    bond_count = ids.shape[1]
    slots = 4 * half
    blocks = pl.pallas_call(
        functools.partial(encode_kernel, half),
        grid_spec=pltpu.PrefetchScalarGridSpec(
            num_scalar_prefetch=2,
            grid=(1,),
            in_specs=[
                resident((rows, width)),
                resident((depth, width)),
                resident((depth, width)),
                resident((width, width)),
                resident((1, width)),
                resident((rows, bond_count)),
            ],
            out_specs=[pl.BlockSpec(memory_space=pltpu.HBM)] * 2,
            scratch_shapes=[
                pltpu.VMEM((extended * tall, LANES), F32),
                pltpu.VMEM((extended * tall, LANES), F32),
                pltpu.VMEM((BLOCK * bond_count, LANES), F32),
                pltpu.VMEM((BLOCK, extended), BF16),
                pltpu.VMEM((slots, BLOCK, width), BF16),
                pltpu.SemaphoreType.DMA((slots,)),
            ],
        ),
        out_shape=[pltpu.HBM((2 * half, BLOCK, width), BF16)] * 2,
        compiler_params=pltpu.CompilerParams(vmem_limit_bytes=40 * MB),
        cost_estimate=pl.CostEstimate(
            flops=40 * rows * width * width,
            bytes_accessed=30 * MB,
            transcendentals=rows * width,
        ),
        name="encode_rows",
    )(info, codes, atoms, low, high, weight, gain, ids)
    return [rows.reshape(half, 2, BLOCK, width) for rows in blocks]


def head_kernel(sizes, scale, table_ref, rows_ref, *refs):
    pieces = refs[: len(sizes)]
    back_ref, send_ref, keep_ref, weights, totals, sems = refs[len(sizes) :]
    width = rows_ref.shape[-1]
    shape = rows_ref.shape
    count = weights.shape[1]
    first = jnp.logical_and(pl.program_id(0) == 0, pl.program_id(1) == 0)
    last = jnp.logical_and(
        pl.program_id(0) == pl.num_programs(0) - 1, pl.program_id(1) == pl.num_programs(1) - 1
    )

    def loads(act):
        shard = 0
        for ref, size in zip(pieces, sizes):
            for i in range(size):
                for layer in range(2):
                    place = weights.at[layer, table_ref[shard]]
                    act(pltpu.make_async_copy(ref.at[i, layer], place, sems.at[layer, shard]))
                shard += 1

    @pl.when(first)
    def _():
        loads(lambda copy: copy.start())
        loads(lambda copy: copy.wait())

    x = rows_ref[...].reshape(-1, width)
    some = jnp.logical_or(first, jnp.max(jnp.abs(x.astype(F32))) > 0)

    @pl.when(some)
    def _():
        low = weights[0].reshape(width, width)
        high = weights[1].reshape(width, width)
        transposed = (((1,), (1,)), ((), ()))
        over_rows = (((0,), (0,)), ((), ()))

        def add(layer, acts, grads):
            value = lax.dot_general(acts, grads, over_rows, preferred_element_type=F32)
            value = value.reshape(totals.shape[1:])

            @pl.when(first)
            def _():
                totals[layer] = value

            @pl.when(jnp.logical_not(first))
            def _():
                totals[layer] += value

        z = jnp.dot(x, low, preferred_element_type=F32)
        s = sigmoid(z)
        act = (z * s).astype(BF16)
        slope = s * (1.0 + z * (1.0 - s))
        err = jnp.dot(act, high, preferred_element_type=F32) - x.astype(F32)
        grad = err.astype(BF16)
        add(1, act, grad)
        up = lax.dot_general(grad, high, transposed, preferred_element_type=F32)
        grad = (up * slope).astype(BF16)
        add(0, x, grad)
        up = lax.dot_general(grad, low, transposed, preferred_element_type=F32)
        back_ref[...] = (up - err).astype(BF16).reshape(shape)

    @pl.when(jnp.logical_not(some))
    def _():
        back_ref[...] = jnp.zeros_like(back_ref)

    @pl.when(last)
    def _():
        bit = table_ref[count]
        for layer in range(2):
            for j in range(count // 2):
                keep_ref[layer, j] = (totals[layer, 2 * j + bit] * scale).astype(BF16)
                send_ref[layer, j] = (totals[layer, 2 * j + 1 - bit] * scale).astype(BF16)


def run_head(rows, pieces, places, scale, name):
    sources, ranks, _, width = rows.shape
    count = lax.axis_size("dom")
    depth = width // count
    tile = 4 if sources % 4 == 0 else 1
    block = pl.BlockSpec((tile, 1, BLOCK, width), lambda r, t, *_: (t, r, 0, 0))
    total = sources * ranks * BLOCK
    sizes = [piece.shape[0] for piece in pieces]
    part = (2, count // 2, depth, width)
    bit = lax.axis_index("dom").astype(jnp.int32) & 1
    return pl.pallas_call(
        functools.partial(head_kernel, sizes, scale),
        grid_spec=pltpu.PrefetchScalarGridSpec(
            num_scalar_prefetch=1,
            grid=(ranks, sources // tile),
            in_specs=[block] + [pl.BlockSpec(memory_space=pltpu.HBM)] * len(pieces),
            out_specs=[block, resident(part), resident(part)],
            scratch_shapes=[
                pltpu.VMEM((2, count, depth, width), BF16),
                pltpu.VMEM((2, count, depth, width), F32),
                pltpu.SemaphoreType.DMA((2, count)),
            ],
        ),
        out_shape=[
            jax.ShapeDtypeStruct(rows.shape, BF16),
            jax.ShapeDtypeStruct(part, BF16),
            jax.ShapeDtypeStruct(part, BF16),
        ],
        compiler_params=pltpu.CompilerParams(vmem_limit_bytes=44 * MB),
        cost_estimate=pl.CostEstimate(
            flops=24 * total * width * width,
            bytes_accessed=5 * total * width * 2 + width * width * 4,
            transcendentals=total * width,
        ),
        name=name,
    )(jnp.stack(places + [bit]).astype(jnp.int32), rows, *pieces)


def block_place(info_ref, block):
    sets = info_ref.shape[1] - 1
    start, dataset, rank = jnp.int32(0), jnp.int32(0), jnp.int32(0)
    for candidate in range(sets):
        blocks = info_ref[0, candidate] // BLOCK
        inside = jnp.logical_and(block >= start, block < start + blocks)
        dataset = jnp.where(inside, candidate, dataset)
        rank = jnp.where(inside, block - start, rank)
        start = start + blocks
    return dataset, rank, info_ref[0, sets]


def place_kernel(half, info_ref, own_ref, mirror_ref, out_ref):
    dataset, _, place = block_place(info_ref, pl.program_id(0))
    is_own = dataset // half == place // half
    out_ref[0] = jnp.where(is_own, own_ref[0, 0], mirror_ref[0, 0])


def place_rows(info, own, mirror, row_blocks):
    half, _, _, width = own.shape
    shape = (1, 1, BLOCK, width)

    def index(of_own, block, info_ref):
        dataset, rank, place = block_place(info_ref, block)
        wanted = (dataset // half == place // half) == of_own
        return jnp.where(wanted, lax.rem(dataset, half), 0), jnp.where(wanted, rank, 0), 0, 0

    return pl.pallas_call(
        functools.partial(place_kernel, half),
        grid_spec=pltpu.PrefetchScalarGridSpec(
            num_scalar_prefetch=1,
            grid=(row_blocks,),
            in_specs=[
                pl.BlockSpec(shape, functools.partial(index, True)),
                pl.BlockSpec(shape, functools.partial(index, False)),
            ],
            out_specs=pl.BlockSpec((1, BLOCK, width), lambda block, *_: (block, 0, 0)),
        ),
        out_shape=jax.ShapeDtypeStruct((row_blocks, BLOCK, width), BF16),
        compiler_params=pltpu.CompilerParams(vmem_limit_bytes=16 * MB),
        name="place_rows",
    )(info, own, mirror)


def halo(cut_rows):
    count = lax.axis_size("dom")
    forward = [(i, i + 1) for i in range(count - 1)]
    backward = [(target, source) for source, target in forward]
    low = lax.ppermute(cut_rows, "dom", forward)
    high = lax.ppermute(cut_rows, "dom", backward)
    return low, high


def exchange(blocks, half):
    groups = [list(range(half)), list(range(half, 2 * half))]
    return lax.all_to_all(
        blocks, "head", split_axis=0, concat_axis=0, axis_index_groups=groups, tiled=True
    )


def across(array, half):
    return lax.ppermute(array, "head", [(i, (i + half) % (2 * half)) for i in range(2 * half)])


def after(value, *others):
    return lax.optimization_barrier((value,) + others)[0]


def swap(array, bit):
    count = lax.axis_size("dom")
    return lax.ppermute(array, "dom", [(i, i ^ (1 << bit)) for i in range(count)])


def merge_kernel(bit_ref, keep_ref, got_ref, send_ref, kept_ref):
    bit = bit_ref[0]
    for layer in range(keep_ref.shape[0]):
        for j in range(kept_ref.shape[1]):
            for out_ref, at in ((kept_ref, 2 * j + bit), (send_ref, 2 * j + 1 - bit)):
                total = keep_ref[layer, at].astype(F32) + got_ref[layer, at].astype(F32)
                out_ref[layer, j] = total.astype(BF16)


def merge(keep, got, bit, first, layers):
    _, count, depth, width = keep.shape
    mine = (lax.axis_index("dom").astype(jnp.int32) >> bit) & 1
    part = pl.BlockSpec((layers, count, depth, width), lambda t, *_: (first // layers, 0, 0, 0))
    shape = (layers, count // 2, depth, width)
    return pl.pallas_call(
        merge_kernel,
        grid_spec=pltpu.PrefetchScalarGridSpec(
            num_scalar_prefetch=1,
            grid=(1,),
            in_specs=[part, part],
            out_specs=[resident(shape)] * 2,
        ),
        out_shape=[jax.ShapeDtypeStruct(shape, BF16)] * 2,
        compiler_params=pltpu.CompilerParams(vmem_limit_bytes=20 * MB),
        name="merge_shares",
    )(mine.reshape(1), keep, got)


def sum_over_dom(send, keep, got, first, layers):
    bits = lax.axis_size("dom").bit_length() - 1
    for bit in range(1, bits):
        send, keep = merge(keep, got, bit, first, layers)
        got = swap(send, bit)
        first = 0
    return keep[:, 0], got[:, 0], send


def total_kernel(*refs):
    *terms, out_ref = refs
    for layer in range(out_ref.shape[0]):
        acc = None
        for ref, at in terms_of(terms, layer):
            value = ref[at].astype(F32)
            acc = value if acc is None else acc + value
        out_ref[layer] = acc


def terms_of(terms, layer):
    keep, got, low, high = terms
    return [(keep, layer), (got, layer), ((low, high)[layer], 0)]


def total(keep, got, low, high):
    return pl.pallas_call(
        total_kernel,
        out_shape=jax.ShapeDtypeStruct(keep.shape, F32),
        compiler_params=pltpu.CompilerParams(vmem_limit_bytes=20 * MB),
        name="total_shares",
    )(keep, got, low, high)


def body(atoms, bonds, triplets, halo_ids, counts, enc_weight, gate_gain, head_weight):
    atom_rows = atoms[0]
    row_count, width = atom_rows.shape
    row_blocks = row_count // BLOCK
    half = lax.axis_size("head") // 2
    tall = width // LANES

    shard = head_weight[0]
    count = lax.axis_size("dom")
    own_weights = lax.all_gather(shard, "dom", axis=0, tiled=False)
    far = across(head_weight, half)
    low, high = halo(pick_rows(atom_rows, halo_ids[0]))
    codes = ((bonds[0] * tall) * 65536 + triplets[0] * tall).reshape(-1)
    place = lax.axis_index("head").astype(jnp.int32).reshape(1, 1)
    info = jnp.concatenate([counts, place], axis=1)
    own_blocks, mirror_blocks = encode(
        info, codes, atom_rows, low, high, enc_weight, gate_gain[None, :], bonds[0].T, half
    )
    own_rows = exchange(own_blocks, half)
    mirror_rows = exchange(mirror_blocks, half)
    mirror_weights = lax.all_gather(far[0], "dom", axis=0, tiled=False)

    scale = 1.0 / math.sqrt(count * row_count)
    orders = [jnp.int32(i) for i in range(count)]
    back, send, keep = run_head(own_rows, [own_weights], orders, scale, "head_own")
    own_back = exchange(back, half)
    own_keep, own_got, own_sent = sum_over_dom(send, keep, swap(send, 0), 0, 2)

    mirror_rows = after(mirror_rows, own_sent)
    back, send, keep = run_head(mirror_rows, [mirror_weights], orders, scale, "head_mirror")
    got = swap(send, 0)
    high_keep, high_got, high_sent = sum_over_dom(send, keep, got, 1, 1)
    low_keep, low_got, low_sent = sum_over_dom(send, keep, got, 0, 1)
    mirror_back = exchange(after(back, high_got, low_sent), half)
    high_part = across((high_keep.astype(F32) + high_got.astype(F32)).astype(BF16), half)
    low_part = across((low_keep.astype(F32) + low_got.astype(F32)).astype(BF16), half)
    row_part = place_rows(info, own_back, mirror_back, row_blocks)
    head_part = total(own_keep, own_got, low_part, after(high_part, row_part))
    return row_part.reshape(1, row_count, width), head_part[None]


def solution(mesh):
    return jax.shard_map(
        body,
        mesh=mesh,
        in_specs=(
            P("dom", "head", None),
            P("dom", None, "head"),
            P("dom", None, "head"),
            P("dom", "head"),
            P("dom", "head"),
            P(),
            P(),
            P("head", None, "dom", None),
        ),
        out_specs=(P("dom", "head", None), P("head", None, "dom", None)),
        check_vma=False,
    )
```

```python
import functools
import math

import jax
import jax.numpy as jnp
from jax import lax
from jax.experimental import pallas as pl
from jax.experimental.pallas import tpu as pltpu
from jax.sharding import PartitionSpec as P

BLOCK = 128
LANES = 128
MB = 1 << 20
VMEM = 58 * MB
F32 = jnp.float32
BF16 = jnp.bfloat16


def sigmoid(x):
    return 0.5 + 0.5 * jnp.tanh(0.5 * x)


def resident(shape):
    return pl.BlockSpec(shape, lambda *_: (0,) * len(shape))


def pick_kernel(ids_ref, rows_ref, out_ref):
    count, total = out_ref.shape[0], rows_ref.shape[0]
    places = lax.broadcasted_iota(jnp.int32, (total, count), 0)
    ones = jnp.where(places == ids_ref[...], 1.0, 0.0).astype(BF16)
    out_ref[...] = lax.dot_general(
        ones, rows_ref[...], (((0,), (0,)), ((), ())), preferred_element_type=F32
    ).astype(BF16)


def pick_rows(rows, ids):
    return pl.pallas_call(
        pick_kernel,
        out_shape=jax.ShapeDtypeStruct((ids.shape[1], rows.shape[1]), rows.dtype),
        compiler_params=pltpu.CompilerParams(vmem_limit_bytes=16 * MB),
        name="pick_rows",
    )(ids, rows)


def block_source(info_ref, dataset, rank):
    start = jnp.int32(0)
    blocks = jnp.int32(0)
    for candidate in range(info_ref.shape[1] - 1):
        here = info_ref[0, candidate] // BLOCK
        start = start + jnp.where(candidate < dataset, here, 0)
        blocks = jnp.where(candidate == dataset, here, blocks)
    live = rank < blocks
    return jnp.where(live, start + rank, 0), live


def fold(arrays):
    rows = lax.broadcasted_iota(jnp.int32, arrays[0].shape, 0)
    for shift in (1, 2, 4):
        first = (rows & shift) == 0
        arrays = [
            jnp.where(first, a, b) + pltpu.roll(jnp.where(first, b, a), 8 - shift, 0)
            for a, b in zip(arrays[::2], arrays[1::2])
        ]
    return arrays[0]


def turn(arrays):
    rows = lax.broadcasted_iota(jnp.int32, arrays[0].shape, 0)
    arrays = list(arrays)
    for shift in (1, 2, 4):
        low = (rows & shift) == 0
        for at in range(8):
            if at & shift == 0:
                a, b = arrays[at], arrays[at + shift]
                arrays[at] = jnp.where(low, a, pltpu.roll(b, shift, 0))
                arrays[at + shift] = jnp.where(low, pltpu.roll(a, 8 - shift, 0), b)
    return arrays


def encode_kernel(
    half, info_ref, codes_ref, atoms_ref, low_ref, high_ref, weight_ref, gain_ref, ids_ref,
    own_ref, mirror_ref, plain, gained, partial, gate_rows, staged, sems,
):
    rows, width = atoms_ref.shape
    depth = low_ref.shape[0]
    tall = width // LANES
    bond_count = ids_ref.shape[1]
    sets = 2 * half
    home = info_ref[0, sets] // half * half

    def leave(slot, act):
        def one(ref, at):
            act(pltpu.make_async_copy(staged.at[slot], ref.at[at], sems.at[slot]))

        pl.when(slot < sets)(lambda: one(own_ref, slot))
        pl.when(slot >= sets)(lambda: one(mirror_ref, slot - sets))

    def spread(ref, base):
        def one(group, carry):
            at = pl.multiple_of(group * 16, 16)
            for k in range(0, tall, 8):
                gains = gain_ref[k : k + 8, :]
                parts = [
                    ref[pl.ds(at, 16), (k + j) * LANES : (k + j + 1) * LANES].astype(F32)
                    for j in range(8)
                ]
                for side in (0, 8):
                    for i, row in enumerate(turn([part[side : side + 8] for part in parts])):
                        place = pl.multiple_of((base + at + side + i) * tall + k, 8)
                        plain[pl.ds(place, 8), :] = row
                        gained[pl.ds(place, 8), :] = row * gains
            return carry

        lax.fori_loop(0, ref.shape[0] // 16, one, 0)

    spread(atoms_ref, 0)
    spread(low_ref, rows)
    spread(high_ref, rows + depth)

    def row_of(ref, place):
        return ref[pl.ds(pl.multiple_of(place, tall), tall), :]

    def product(code):
        value = row_of(plain, code >> 16) * row_of(gained, code & 0xFFFF)
        return sum(value[k : k + 8] for k in range(0, tall, 8))

    def encode_block(source, slot):
        base = pl.multiple_of(source * BLOCK, BLOCK)

        def score(group, carry):
            for bond in range(bond_count):
                at = bond * rows + base + group * 8
                place = pl.multiple_of(bond * BLOCK + group * 8, 8)
                partial[pl.ds(place, 8), :] = fold([product(codes_ref[at + j]) for j in range(8)])
            return carry

        lax.fori_loop(0, BLOCK // 8, score, 0)
        logits = jnp.sum(partial[...], axis=1, keepdims=True) * (1.0 / math.sqrt(width))
        gates = sigmoid(logits)
        ids = ids_ref[pl.ds(base, BLOCK), :]
        for at in range(0, gate_rows.shape[1], LANES):
            places = lax.broadcasted_iota(jnp.int32, (BLOCK, LANES), 1) + at
            acc = jnp.zeros((BLOCK, LANES), F32)
            for bond in range(bond_count):
                gate = gates[bond * BLOCK : (bond + 1) * BLOCK]
                acc = acc + jnp.where(places == ids[:, bond : bond + 1], gate, 0.0)
            gate_rows[:, at : at + LANES] = acc.astype(BF16)
        message = jnp.dot(gate_rows[:, :rows], atoms_ref[...], preferred_element_type=F32)
        for ref, at in ((low_ref, rows), (high_ref, rows + depth)):
            message += jnp.dot(
                gate_rows[:, at : at + depth], ref[...], preferred_element_type=F32
            )
        update = jnp.dot(message.astype(BF16), weight_ref[...], preferred_element_type=F32)
        own = atoms_ref[pl.ds(base, BLOCK), :].astype(F32)
        staged[slot] = (own + update * sigmoid(update)).astype(BF16)

    def one(slot, carry):
        dataset = lax.rem(home + slot // 2, sets)
        source, live = block_source(info_ref, dataset, lax.rem(slot, 2))
        pl.when(live)(lambda: encode_block(source, slot))

        @pl.when(jnp.logical_not(live))
        def _():
            staged[slot] = jnp.zeros(staged.shape[1:], BF16)

        leave(slot, lambda copy: copy.start())
        return carry

    def settle(slot, carry):
        leave(slot, lambda copy: copy.wait())
        return carry

    lax.fori_loop(0, 2 * sets, one, 0)
    lax.fori_loop(0, 2 * sets, settle, 0)


def encode(info, codes, atoms, low, high, weight, gain, ids, half):
    rows, width = atoms.shape
    depth = low.shape[0]
    tall = width // LANES
    extended = rows + 2 * depth
    bond_count = ids.shape[1]
    slots = 4 * half
    blocks = pl.pallas_call(
        functools.partial(encode_kernel, half),
        grid_spec=pltpu.PrefetchScalarGridSpec(
            num_scalar_prefetch=2,
            grid=(1,),
            in_specs=[
                resident((rows, width)),
                resident((depth, width)),
                resident((depth, width)),
                resident((width, width)),
                resident((tall, LANES)),
                resident((rows, bond_count)),
            ],
            out_specs=[pl.BlockSpec(memory_space=pltpu.HBM)] * 2,
            scratch_shapes=[
                pltpu.VMEM((extended * tall, LANES), F32),
                pltpu.VMEM((extended * tall, LANES), F32),
                pltpu.VMEM((BLOCK * bond_count, LANES), F32),
                pltpu.VMEM((BLOCK, extended), BF16),
                pltpu.VMEM((slots, BLOCK, width), BF16),
                pltpu.SemaphoreType.DMA((slots,)),
            ],
        ),
        out_shape=[pltpu.HBM((2 * half, BLOCK, width), BF16)] * 2,
        compiler_params=pltpu.CompilerParams(vmem_limit_bytes=40 * MB),
        cost_estimate=pl.CostEstimate(
            flops=40 * rows * width * width,
            bytes_accessed=30 * MB,
            transcendentals=rows * width,
        ),
        name="encode_rows",
    )(info, codes, atoms, low, high, weight, gain, ids)
    return [rows.reshape(half, 2, BLOCK, width) for rows in blocks]


def head_kernel(
    scale, bit_ref, rows_ref, weights_ref, back_ref, send_ref, keep_ref,
    x, weights, act, slope, err, grad, back, shares, in_sems, weight_sems, back_sems, share_sems,
):
    width = x.shape[-1]
    tile = x.shape[1] * x.shape[2]
    count = weights.shape[1]
    chunk = width // 4
    chunks = [slice(at, at + chunk) for at in range(0, width, chunk)]
    transposed = (((1,), (1,)), ((), ()))
    over_rows = (((0,), (0,)), ((), ()))
    bit = bit_ref[0]

    def rows_in(rank):
        return pltpu.make_async_copy(rows_ref.at[:, rank], x.at[rank], in_sems.at[rank])

    def weights_in(layer):
        return [
            pltpu.make_async_copy(
                weights_ref.at[i, layer], weights.at[layer, i], weight_sems.at[layer, i]
            )
            for i in range(count)
        ]

    def back_out(rank):
        return pltpu.make_async_copy(back.at[rank], back_ref.at[:, rank], back_sems.at[rank])

    def shares_out(layer):
        copies = []
        for j in range(count // 2):
            for ref, at in ((keep_ref, 2 * j + bit), (send_ref, 2 * j + 1 - bit)):
                copies.append(
                    pltpu.make_async_copy(
                        shares.at[layer, at], ref.at[layer, j],
                        share_sems.at[layer, len(copies)],
                    )
                )
        return copies

    def matrix(layer):
        return weights[layer].reshape(width, width)

    def forward(rank, wait):
        inputs = x[rank].reshape(tile, width)
        low = matrix(0)
        for at in chunks:
            z = jnp.dot(inputs, low[:, at], preferred_element_type=F32)
            s = sigmoid(z)
            act[rank * tile : (rank + 1) * tile, at] = (z * s).astype(BF16)
            slope[rank, :, at] = s * (1.0 + z * (1.0 - s))
        if wait:
            for copy in weights_in(1):
                copy.wait()
        acts = act[rank * tile : (rank + 1) * tile, :]
        high = matrix(1)
        for at in chunks:
            value = jnp.dot(acts, high[:, at], preferred_element_type=F32)
            value = value - inputs[:, at].astype(F32)
            err[rank, :, at] = value
            grad[1, rank * tile : (rank + 1) * tile, at] = value.astype(BF16)

    def backward(rank):
        rows = slice(rank * tile, (rank + 1) * tile)
        grads = grad[1, rows, :]
        high = matrix(1)
        for at in chunks:
            up = lax.dot_general(grads, high[at, :], transposed, preferred_element_type=F32)
            grad[0, rows, at] = (up * slope[rank, :, at]).astype(BF16)
        grads = grad[0, rows, :]
        low = matrix(0)
        shape = x.shape[1:3] + (chunk,)
        for at in chunks:
            up = lax.dot_general(grads, low[at, :], transposed, preferred_element_type=F32)
            back[rank, :, :, at] = (up - err[rank, :, at]).astype(BF16).reshape(shape)

    def share(layer, acts, rows):
        value = lax.dot_general(
            acts, grad[layer, :rows, :], over_rows, preferred_element_type=F32
        )
        shares[layer] = (value * scale).astype(BF16).reshape(shares.shape[1:])

    for rank in range(2):
        rows_in(rank).start()
    for layer in range(2):
        for copy in weights_in(layer):
            copy.start()
    rows_in(0).wait()
    for copy in weights_in(0):
        copy.wait()
    forward(0, True)
    rows_in(1).wait()
    some = jnp.max(jnp.abs(x[1].reshape(tile, width).astype(F32))) > 0
    none = jnp.logical_not(some)
    pl.when(some)(lambda: forward(1, False))
    pl.when(some)(lambda: share(1, act[...], 2 * tile))
    pl.when(none)(lambda: share(1, act[:tile, :], tile))
    for copy in shares_out(1):
        copy.start()
    backward(0)
    back_out(0).start()
    pl.when(some)(lambda: backward(1))

    @pl.when(none)
    def _():
        back[1] = jnp.zeros(back.shape[1:], BF16)

    back_out(1).start()
    pl.when(some)(lambda: share(0, x[...].reshape(2 * tile, width), 2 * tile))
    pl.when(none)(lambda: share(0, x[0].reshape(tile, width), tile))
    for copy in shares_out(0):
        copy.start()
    for rank in range(2):
        back_out(rank).wait()
    for layer in range(2):
        for copy in shares_out(layer):
            copy.wait()


def run_head(rows, weights, scale, name):
    sources, ranks, _, width = rows.shape
    count, layers, depth, _ = weights.shape
    tile = sources * BLOCK
    total = ranks * tile
    part = (layers, count // 2, depth, width)
    bit = lax.axis_index("dom").astype(jnp.int32) & 1
    in_hbm = pl.BlockSpec(memory_space=pltpu.HBM)
    return pl.pallas_call(
        functools.partial(head_kernel, scale),
        grid_spec=pltpu.PrefetchScalarGridSpec(
            num_scalar_prefetch=1,
            grid=(1,),
            in_specs=[in_hbm] * 2,
            out_specs=[in_hbm] * 3,
            scratch_shapes=[
                pltpu.VMEM((ranks, sources, BLOCK, width), BF16),
                pltpu.VMEM((layers, count, depth, width), BF16),
                pltpu.VMEM((total, width), BF16),
                pltpu.VMEM((ranks, tile, width), F32),
                pltpu.VMEM((ranks, tile, width), F32),
                pltpu.VMEM((layers, total, width), BF16),
                pltpu.VMEM((ranks, sources, BLOCK, width), BF16),
                pltpu.VMEM((layers, count, depth, width), BF16),
                pltpu.SemaphoreType.DMA((ranks,)),
                pltpu.SemaphoreType.DMA((layers, count)),
                pltpu.SemaphoreType.DMA((ranks,)),
                pltpu.SemaphoreType.DMA((layers, count)),
            ],
        ),
        out_shape=[pltpu.HBM(rows.shape, BF16), pltpu.HBM(part, BF16), pltpu.HBM(part, BF16)],
        compiler_params=pltpu.CompilerParams(vmem_limit_bytes=VMEM),
        cost_estimate=pl.CostEstimate(
            flops=24 * total * width * width,
            bytes_accessed=5 * total * width * 2 + width * width * 4,
            transcendentals=total * width,
        ),
        name=name,
    )(bit.reshape(1), rows, weights)


def block_place(info_ref, block):
    sets = info_ref.shape[1] - 1
    start, dataset, rank = jnp.int32(0), jnp.int32(0), jnp.int32(0)
    for candidate in range(sets):
        blocks = info_ref[0, candidate] // BLOCK
        inside = jnp.logical_and(block >= start, block < start + blocks)
        dataset = jnp.where(inside, candidate, dataset)
        rank = jnp.where(inside, block - start, rank)
        start = start + blocks
    return dataset, rank, info_ref[0, sets]


def place_kernel(half, info_ref, own_ref, mirror_ref, out_ref):
    dataset, _, place = block_place(info_ref, pl.program_id(0))
    is_own = dataset // half == place // half
    out_ref[0] = jnp.where(is_own, own_ref[0, 0], mirror_ref[0, 0])


def place_rows(info, own, mirror, row_blocks):
    half, _, _, width = own.shape
    shape = (1, 1, BLOCK, width)

    def index(of_own, block, info_ref):
        dataset, rank, place = block_place(info_ref, block)
        wanted = (dataset // half == place // half) == of_own
        return jnp.where(wanted, lax.rem(dataset, half), 0), jnp.where(wanted, rank, 0), 0, 0

    return pl.pallas_call(
        functools.partial(place_kernel, half),
        grid_spec=pltpu.PrefetchScalarGridSpec(
            num_scalar_prefetch=1,
            grid=(row_blocks,),
            in_specs=[
                pl.BlockSpec(shape, functools.partial(index, True)),
                pl.BlockSpec(shape, functools.partial(index, False)),
            ],
            out_specs=pl.BlockSpec((1, BLOCK, width), lambda block, *_: (block, 0, 0)),
        ),
        out_shape=jax.ShapeDtypeStruct((row_blocks, BLOCK, width), BF16),
        compiler_params=pltpu.CompilerParams(vmem_limit_bytes=16 * MB),
        name="place_rows",
    )(info, own, mirror)


def halo(cut_rows):
    count = lax.axis_size("dom")
    forward = [(i, i + 1) for i in range(count - 1)]
    backward = [(target, source) for source, target in forward]
    low = lax.ppermute(cut_rows, "dom", forward)
    high = lax.ppermute(cut_rows, "dom", backward)
    return low, high


def exchange(blocks, half):
    groups = [list(range(half)), list(range(half, 2 * half))]
    return lax.all_to_all(
        blocks, "head", split_axis=0, concat_axis=0, axis_index_groups=groups, tiled=True
    )


def across(array, half):
    return lax.ppermute(array, "head", [(i, (i + half) % (2 * half)) for i in range(2 * half)])


def after(value, *others):
    return lax.optimization_barrier((value,) + others)[0]


def swap(array, bit):
    count = lax.axis_size("dom")
    return lax.ppermute(array, "dom", [(i, i ^ (1 << bit)) for i in range(count)])


def merge_kernel(bit_ref, keep_ref, got_ref, send_ref, kept_ref):
    bit = bit_ref[0]
    for layer in range(keep_ref.shape[0]):
        for j in range(kept_ref.shape[1]):
            for out_ref, at in ((kept_ref, 2 * j + bit), (send_ref, 2 * j + 1 - bit)):
                total = keep_ref[layer, at].astype(F32) + got_ref[layer, at].astype(F32)
                out_ref[layer, j] = total.astype(BF16)


def merge(keep, got, bit, first, layers):
    _, count, depth, width = keep.shape
    mine = (lax.axis_index("dom").astype(jnp.int32) >> bit) & 1
    part = pl.BlockSpec((layers, count, depth, width), lambda t, *_: (first // layers, 0, 0, 0))
    shape = (layers, count // 2, depth, width)
    return pl.pallas_call(
        merge_kernel,
        grid_spec=pltpu.PrefetchScalarGridSpec(
            num_scalar_prefetch=1,
            grid=(1,),
            in_specs=[part, part],
            out_specs=[resident(shape)] * 2,
        ),
        out_shape=[jax.ShapeDtypeStruct(shape, BF16)] * 2,
        compiler_params=pltpu.CompilerParams(vmem_limit_bytes=VMEM),
        name="merge_shares",
    )(mine.reshape(1), keep, got)


def sum_over_dom(send, keep, got, first, layers):
    bits = lax.axis_size("dom").bit_length() - 1
    for bit in range(1, bits):
        send, keep = merge(keep, got, bit, first, layers)
        got = swap(send, bit)
        first = 0
    return keep[:, 0], got[:, 0], send


def total_kernel(layer, keep_ref, got_ref, far_ref, out_ref):
    total = keep_ref[0].astype(F32) + got_ref[0].astype(F32) + far_ref[0].astype(F32)
    out_ref[0] = total


def total(keep, got, far, layer, out=None):
    layers, depth, width = keep.shape
    tile = depth // 4
    mine = pl.BlockSpec((1, tile, width), lambda t: (layer, t, 0))
    came = pl.BlockSpec((1, tile, width), lambda t: (0, t, 0))
    operands = [keep, got, far]
    specs = [mine, mine, came]
    kernel = functools.partial(total_kernel, layer)
    if out is not None:
        operands.append(out)
        specs.append(pl.BlockSpec(memory_space=pl.ANY))
        kernel = lambda a, b, c, _, o: total_kernel(layer, a, b, c, o)
    return pl.pallas_call(
        kernel,
        grid=(4,),
        in_specs=specs,
        out_specs=mine,
        out_shape=jax.ShapeDtypeStruct(keep.shape, F32),
        input_output_aliases={} if out is None else {3: 0},
        compiler_params=pltpu.CompilerParams(vmem_limit_bytes=VMEM),
        name="total_share",
    )(*operands)


def body(atoms, bonds, triplets, halo_ids, counts, enc_weight, gate_gain, head_weight):
    atom_rows = atoms[0]
    row_count, width = atom_rows.shape
    row_blocks = row_count // BLOCK
    half = lax.axis_size("head") // 2
    tall = width // LANES

    shard = head_weight[0]
    count = lax.axis_size("dom")
    own_weights = lax.all_gather(shard, "dom", axis=0, tiled=False)
    far = across(head_weight, half)
    low, high = halo(pick_rows(atom_rows, halo_ids))
    codes = ((bonds[0] * tall) * 65536 + triplets[0] * tall).reshape(-1)
    place = lax.axis_index("head").astype(jnp.int32).reshape(1, 1)
    info = jnp.concatenate([counts, place], axis=1)
    own_blocks, mirror_blocks = encode(
        info, codes, atom_rows, low, high, enc_weight, gate_gain.reshape(tall, LANES),
        bonds[0].T, half
    )
    own_rows = exchange(after(own_blocks, far), half)
    mirror_rows = exchange(mirror_blocks, half)
    mirror_weights = lax.all_gather(far[0], "dom", axis=0, tiled=False)

    scale = 1.0 / math.sqrt(count * row_count)
    back, own_send, own_keep = run_head(own_rows, own_weights, scale, "head_own")
    own_back = exchange(back, half)
    own_got = swap(own_send, 0)

    back, send, keep = run_head(mirror_rows, mirror_weights, scale, "head_mirror")
    got = swap(send, 0)
    high_keep, high_got, high_sent = sum_over_dom(send, keep, got, 1, 1)
    low_keep, low_got, low_sent = sum_over_dom(send, keep, got, 0, 1)
    mirror_back = exchange(after(back, low_got), half)
    high_part = across((high_keep.astype(F32) + high_got.astype(F32)).astype(BF16), half)
    low_part = across((low_keep.astype(F32) + low_got.astype(F32)).astype(BF16), half)
    own_keep, own_got, _ = sum_over_dom(own_send, after(own_keep, low_got), own_got, 0, 2)
    row_part = place_rows(info, own_back, mirror_back, row_blocks)
    head_part = total(own_keep, own_got, after(high_part, row_part), 1)
    head_part = total(own_keep, own_got, after(low_part, head_part), 0, head_part)
    return row_part.reshape(1, row_count, width), head_part[None]


def solution(mesh):
    return jax.shard_map(
        body,
        mesh=mesh,
        in_specs=(
            P("dom", "head", None),
            P("dom", None, "head"),
            P("dom", None, "head"),
            P("dom", "head"),
            P("dom", "head"),
            P(),
            P(),
            P("head", None, "dom", None),
        ),
        out_specs=(P("dom", "head", None), P("head", None, "dom", None)),
        check_vma=False,
    )
```

```python
import functools
import math

import jax
import jax.numpy as jnp
from jax import lax
from jax.experimental import pallas as pl
from jax.experimental.pallas import tpu as pltpu
from jax.sharding import PartitionSpec as P

BLOCK = 128
LANES = 128
MB = 1 << 20
VMEM = 58 * MB
F32 = jnp.float32
BF16 = jnp.bfloat16
ANY = pl.BlockSpec(memory_space=pl.ANY)


def sigmoid(x):
    return 0.5 + 0.5 * jnp.tanh(0.5 * x)


def resident(shape):
    return pl.BlockSpec(shape, lambda *_: (0,) * len(shape))


def pick_kernel(ids_ref, rows_ref, out_ref):
    count, total = out_ref.shape[0], rows_ref.shape[0]
    places = lax.broadcasted_iota(jnp.int32, (total, count), 0)
    ones = jnp.where(places == ids_ref[...], 1.0, 0.0).astype(BF16)
    out_ref[...] = lax.dot_general(
        ones, rows_ref[...], (((0,), (0,)), ((), ())), preferred_element_type=F32
    ).astype(BF16)


def pick_rows(rows, ids):
    return pl.pallas_call(
        pick_kernel,
        out_shape=jax.ShapeDtypeStruct((ids.shape[1], rows.shape[1]), rows.dtype),
        compiler_params=pltpu.CompilerParams(vmem_limit_bytes=16 * MB),
        name="pick_rows",
    )(ids, rows)


def block_place(info_ref, block):
    sets = info_ref.shape[1] - 1
    start, dataset, rank = jnp.int32(0), jnp.int32(0), jnp.int32(0)
    for candidate in range(sets):
        blocks = info_ref[0, candidate] // BLOCK
        inside = jnp.logical_and(block >= start, block < start + blocks)
        dataset = jnp.where(inside, candidate, dataset)
        rank = jnp.where(inside, block - start, rank)
        start = start + blocks
    return dataset, rank, info_ref[0, sets]


def fold(arrays):
    rows = lax.broadcasted_iota(jnp.int32, arrays[0].shape, 0)
    for shift in (1, 2, 4):
        first = (rows & shift) == 0
        arrays = [
            jnp.where(first, a, b) + pltpu.roll(jnp.where(first, b, a), 8 - shift, 0)
            for a, b in zip(arrays[::2], arrays[1::2])
        ]
    return arrays[0]


def turn(arrays):
    rows = lax.broadcasted_iota(jnp.int32, arrays[0].shape, 0)
    arrays = list(arrays)
    for shift in (1, 2, 4):
        low = (rows & shift) == 0
        for at in range(8):
            if at & shift == 0:
                a, b = arrays[at], arrays[at + shift]
                arrays[at] = jnp.where(low, a, pltpu.roll(b, shift, 0))
                arrays[at + shift] = jnp.where(low, pltpu.roll(a, 8 - shift, 0), b)
    return arrays


def encode_kernel(
    half, batch, info_ref, codes_ref, atoms_ref, low_ref, high_ref, weight_ref, gain_ref,
    ids_ref, own_ref, mirror_ref, plain, gained, partial, gate_rows, staged, zeros, sems,
):
    rows, width = atoms_ref.shape
    depth = low_ref.shape[0]
    tall = width // LANES
    bond_count = ids_ref.shape[1]
    sets = 2 * half
    home = info_ref[0, sets] // half * half
    tile = batch * BLOCK

    def leave(source, slot, act):
        def one(ref, at):
            act(pltpu.make_async_copy(source, ref.at[at], sems.at[slot]))

        pl.when(slot < sets)(lambda: one(own_ref, slot))
        pl.when(slot >= sets)(lambda: one(mirror_ref, slot - sets))

    zeros[...] = jnp.zeros_like(zeros)

    def blank(slot, carry):
        dataset = lax.rem(home + slot // 2, sets)
        empty = info_ref[0, dataset] // BLOCK <= lax.rem(slot, 2)
        pl.when(empty)(lambda: leave(zeros, slot, lambda copy: copy.start()))
        return carry

    lax.fori_loop(0, 2 * sets, blank, 0)

    def spread(ref, base):
        def one(group, carry):
            at = pl.multiple_of(group * 16, 16)
            for k in range(0, tall, 8):
                gains = gain_ref[k : k + 8, :]
                parts = [
                    ref[pl.ds(at, 16), (k + j) * LANES : (k + j + 1) * LANES].astype(F32)
                    for j in range(8)
                ]
                for side in (0, 8):
                    for i, row in enumerate(turn([part[side : side + 8] for part in parts])):
                        place = pl.multiple_of((base + at + side + i) * tall + k, 8)
                        plain[pl.ds(place, 8), :] = row
                        gained[pl.ds(place, 8), :] = row * gains
            return carry

        lax.fori_loop(0, ref.shape[0] // 16, one, 0)

    spread(atoms_ref, 0)
    spread(low_ref, rows)
    spread(high_ref, rows + depth)

    def row_of(ref, place):
        return ref[pl.ds(pl.multiple_of(place, tall), tall), :]

    def product(code):
        value = row_of(plain, code >> 16) * row_of(gained, code & 0xFFFF)
        return sum(value[k : k + 8] for k in range(0, tall, 8))

    def encode_tile(step, carry):
        base = pl.multiple_of(step * tile, tile)

        def score(group, carry):
            for bond in range(bond_count):
                at = bond * rows + base + group * 8
                place = pl.multiple_of(bond * tile + group * 8, 8)
                partial[pl.ds(place, 8), :] = fold([product(codes_ref[at + j]) for j in range(8)])
            return carry

        lax.fori_loop(0, tile // 8, score, 0)
        for block in range(batch):
            ids = ids_ref[pl.ds(base + block * BLOCK, BLOCK), :]
            gates = []
            for bond in range(bond_count):
                at = bond * tile + block * BLOCK
                logits = jnp.sum(partial[at : at + BLOCK, :], axis=1, keepdims=True)
                gates.append(sigmoid(logits * (1.0 / math.sqrt(width))))
            for at in range(0, gate_rows.shape[1], LANES):
                places = lax.broadcasted_iota(jnp.int32, (BLOCK, LANES), 1) + at
                acc = jnp.zeros((BLOCK, LANES), F32)
                for bond in range(bond_count):
                    acc = acc + jnp.where(places == ids[:, bond : bond + 1], gates[bond], 0.0)
                gate_rows[block * BLOCK : (block + 1) * BLOCK, at : at + LANES] = acc.astype(BF16)
        message = jnp.dot(gate_rows[:, :rows], atoms_ref[...], preferred_element_type=F32)
        for ref, at in ((low_ref, rows), (high_ref, rows + depth)):
            message += jnp.dot(
                gate_rows[:, at : at + depth], ref[...], preferred_element_type=F32
            )
        update = jnp.dot(message.astype(BF16), weight_ref[...], preferred_element_type=F32)
        own = atoms_ref[pl.ds(base, tile), :].astype(F32)
        staged[step] = (own + update * sigmoid(update)).astype(BF16).reshape(staged.shape[1:])
        for block in range(batch):
            dataset, rank, _ = block_place(info_ref, step * batch + block)
            slot = lax.rem(dataset - home + sets, sets) * 2 + rank
            leave(staged.at[step, block], slot, lambda copy: copy.start())
        return carry

    lax.fori_loop(0, rows // tile, encode_tile, 0)

    def settle(slot, carry):
        leave(zeros, slot, lambda copy: copy.wait())
        return carry

    lax.fori_loop(0, 2 * sets, settle, 0)


def encode(info, codes, atoms, low, high, weight, gain, ids, half):
    rows, width = atoms.shape
    depth = low.shape[0]
    tall = width // LANES
    extended = rows + 2 * depth
    bond_count = ids.shape[1]
    slots = 4 * half
    row_blocks = rows // BLOCK
    batch = 4 if row_blocks % 4 == 0 else 1
    blocks = pl.pallas_call(
        functools.partial(encode_kernel, half, batch),
        grid_spec=pltpu.PrefetchScalarGridSpec(
            num_scalar_prefetch=2,
            grid=(1,),
            in_specs=[
                resident((rows, width)),
                resident((depth, width)),
                resident((depth, width)),
                resident((width, width)),
                resident((tall, LANES)),
                resident((rows, bond_count)),
            ],
            out_specs=[pl.BlockSpec(memory_space=pltpu.HBM)] * 2,
            scratch_shapes=[
                pltpu.VMEM((extended * tall, LANES), F32),
                pltpu.VMEM((extended * tall, LANES), F32),
                pltpu.VMEM((batch * BLOCK * bond_count, LANES), F32),
                pltpu.VMEM((batch * BLOCK, extended), BF16),
                pltpu.VMEM((row_blocks // batch, batch, BLOCK, width), BF16),
                pltpu.VMEM((BLOCK, width), BF16),
                pltpu.SemaphoreType.DMA((slots,)),
            ],
        ),
        out_shape=[pltpu.HBM((2 * half, BLOCK, width), BF16)] * 2,
        compiler_params=pltpu.CompilerParams(vmem_limit_bytes=44 * MB),
        cost_estimate=pl.CostEstimate(
            flops=40 * rows * width * width,
            bytes_accessed=30 * MB,
            transcendentals=rows * width,
        ),
        name="encode_rows",
    )(info, codes, atoms, low, high, weight, gain, ids)
    return [rows.reshape(half, 2, BLOCK, width) for rows in blocks]


def head_kernel(scale, part_count, tokens, bit_ref, rows_ref, *refs):
    weight_refs = refs[:part_count]
    (
        back_ref, send_ref, keep_ref, x, weights, act, slope, err, grad, back, shares,
        in_sems, weight_sems, back_sems, share_sems,
    ) = refs[part_count + tokens :]
    width = x.shape[-1]
    tile = x.shape[1] * x.shape[2]
    count = weights.shape[1]
    chunk = width // 4
    chunks = [slice(at, at + chunk) for at in range(0, width, chunk)]
    transposed = (((1,), (1,)), ((), ()))
    over_rows = (((0,), (0,)), ((), ()))
    bit = bit_ref[0]

    def rows_in(rank):
        return pltpu.make_async_copy(rows_ref.at[:, rank], x.at[rank], in_sems.at[rank])

    def weights_in(layer):
        copies = []
        at = 0
        for ref in weight_refs:
            depth = ref.shape[2]
            for i in range(count):
                place = weights.at[layer, i, pl.ds(at, depth)]
                sem = weight_sems.at[layer, len(copies)]
                copies.append(pltpu.make_async_copy(ref.at[i, layer], place, sem))
            at += depth
        return copies

    def back_out(rank):
        return pltpu.make_async_copy(back.at[rank], back_ref.at[:, rank], back_sems.at[rank])

    def shares_out(layer):
        copies = []
        for j in range(count // 2):
            for ref, at in ((keep_ref, 2 * j + bit), (send_ref, 2 * j + 1 - bit)):
                copies.append(
                    pltpu.make_async_copy(
                        shares.at[layer, at], ref.at[layer, j],
                        share_sems.at[layer, len(copies)],
                    )
                )
        return copies

    def matrix(layer):
        return weights[layer].reshape(width, width)

    def forward(rank, wait):
        inputs = x[rank].reshape(tile, width)
        low = matrix(0)
        for at in chunks:
            z = jnp.dot(inputs, low[:, at], preferred_element_type=F32)
            s = sigmoid(z)
            act[rank * tile : (rank + 1) * tile, at] = (z * s).astype(BF16)
            slope[rank, :, at] = s * (1.0 + z * (1.0 - s))
        if wait:
            for copy in weights_in(1):
                copy.wait()
        acts = act[rank * tile : (rank + 1) * tile, :]
        high = matrix(1)
        for at in chunks:
            value = jnp.dot(acts, high[:, at], preferred_element_type=F32)
            value = value - inputs[:, at].astype(F32)
            err[rank, :, at] = value
            grad[1, rank * tile : (rank + 1) * tile, at] = value.astype(BF16)

    def backward(rank):
        rows = slice(rank * tile, (rank + 1) * tile)
        grads = grad[1, rows, :]
        high = matrix(1)
        for at in chunks:
            up = lax.dot_general(grads, high[at, :], transposed, preferred_element_type=F32)
            grad[0, rows, at] = (up * slope[rank, :, at]).astype(BF16)
        grads = grad[0, rows, :]
        low = matrix(0)
        shape = x.shape[1:3] + (chunk,)
        for at in chunks:
            up = lax.dot_general(grads, low[at, :], transposed, preferred_element_type=F32)
            back[rank, :, :, at] = (up - err[rank, :, at]).astype(BF16).reshape(shape)

    def share(layer, acts, rows):
        value = lax.dot_general(
            acts, grad[layer, :rows, :], over_rows, preferred_element_type=F32
        )
        shares[layer] = (value * scale).astype(BF16).reshape(shares.shape[1:])

    for rank in range(2):
        rows_in(rank).start()
    for layer in range(2):
        for copy in weights_in(layer):
            copy.start()
    rows_in(0).wait()
    for copy in weights_in(0):
        copy.wait()
    forward(0, True)
    rows_in(1).wait()
    some = jnp.max(jnp.abs(x[1].reshape(tile, width).astype(F32))) > 0
    none = jnp.logical_not(some)
    pl.when(some)(lambda: forward(1, False))
    pl.when(some)(lambda: share(1, act[...], 2 * tile))
    pl.when(none)(lambda: share(1, act[:tile, :], tile))
    for copy in shares_out(1):
        copy.start()
    backward(0)
    back_out(0).start()
    pl.when(some)(lambda: backward(1))

    @pl.when(none)
    def _():
        back[1] = jnp.zeros(back.shape[1:], BF16)

    back_out(1).start()
    pl.when(some)(lambda: share(0, x[...].reshape(2 * tile, width), 2 * tile))
    pl.when(none)(lambda: share(0, x[0].reshape(tile, width), tile))
    for copy in shares_out(0):
        copy.start()
    for rank in range(2):
        back_out(rank).wait()
    for layer in range(2):
        for copy in shares_out(layer):
            copy.wait()


def run_head(rows, parts, scale, name, *tokens):
    sources, ranks, _, width = rows.shape
    count, layers, _, _ = parts[0].shape
    depth = width // count
    tile = sources * BLOCK
    total = ranks * tile
    part = (layers, count // 2, depth, width)
    bit = lax.axis_index("dom").astype(jnp.int32) & 1
    in_hbm = pl.BlockSpec(memory_space=pltpu.HBM)
    return pl.pallas_call(
        functools.partial(head_kernel, scale, len(parts), len(tokens)),
        grid_spec=pltpu.PrefetchScalarGridSpec(
            num_scalar_prefetch=1,
            grid=(1,),
            in_specs=[ANY] + [in_hbm] * len(parts) + [ANY] * len(tokens),
            out_specs=[in_hbm] * 3,
            scratch_shapes=[
                pltpu.VMEM((ranks, sources, BLOCK, width), BF16),
                pltpu.VMEM((layers, count, depth, width), BF16),
                pltpu.VMEM((total, width), BF16),
                pltpu.VMEM((ranks, tile, width), F32),
                pltpu.VMEM((ranks, tile, width), F32),
                pltpu.VMEM((layers, total, width), BF16),
                pltpu.VMEM((ranks, sources, BLOCK, width), BF16),
                pltpu.VMEM((layers, count, depth, width), BF16),
                pltpu.SemaphoreType.DMA((ranks,)),
                pltpu.SemaphoreType.DMA((layers, count * len(parts))),
                pltpu.SemaphoreType.DMA((ranks,)),
                pltpu.SemaphoreType.DMA((layers, count)),
            ],
        ),
        out_shape=[pltpu.HBM(rows.shape, BF16), pltpu.HBM(part, BF16), pltpu.HBM(part, BF16)],
        compiler_params=pltpu.CompilerParams(vmem_limit_bytes=VMEM),
        cost_estimate=pl.CostEstimate(
            flops=24 * total * width * width,
            bytes_accessed=5 * total * width * 2 + width * width * 4,
            transcendentals=total * width,
        ),
        name=name,
    )(bit.reshape(1), rows, *parts, *tokens)


def place_kernel(half, info_ref, own_ref, mirror_ref, out_ref):
    dataset, _, place = block_place(info_ref, pl.program_id(0))
    is_own = dataset // half == place // half
    out_ref[0] = jnp.where(is_own, own_ref[0, 0], mirror_ref[0, 0])


def place_rows(info, own, mirror, row_blocks):
    half, _, _, width = own.shape
    shape = (1, 1, BLOCK, width)

    def index(of_own, block, info_ref):
        dataset, rank, place = block_place(info_ref, block)
        wanted = (dataset // half == place // half) == of_own
        return jnp.where(wanted, lax.rem(dataset, half), 0), jnp.where(wanted, rank, 0), 0, 0

    return pl.pallas_call(
        functools.partial(place_kernel, half),
        grid_spec=pltpu.PrefetchScalarGridSpec(
            num_scalar_prefetch=1,
            grid=(row_blocks,),
            in_specs=[
                pl.BlockSpec(shape, functools.partial(index, True)),
                pl.BlockSpec(shape, functools.partial(index, False)),
            ],
            out_specs=pl.BlockSpec((1, BLOCK, width), lambda block, *_: (block, 0, 0)),
        ),
        out_shape=jax.ShapeDtypeStruct((row_blocks, BLOCK, width), BF16),
        compiler_params=pltpu.CompilerParams(vmem_limit_bytes=16 * MB),
        name="place_rows",
    )(info, own, mirror)


def halo(cut_rows):
    count = lax.axis_size("dom")
    forward = [(i, i + 1) for i in range(count - 1)]
    backward = [(target, source) for source, target in forward]
    low = lax.ppermute(cut_rows, "dom", forward)
    high = lax.ppermute(cut_rows, "dom", backward)
    return low, high


def exchange(blocks, half):
    groups = [list(range(half)), list(range(half, 2 * half))]
    return lax.all_to_all(
        blocks, "head", split_axis=0, concat_axis=0, axis_index_groups=groups, tiled=True
    )


def across(array, half):
    return lax.ppermute(array, "head", [(i, (i + half) % (2 * half)) for i in range(2 * half)])


def after(array, *tokens):
    return pl.pallas_call(
        lambda *refs: None,
        in_specs=[ANY] * (1 + len(tokens)),
        out_specs=ANY,
        out_shape=jax.ShapeDtypeStruct(array.shape, array.dtype),
        input_output_aliases={0: 0},
        compiler_params=pltpu.CompilerParams(vmem_limit_bytes=VMEM),
        name="after",
    )(array, *tokens)


def swap(array, bit):
    count = lax.axis_size("dom")
    return lax.ppermute(array, "dom", [(i, i ^ (1 << bit)) for i in range(count)])


def merge_kernel(tokens, bit_ref, keep_ref, got_ref, *refs):
    send_ref, kept_ref = refs[tokens:]
    bit = bit_ref[0]
    for layer in range(keep_ref.shape[0]):
        for j in range(kept_ref.shape[1]):
            for out_ref, at in ((kept_ref, 2 * j + bit), (send_ref, 2 * j + 1 - bit)):
                total = keep_ref[layer, at].astype(F32) + got_ref[layer, at].astype(F32)
                out_ref[layer, j] = total.astype(BF16)


def merge(keep, got, bit, first, layers, tokens):
    _, count, depth, width = keep.shape
    mine = (lax.axis_index("dom").astype(jnp.int32) >> bit) & 1
    part = pl.BlockSpec((layers, count, depth, width), lambda t, *_: (first // layers, 0, 0, 0))
    shape = (layers, count // 2, depth, width)
    return pl.pallas_call(
        functools.partial(merge_kernel, len(tokens)),
        grid_spec=pltpu.PrefetchScalarGridSpec(
            num_scalar_prefetch=1,
            grid=(1,),
            in_specs=[part, part] + [ANY] * len(tokens),
            out_specs=[resident(shape)] * 2,
        ),
        out_shape=[jax.ShapeDtypeStruct(shape, BF16)] * 2,
        compiler_params=pltpu.CompilerParams(vmem_limit_bytes=VMEM),
        name="merge_shares",
    )(mine.reshape(1), keep, got, *tokens)


def sum_over_dom(keep, got, first, layers, *tokens):
    bits = lax.axis_size("dom").bit_length() - 1
    for bit in range(1, bits):
        send, keep = merge(keep, got, bit, first, layers, tokens)
        got = swap(send, bit)
        first = 0
    return keep[:, 0], got[:, 0], send


def add_kernel(keep_ref, got_ref, *refs):
    refs[-1][...] = (keep_ref[...].astype(F32) + got_ref[...].astype(F32)).astype(BF16)


def add(keep, got, *tokens):
    whole = resident(keep.shape)
    return pl.pallas_call(
        add_kernel,
        grid=(1,),
        in_specs=[whole, whole] + [ANY] * len(tokens),
        out_specs=whole,
        out_shape=jax.ShapeDtypeStruct(keep.shape, BF16),
        compiler_params=pltpu.CompilerParams(vmem_limit_bytes=16 * MB),
        name="add_shares",
    )(keep, got, *tokens)


def total_kernel(keep_ref, got_ref, far_ref, *refs):
    total = keep_ref[0].astype(F32) + got_ref[0].astype(F32) + far_ref[0].astype(F32)
    refs[-1][0] = total


def total(keep, got, far, layer, out=None, *tokens):
    _, depth, width = keep.shape
    mine = pl.BlockSpec((1, depth, width), lambda t: (layer, 0, 0))
    came = pl.BlockSpec((1, depth, width), lambda t: (0, 0, 0))
    tokens = tokens if out is None else (out,) + tokens
    return pl.pallas_call(
        total_kernel,
        grid=(1,),
        in_specs=[mine, mine, came] + [ANY] * len(tokens),
        out_specs=mine,
        out_shape=jax.ShapeDtypeStruct(keep.shape, F32),
        input_output_aliases={} if out is None else {3: 0},
        compiler_params=pltpu.CompilerParams(vmem_limit_bytes=16 * MB),
        name="total_share",
    )(keep, got, far, *tokens)


def body(atoms, bonds, triplets, halo_ids, counts, enc_weight, gate_gain, head_weight):
    atom_rows = atoms[0]
    row_count, width = atom_rows.shape
    row_blocks = row_count // BLOCK
    half = lax.axis_size("head") // 2
    tall = width // LANES

    shard = head_weight[0]
    count = lax.axis_size("dom")
    cut = shard.shape[1] // 4 * 3

    def gather(shard):
        return lax.all_gather(shard, "dom", axis=0, tiled=False)

    own_weights = [gather(shard)]
    far = [across(shard[:, :cut], half), across(shard[:, cut:], half)]
    mirror_weights = [gather(piece) for piece in far]
    low, high = halo(pick_rows(atom_rows, halo_ids))
    codes = ((bonds[0] * tall) * 65536 + triplets[0] * tall).reshape(-1)
    place = lax.axis_index("head").astype(jnp.int32).reshape(1, 1)
    info = jnp.concatenate([counts, place], axis=1)
    own_blocks, mirror_blocks = encode(
        info, codes, atom_rows, low, high, enc_weight, gate_gain.reshape(tall, LANES),
        bonds[0].T, half
    )
    mirror_rows = exchange(after(mirror_blocks, far[0]), half)
    own_rows = exchange(after(own_blocks, mirror_rows), half)

    scale = 1.0 / math.sqrt(count * row_count)
    back, send, keep = run_head(mirror_rows, mirror_weights, scale, "head_mirror")
    got = swap(send, 0)
    high_keep, high_got, high_sent = sum_over_dom(keep, got, 1, 1)
    low_keep, low_got, low_sent = sum_over_dom(keep, got, 0, 1, high_sent)
    mirror_back = exchange(after(back, low_sent), half)
    back, own_send, own_keep = run_head(own_rows, own_weights, scale, "head_own", low_sent)
    high_part = across(add(high_keep, high_got, own_send), half)
    low_sum = add(low_keep, low_got, own_send)
    low_part = across(low_sum, half)
    own_back = exchange(after(back, mirror_back), half)
    own_keep, own_got, _ = sum_over_dom(own_keep, swap(own_send, 0), 0, 2, low_sum)
    row_part = place_rows(info, own_back, mirror_back, row_blocks)
    head_part = total(own_keep, own_got, high_part, 1, None, row_part)
    head_part = total(own_keep, own_got, low_part, 0, head_part)
    return row_part.reshape(1, row_count, width), head_part[None]


def solution(mesh):
    return jax.shard_map(
        body,
        mesh=mesh,
        in_specs=(
            P("dom", "head", None),
            P("dom", None, "head"),
            P("dom", None, "head"),
            P("dom", "head"),
            P("dom", "head"),
            P(),
            P(),
            P("head", None, "dom", None),
        ),
        out_specs=(P("dom", "head", None), P("head", None, "dom", None)),
        check_vma=False,
    )
```

```python
import functools
import math

import jax
import jax.numpy as jnp
from jax import lax
from jax.experimental import pallas as pl
from jax.experimental.pallas import tpu as pltpu
from jax.sharding import PartitionSpec as P

BLOCK = 128
LANES = 128
MB = 1 << 20
VMEM = 58 * MB
F32 = jnp.float32
BF16 = jnp.bfloat16
ANY = pl.BlockSpec(memory_space=pl.ANY)
IN_VMEM = pl.BlockSpec(memory_space=pltpu.VMEM)


def sigmoid(x):
    return 0.5 + 0.5 * jnp.tanh(0.5 * x)


def hbm(array):
    return pltpu.with_memory_space_constraint(array, pltpu.HBM)


def resident(shape):
    return pl.BlockSpec(shape, lambda *_: (0,) * len(shape))


def pick_kernel(ids_ref, rows_ref, shard_ref, out_ref, low_ref, high_ref, held, sems):
    layers = (low_ref, high_ref)
    loads = [
        pltpu.make_async_copy(shard_ref.at[0, i], held.at[i], sems.at[0, i]) for i in range(2)
    ]
    stores = [pltpu.make_async_copy(held.at[i], layers[i], sems.at[1, i]) for i in range(2)]
    for load in loads:
        load.start()
    count, total = out_ref.shape[0], rows_ref.shape[0]
    places = lax.broadcasted_iota(jnp.int32, (total, count), 0)
    ones = jnp.where(places == ids_ref[...], 1.0, 0.0).astype(BF16)
    out_ref[...] = lax.dot_general(
        ones, rows_ref[...], (((0,), (0,)), ((), ())), preferred_element_type=F32
    ).astype(BF16)
    for load, store in zip(loads, stores):
        load.wait()
        store.start()
    for store in stores:
        store.wait()


def pick_rows(rows, ids, shard):
    layer = shard.shape[2:]
    return pl.pallas_call(
        pick_kernel,
        in_specs=[pl.BlockSpec(memory_space=pltpu.VMEM)] * 2 + [ANY],
        out_specs=[pl.BlockSpec(memory_space=pltpu.VMEM)] + [ANY] * 2,
        out_shape=[
            jax.ShapeDtypeStruct((ids.shape[1], rows.shape[1]), rows.dtype),
            pltpu.HBM(layer, shard.dtype),
            pltpu.HBM(layer, shard.dtype),
        ],
        scratch_shapes=[pltpu.VMEM((2,) + layer, shard.dtype), pltpu.SemaphoreType.DMA((2, 2))],
        compiler_params=pltpu.CompilerParams(vmem_limit_bytes=16 * MB),
        name="pick_rows",
    )(ids, rows, shard)


def block_place(info_ref, block):
    sets = info_ref.shape[1] - 1
    start, dataset, rank = jnp.int32(0), jnp.int32(0), jnp.int32(0)
    for candidate in range(sets):
        blocks = info_ref[0, candidate] // BLOCK
        inside = jnp.logical_and(block >= start, block < start + blocks)
        dataset = jnp.where(inside, candidate, dataset)
        rank = jnp.where(inside, block - start, rank)
        start = start + blocks
    return dataset, rank, info_ref[0, sets]


def encode_kernel(
    half, batch, info_ref, codes_ref, atoms_ref, low_ref, high_ref, weight_ref, gain_ref,
    ids_ref, lanes_ref, own_ref, mirror_ref, gained, scores, partial, gate_rows, staged, zeros,
    sems,
):
    rows, width = atoms_ref.shape
    depth = low_ref.shape[0]
    bond_count = ids_ref.shape[1]
    sets = 2 * half
    home = info_ref[0, sets] // half * half
    tile = batch * BLOCK

    def leave(source, slot, act):
        def one(ref, at):
            act(pltpu.make_async_copy(source, ref.at[at], sems.at[slot]))

        pl.when(slot < sets)(lambda: one(own_ref, slot))
        pl.when(slot >= sets)(lambda: one(mirror_ref, slot - sets))

    zeros[...] = jnp.zeros_like(zeros)

    def blank(slot, carry):
        dataset = lax.rem(home + slot // 2, sets)
        empty = info_ref[0, dataset] // BLOCK <= lax.rem(slot, 2)
        pl.when(empty)(lambda: leave(zeros, slot, lambda copy: copy.start()))
        return carry

    lax.fori_loop(0, 2 * sets, blank, 0)

    extended = rows + 2 * depth
    parts = ((atoms_ref, 0), (low_ref, rows), (high_ref, rows + depth))
    for ref, at in parts:
        gained[at : at + ref.shape[0], :] = (ref[...].astype(F32) * gain_ref[...]).astype(BF16)
    for ref, base in parts:
        step = min(ref.shape[0], 2 * LANES)
        for at in range(0, ref.shape[0], step):
            value = lax.dot_general(
                gained[...], ref[at : at + step, :], (((1,), (1,)), ((), ())),
                preferred_element_type=F32,
            )
            for k in range(0, step, LANES):
                piece = (base + at + k) // LANES
                scores[piece * extended : (piece + 1) * extended, :] = value[:, k : k + LANES]

    def encode_tile(step, carry):
        base = pl.multiple_of(step * tile, tile)

        def score(group, carry):
            for bond in range(bond_count):
                at = bond * rows + base + group * 8
                place = pl.multiple_of(bond * tile + group * 8, 8)
                for j in range(8):
                    partial[pl.ds(place + j, 1), :] = scores[pl.ds(codes_ref[at + j], 1), :]
            return carry

        lax.fori_loop(0, tile // 8, score, 0)
        for block in range(batch):
            ids = ids_ref[pl.ds(base + block * BLOCK, BLOCK), :]
            lanes = lanes_ref[pl.ds(base + block * BLOCK, BLOCK), :]
            gates = []
            for bond in range(bond_count):
                at = bond * tile + block * BLOCK
                places = lax.broadcasted_iota(jnp.int32, (BLOCK, LANES), 1)
                chosen = jnp.where(
                    places == lanes[:, bond : bond + 1], partial[at : at + BLOCK, :], 0.0
                )
                logits = jnp.sum(chosen, axis=1, keepdims=True)
                gates.append(sigmoid(logits * (1.0 / math.sqrt(width))))
            for at in range(0, gate_rows.shape[1], LANES):
                places = lax.broadcasted_iota(jnp.int32, (BLOCK, LANES), 1) + at
                acc = jnp.zeros((BLOCK, LANES), F32)
                for bond in range(bond_count):
                    acc = acc + jnp.where(places == ids[:, bond : bond + 1], gates[bond], 0.0)
                gate_rows[block * BLOCK : (block + 1) * BLOCK, at : at + LANES] = acc.astype(BF16)
        message = jnp.dot(gate_rows[:, :rows], atoms_ref[...], preferred_element_type=F32)
        for ref, at in ((low_ref, rows), (high_ref, rows + depth)):
            message += jnp.dot(
                gate_rows[:, at : at + depth], ref[...], preferred_element_type=F32
            )
        update = jnp.dot(message.astype(BF16), weight_ref[...], preferred_element_type=F32)
        own = atoms_ref[pl.ds(base, tile), :].astype(F32)
        staged[step] = (own + update * sigmoid(update)).astype(BF16).reshape(staged.shape[1:])
        for block in range(batch):
            dataset, rank, _ = block_place(info_ref, step * batch + block)
            slot = lax.rem(dataset - home + sets, sets) * 2 + rank
            leave(staged.at[step, block], slot, lambda copy: copy.start())
        return carry

    lax.fori_loop(0, rows // tile, encode_tile, 0)

    def settle(slot, carry):
        leave(zeros, slot, lambda copy: copy.wait())
        return carry

    lax.fori_loop(0, 2 * sets, settle, 0)


def encode(info, codes, atoms, low, high, weight, gain, ids, lanes, half):
    rows, width = atoms.shape
    depth = low.shape[0]
    extended = rows + 2 * depth
    bond_count = ids.shape[1]
    slots = 4 * half
    row_blocks = rows // BLOCK
    batch = 4 if row_blocks % 4 == 0 else 1
    blocks = pl.pallas_call(
        functools.partial(encode_kernel, half, batch),
        grid_spec=pltpu.PrefetchScalarGridSpec(
            num_scalar_prefetch=2,
            grid=(1,),
            in_specs=[
                resident((rows, width)),
                resident((depth, width)),
                resident((depth, width)),
                resident((width, width)),
                resident((1, width)),
                resident((rows, bond_count)),
                resident((rows, bond_count)),
            ],
            out_specs=[pl.BlockSpec(memory_space=pltpu.HBM)] * 2,
            scratch_shapes=[
                pltpu.VMEM((extended, width), BF16),
                pltpu.VMEM((extended // LANES * extended, LANES), F32),
                pltpu.VMEM((batch * BLOCK * bond_count, LANES), F32),
                pltpu.VMEM((batch * BLOCK, extended), BF16),
                pltpu.VMEM((row_blocks // batch, batch, BLOCK, width), BF16),
                pltpu.VMEM((BLOCK, width), BF16),
                pltpu.SemaphoreType.DMA((slots,)),
            ],
        ),
        out_shape=[pltpu.HBM((2 * half, BLOCK, width), BF16)] * 2,
        compiler_params=pltpu.CompilerParams(vmem_limit_bytes=44 * MB),
        cost_estimate=pl.CostEstimate(
            flops=40 * rows * width * width,
            bytes_accessed=30 * MB,
            transcendentals=rows * width,
        ),
        name="encode_rows",
    )(info, codes, atoms, low, high, weight, gain, ids, lanes)
    return [rows.reshape(half, 2, BLOCK, width) for rows in blocks]


def head_kernel(scale, part_count, tokens, bit_ref, rows_ref, *refs):
    weight_refs = refs[:part_count]
    (
        back_ref, send_ref, keep_ref, x, weights, act, slope, err, grad, back, shares,
        in_sems, weight_sems, back_sems,
    ) = refs[part_count + tokens :]
    width = x.shape[-1]
    tile = x.shape[1] * x.shape[2]
    count = weights.shape[1]
    chunk = width // 4
    chunks = [slice(at, at + chunk) for at in range(0, width, chunk)]
    transposed = (((1,), (1,)), ((), ()))
    over_rows = (((0,), (0,)), ((), ()))
    bit = bit_ref[0]

    def rows_in(rank):
        return pltpu.make_async_copy(rows_ref.at[:, rank], x.at[rank], in_sems.at[rank])

    def weights_in(layer):
        copies = []
        for i in range(count):
            source = weight_refs[0].at[i, layer] if part_count == 1 else weight_refs[layer].at[i]
            copies.append(
                pltpu.make_async_copy(source, weights.at[layer, i], weight_sems.at[layer, i])
            )
        return copies

    def back_out(rank):
        return pltpu.make_async_copy(back.at[rank], back_ref.at[:, rank], back_sems.at[rank])

    def matrix(layer):
        return weights[layer].reshape(width, width)

    def forward(rank, wait):
        inputs = x[rank].reshape(tile, width)
        low = matrix(0)
        for at in chunks:
            z = jnp.dot(inputs, low[:, at], preferred_element_type=F32)
            s = sigmoid(z)
            act[rank * tile : (rank + 1) * tile, at] = (z * s).astype(BF16)
            slope[rank, :, at] = s * (1.0 + z * (1.0 - s))
        if wait:
            for copy in weights_in(1):
                copy.wait()
        acts = act[rank * tile : (rank + 1) * tile, :]
        high = matrix(1)
        for at in chunks:
            value = jnp.dot(acts, high[:, at], preferred_element_type=F32)
            value = value - inputs[:, at].astype(F32)
            err[rank, :, at] = value
            grad[1, rank * tile : (rank + 1) * tile, at] = value.astype(BF16)

    def backward(rank):
        rows = slice(rank * tile, (rank + 1) * tile)
        grads = grad[1, rows, :]
        high = matrix(1)
        for at in chunks:
            up = lax.dot_general(grads, high[at, :], transposed, preferred_element_type=F32)
            grad[0, rows, at] = (up * slope[rank, :, at]).astype(BF16)
        grads = grad[0, rows, :]
        low = matrix(0)
        shape = x.shape[1:3] + (chunk,)
        for at in chunks:
            up = lax.dot_general(grads, low[at, :], transposed, preferred_element_type=F32)
            back[rank, :, :, at] = (up - err[rank, :, at]).astype(BF16).reshape(shape)

    def share(layer, acts, rows):
        value = lax.dot_general(
            acts, grad[layer, :rows, :], over_rows, preferred_element_type=F32
        )
        shares[...] = (value * scale).astype(BF16).reshape(shares.shape)
        for j in range(count // 2):
            keep_ref[layer, j] = shares[2 * j + bit]
            send_ref[layer, j] = shares[2 * j + 1 - bit]

    for rank in range(2):
        rows_in(rank).start()
    for layer in range(2):
        for copy in weights_in(layer):
            copy.start()
    rows_in(0).wait()
    for copy in weights_in(0):
        copy.wait()
    forward(0, True)
    rows_in(1).wait()
    some = jnp.max(jnp.abs(x[1].reshape(tile, width).astype(F32))) > 0
    none = jnp.logical_not(some)
    pl.when(some)(lambda: forward(1, False))
    pl.when(some)(lambda: share(1, act[...], 2 * tile))
    pl.when(none)(lambda: share(1, act[:tile, :], tile))
    backward(0)
    back_out(0).start()
    pl.when(some)(lambda: backward(1))

    @pl.when(none)
    def _():
        back[1] = jnp.zeros(back.shape[1:], BF16)

    back_out(1).start()
    pl.when(some)(lambda: share(0, x[...].reshape(2 * tile, width), 2 * tile))
    pl.when(none)(lambda: share(0, x[0].reshape(tile, width), tile))
    for rank in range(2):
        back_out(rank).wait()


def run_head(rows, parts, scale, near, *tokens):
    sources, ranks, _, width = rows.shape
    count = parts[0].shape[0]
    depth = width // count
    layers = 2
    tile = sources * BLOCK
    total = ranks * tile
    part = (layers, count // 2, depth, width)
    bit = lax.axis_index("dom").astype(jnp.int32) & 1
    in_hbm = pl.BlockSpec(memory_space=pltpu.HBM)
    return pl.pallas_call(
        functools.partial(head_kernel, scale, len(parts), len(tokens)),
        grid_spec=pltpu.PrefetchScalarGridSpec(
            num_scalar_prefetch=1,
            grid=(1,),
            in_specs=[ANY] + [in_hbm] * len(parts) + [ANY] * len(tokens),
            out_specs=[in_hbm] + [IN_VMEM if near else resident(part)] * 2,
            scratch_shapes=[
                pltpu.VMEM((ranks, sources, BLOCK, width), BF16),
                pltpu.VMEM((layers, count, depth, width), BF16),
                pltpu.VMEM((total, width), BF16),
                pltpu.VMEM((ranks, tile, width), F32),
                pltpu.VMEM((ranks, tile, width), F32),
                pltpu.VMEM((layers, total, width), BF16),
                pltpu.VMEM((ranks, sources, BLOCK, width), BF16),
                pltpu.VMEM((count, depth, width), BF16),
                pltpu.SemaphoreType.DMA((ranks,)),
                pltpu.SemaphoreType.DMA((layers, count)),
                pltpu.SemaphoreType.DMA((ranks,)),
            ],
        ),
        out_shape=[pltpu.HBM(rows.shape, BF16)] + [(pltpu.VMEM if near else pltpu.HBM)(part, BF16)] * 2,
        compiler_params=pltpu.CompilerParams(vmem_limit_bytes=48 * MB if near else VMEM),
        cost_estimate=pl.CostEstimate(
            flops=24 * total * width * width,
            bytes_accessed=5 * total * width * 2 + width * width * 4,
            transcendentals=total * width,
        ),
        name="head_mirror" if near else "head_own",
    )(bit.reshape(1), *map(hbm, (rows, *parts, *tokens)))


def place_kernel(half, info_ref, own_ref, mirror_ref, out_ref):
    dataset, _, place = block_place(info_ref, pl.program_id(0))
    is_own = dataset // half == place // half
    out_ref[0] = jnp.where(is_own, own_ref[0, 0], mirror_ref[0, 0])


def place_rows(info, own, mirror, row_blocks):
    half, _, _, width = own.shape
    shape = (1, 1, BLOCK, width)

    def index(of_own, block, info_ref):
        dataset, rank, place = block_place(info_ref, block)
        wanted = (dataset // half == place // half) == of_own
        return jnp.where(wanted, lax.rem(dataset, half), 0), jnp.where(wanted, rank, 0), 0, 0

    return pl.pallas_call(
        functools.partial(place_kernel, half),
        grid_spec=pltpu.PrefetchScalarGridSpec(
            num_scalar_prefetch=1,
            grid=(row_blocks,),
            in_specs=[
                pl.BlockSpec(shape, functools.partial(index, True)),
                pl.BlockSpec(shape, functools.partial(index, False)),
            ],
            out_specs=pl.BlockSpec((1, BLOCK, width), lambda block, *_: (block, 0, 0)),
        ),
        out_shape=jax.ShapeDtypeStruct((row_blocks, BLOCK, width), BF16),
        compiler_params=pltpu.CompilerParams(vmem_limit_bytes=16 * MB),
        name="place_rows",
    )(info, own, mirror)


def halo(cut_rows):
    count = lax.axis_size("dom")
    forward = [(i, i + 1) for i in range(count - 1)]
    backward = [(target, source) for source, target in forward]
    low = lax.ppermute(cut_rows, "dom", forward)
    high = lax.ppermute(cut_rows, "dom", backward)
    return low, high


def exchange(blocks, half):
    groups = [list(range(half)), list(range(half, 2 * half))]
    return lax.all_to_all(
        blocks, "head", split_axis=0, concat_axis=0, axis_index_groups=groups, tiled=True
    )


def across(array, half):
    return lax.ppermute(array, "head", [(i, (i + half) % (2 * half)) for i in range(2 * half)])


def after(array, *tokens):
    return pl.pallas_call(
        lambda *refs: None,
        in_specs=[ANY] * (1 + len(tokens)),
        out_specs=ANY,
        out_shape=pltpu.HBM(array.shape, array.dtype),
        input_output_aliases={0: 0},
        compiler_params=pltpu.CompilerParams(vmem_limit_bytes=VMEM),
        name="after",
    )(hbm(array), *map(hbm, tokens))


def swap(array, bit):
    count = lax.axis_size("dom")
    return lax.ppermute(array, "dom", [(i, i ^ (1 << bit)) for i in range(count)])


def merge_kernel(first, tokens, bit_ref, keep_ref, got_ref, *refs):
    send_ref, kept_ref = refs[tokens:]
    bit = bit_ref[0]
    for layer in range(send_ref.shape[0]):
        for j in range(kept_ref.shape[1]):
            for out_ref, at in ((kept_ref, 2 * j + bit), (send_ref, 2 * j + 1 - bit)):
                keep = keep_ref[first + layer, at].astype(F32)
                out_ref[layer, j] = (keep + got_ref[first + layer, at].astype(F32)).astype(BF16)


def merge(keep, got, bit, first, layers, tokens):
    _, count, depth, width = keep.shape
    mine = (lax.axis_index("dom").astype(jnp.int32) >> bit) & 1
    shape = (layers, count // 2, depth, width)
    return pl.pallas_call(
        functools.partial(merge_kernel, first, len(tokens)),
        grid_spec=pltpu.PrefetchScalarGridSpec(
            num_scalar_prefetch=1,
            grid=(1,),
            in_specs=[IN_VMEM, IN_VMEM] + [ANY] * len(tokens),
            out_specs=[IN_VMEM] * 2,
        ),
        out_shape=[pltpu.VMEM(shape, BF16)] * 2,
        compiler_params=pltpu.CompilerParams(vmem_limit_bytes=16 * MB),
        name="merge_shares",
    )(mine.reshape(1), keep, got, *tokens)


def sum_over_dom(keep, got, first, layers, *tokens):
    bits = lax.axis_size("dom").bit_length() - 1
    for bit in range(1, bits):
        send, keep = merge(keep, got, bit, first, layers, tokens)
        got = swap(send, bit)
        first = 0
    return keep[:, 0], got[:, 0], send


def add_kernel(keep_ref, got_ref, *refs):
    refs[-1][...] = (keep_ref[...].astype(F32) + got_ref[...].astype(F32)).astype(BF16)


def add(keep, got, *tokens):
    return pl.pallas_call(
        add_kernel,
        in_specs=[IN_VMEM, IN_VMEM] + [ANY] * len(tokens),
        out_specs=IN_VMEM,
        out_shape=pltpu.VMEM(keep.shape, BF16),
        compiler_params=pltpu.CompilerParams(vmem_limit_bytes=16 * MB),
        name="add_shares",
    )(keep, got, *tokens)


def total_kernel(keep_ref, got_ref, far_ref, *refs):
    total = keep_ref[0].astype(F32) + got_ref[0].astype(F32) + far_ref[0].astype(F32)
    refs[-1][0] = total


def total(keep, got, far, layer, out=None, *tokens):
    _, depth, width = keep.shape
    mine = pl.BlockSpec((1, depth, width), lambda t: (layer, 0, 0))
    came = pl.BlockSpec((1, depth, width), lambda t: (0, 0, 0))
    tokens = list(map(hbm, tokens if out is None else (out,) + tokens))
    return pl.pallas_call(
        total_kernel,
        grid=(1,),
        in_specs=[mine, mine, came] + [ANY] * len(tokens),
        out_specs=mine,
        out_shape=pltpu.HBM(keep.shape, F32),
        input_output_aliases={} if out is None else {3: 0},
        compiler_params=pltpu.CompilerParams(vmem_limit_bytes=16 * MB),
        name="total_share",
    )(keep, got, far, *tokens)


def body(atoms, bonds, triplets, halo_ids, counts, enc_weight, gate_gain, head_weight):
    atom_rows = atoms[0]
    row_count, width = atom_rows.shape
    row_blocks = row_count // BLOCK
    half = lax.axis_size("head") // 2

    count = lax.axis_size("dom")

    def gather(shard):
        return lax.all_gather(shard, "dom", axis=0, tiled=False)

    own_weights = [gather(head_weight[0])]
    picked, *layers = pick_rows(atom_rows, halo_ids, head_weight)
    far = [across(layer, half) for layer in layers]
    low, high = halo(picked)
    extended = row_count + 2 * low.shape[0]
    codes = ((triplets[0] // LANES) * extended + bonds[0]).reshape(-1)
    place = lax.axis_index("head").astype(jnp.int32).reshape(1, 1)
    info = jnp.concatenate([counts, place], axis=1)
    own_blocks, mirror_blocks = encode(
        info, codes, atom_rows, low, high, enc_weight, gate_gain[None, :],
        bonds[0].T, (triplets[0] % LANES).T, half
    )
    near = after(far[0], own_blocks)
    own_rows = exchange(after(own_blocks, near), half)
    mirror_weights = [gather(near), gather(after(far[1], own_rows))]
    mirror_rows = exchange(after(mirror_blocks, own_rows), half)

    scale = 1.0 / math.sqrt(count * row_count)
    back, own_send, own_keep = run_head(own_rows, own_weights, scale, False)
    own_back = exchange(after(back, mirror_rows), half)
    own_got = swap(own_send, 0)

    back, send, keep = run_head(mirror_rows, mirror_weights, scale, True, own_send)
    mirror_back = exchange(after(back, own_back), half)
    got = swap(send, 0)
    high_keep, high_got, high_sent = sum_over_dom(keep, got, 1, 1)
    high_sum = add(high_keep, high_got)
    high_part = across(high_sum, half)
    low_keep, low_got, _ = sum_over_dom(keep, got, 0, 1, high_sum)
    low_sum = add(low_keep, low_got, high_part)
    low_part = across(low_sum, half)
    own_keep, own_got, _ = sum_over_dom(own_keep, own_got, 0, 2, low_sum)
    row_part = place_rows(info, own_back, mirror_back, row_blocks)
    head_part = total(own_keep, own_got, high_part, 1, None, row_part)
    head_part = total(own_keep, own_got, low_part, 0, head_part)
    return row_part.reshape(1, row_count, width), head_part[None]


def solution(mesh):
    return jax.shard_map(
        body,
        mesh=mesh,
        in_specs=(
            P("dom", "head", None),
            P("dom", None, "head"),
            P("dom", None, "head"),
            P("dom", "head"),
            P("dom", "head"),
            P(),
            P(),
            P("head", None, "dom", None),
        ),
        out_specs=(P("dom", "head", None), P("head", None, "dom", None)),
        check_vma=False,
    )
```

```python
import functools
import math

import jax
import jax.numpy as jnp
from jax import lax
from jax.experimental import pallas as pl
from jax.experimental.pallas import tpu as pltpu
from jax.sharding import PartitionSpec as P

BLOCK = 128
LANES = 128
MB = 1 << 20
VMEM = 58 * MB
F32 = jnp.float32
BF16 = jnp.bfloat16
ANY = pl.BlockSpec(memory_space=pl.ANY)
IN_VMEM = pl.BlockSpec(memory_space=pltpu.VMEM)


def sigmoid(x):
    return 0.5 + 0.5 * jnp.tanh(0.5 * x)


def hbm(array):
    return pltpu.with_memory_space_constraint(array, pltpu.HBM)


def resident(shape):
    return pl.BlockSpec(shape, lambda *_: (0,) * len(shape))


def pick_kernel(ids_ref, rows_ref, shard_ref, out_ref, first_ref, last_ref, held, sems):
    cut = first_ref.shape[1]
    load = pltpu.make_async_copy(shard_ref.at[0], held, sems.at[0])
    stores = [
        pltpu.make_async_copy(held.at[:, pl.ds(at, ref.shape[1])], ref, sems.at[i])
        for i, ref, at in ((1, first_ref, 0), (2, last_ref, cut))
    ]
    load.start()
    count, total = out_ref.shape[0], rows_ref.shape[0]
    places = lax.broadcasted_iota(jnp.int32, (total, count), 0)
    ones = jnp.where(places == ids_ref[...], 1.0, 0.0).astype(BF16)
    out_ref[...] = lax.dot_general(
        ones, rows_ref[...], (((0,), (0,)), ((), ())), preferred_element_type=F32
    ).astype(BF16)
    load.wait()
    for store in stores:
        store.start()
    for store in stores:
        store.wait()


def pick_rows(rows, ids, shard):
    _, layers, depth, width = shard.shape
    cut = depth * 5 // 8
    return pl.pallas_call(
        pick_kernel,
        in_specs=[IN_VMEM, IN_VMEM, ANY],
        out_specs=[IN_VMEM, ANY, ANY],
        out_shape=[
            jax.ShapeDtypeStruct((ids.shape[1], rows.shape[1]), rows.dtype),
            pltpu.HBM((layers, cut, width), shard.dtype),
            pltpu.HBM((layers, depth - cut, width), shard.dtype),
        ],
        scratch_shapes=[pltpu.VMEM(shard.shape[1:], shard.dtype), pltpu.SemaphoreType.DMA((3,))],
        compiler_params=pltpu.CompilerParams(vmem_limit_bytes=16 * MB),
        name="pick_rows",
    )(ids, rows, hbm(shard))


def block_place(info_ref, block):
    sets = info_ref.shape[1] - 1
    start, dataset, rank = jnp.int32(0), jnp.int32(0), jnp.int32(0)
    for candidate in range(sets):
        blocks = info_ref[0, candidate] // BLOCK
        inside = jnp.logical_and(block >= start, block < start + blocks)
        dataset = jnp.where(inside, candidate, dataset)
        rank = jnp.where(inside, block - start, rank)
        start = start + blocks
    return dataset, rank, info_ref[0, sets]


def encode_kernel(
    half, batch, info_ref, codes_ref, atoms_ref, low_ref, high_ref, weight_ref, gain_ref,
    pairs_ref, own_ref, mirror_ref, gained, scores, partial, wanted, gates, gate_rows, staged,
    zeros, weight, sems, weight_sem,
):
    rows, width = atoms_ref.shape
    depth = low_ref.shape[0]
    bond_count = pairs_ref.shape[1]
    sets = 2 * half
    weight_in = pltpu.make_async_copy(weight_ref, weight, weight_sem)
    weight_in.start()
    home = info_ref[0, sets] // half * half
    tile = batch * BLOCK

    def leave(source, slot, act):
        def one(ref, at):
            act(pltpu.make_async_copy(source, ref.at[at], sems.at[slot]))

        pl.when(slot < sets)(lambda: one(own_ref, slot))
        pl.when(slot >= sets)(lambda: one(mirror_ref, slot - sets))

    zeros[...] = jnp.zeros_like(zeros)

    def blank(slot, carry):
        dataset = lax.rem(home + slot // 2, sets)
        empty = info_ref[0, dataset] // BLOCK <= lax.rem(slot, 2)
        pl.when(empty)(lambda: leave(zeros, slot, lambda copy: copy.start()))
        return carry

    lax.fori_loop(0, 2 * sets, blank, 0)

    extended = rows + 2 * depth
    parts = ((atoms_ref, 0), (low_ref, rows), (high_ref, rows + depth))
    for ref, at in parts:
        gained[at : at + ref.shape[0], :] = (ref[...].astype(F32) * gain_ref[...]).astype(BF16)
    for ref, base in parts:
        step = min(ref.shape[0], 2 * LANES)
        for at in range(0, ref.shape[0], step):
            value = lax.dot_general(
                gained[...], ref[at : at + step, :], (((1,), (1,)), ((), ())),
                preferred_element_type=F32,
            )
            for k in range(0, step, LANES):
                piece = (base + at + k) // LANES
                scores[piece * extended : (piece + 1) * extended, :] = value[:, k : k + LANES]

    def encode_tile(step, carry):
        base = pl.multiple_of(step * tile, tile)

        def score(group, carry):
            for bond in range(bond_count):
                at = bond * rows + base + group * 8
                place = pl.multiple_of(bond * tile + group * 8, 8)
                for j in range(8):
                    partial[pl.ds(place + j, 1), :] = scores[pl.ds(codes_ref[at + j], 1), :]
            return carry

        lax.fori_loop(0, tile // 8, score, 0)
        places = lax.broadcasted_iota(jnp.int32, (BLOCK, LANES), 1)
        for block in range(batch):
            pairs = pairs_ref[pl.ds(base + block * BLOCK, BLOCK), :]
            for bond in range(bond_count):
                at = bond * tile + block * BLOCK
                pair = jnp.broadcast_to(pairs[:, bond : bond + 1], (BLOCK, LANES))
                wanted[bond] = pair // LANES
                picked = places == pair % LANES
                logits = jnp.sum(
                    jnp.where(picked, partial[at : at + BLOCK, :], 0.0), axis=1, keepdims=True
                )
                gate = sigmoid(logits * (1.0 / math.sqrt(width)))
                gates[bond] = jnp.broadcast_to(gate, (BLOCK, LANES))
            for at in range(0, extended, LANES):
                acc = jnp.zeros((BLOCK, LANES), F32)
                for bond in range(bond_count):
                    acc = acc + jnp.where(wanted[bond] == places + at, gates[bond], 0.0)
                gate_rows[block * BLOCK : (block + 1) * BLOCK, at : at + LANES] = acc.astype(BF16)
        message = jnp.dot(gate_rows[:, :rows], atoms_ref[...], preferred_element_type=F32)
        for ref, at in ((low_ref, rows), (high_ref, rows + depth)):
            message += jnp.dot(
                gate_rows[:, at : at + depth], ref[...], preferred_element_type=F32
            )
        pl.when(step == 0)(lambda: weight_in.wait())
        update = jnp.dot(message.astype(BF16), weight[...], preferred_element_type=F32)
        own = atoms_ref[pl.ds(base, tile), :].astype(F32)
        staged[step] = (own + update * sigmoid(update)).astype(BF16).reshape(staged.shape[1:])
        for block in range(batch):
            dataset, rank, _ = block_place(info_ref, step * batch + block)
            slot = lax.rem(dataset - home + sets, sets) * 2 + rank
            leave(staged.at[step, block], slot, lambda copy: copy.start())
        return carry

    lax.fori_loop(0, rows // tile, encode_tile, 0)

    def settle(slot, carry):
        leave(zeros, slot, lambda copy: copy.wait())
        return carry

    lax.fori_loop(0, 2 * sets, settle, 0)


def encode(info, codes, atoms, low, high, weight, gain, pairs, half):
    rows, width = atoms.shape
    depth = low.shape[0]
    extended = rows + 2 * depth
    bond_count = pairs.shape[1]
    slots = 4 * half
    row_blocks = rows // BLOCK
    batch = 4 if row_blocks % 4 == 0 else 1
    blocks = pl.pallas_call(
        functools.partial(encode_kernel, half, batch),
        grid_spec=pltpu.PrefetchScalarGridSpec(
            num_scalar_prefetch=2,
            grid=(1,),
            in_specs=[
                resident((rows, width)),
                resident((depth, width)),
                resident((depth, width)),
                ANY,
                resident((1, width)),
                resident((rows, bond_count)),
            ],
            out_specs=[pl.BlockSpec(memory_space=pltpu.HBM)] * 2,
            scratch_shapes=[
                pltpu.VMEM((extended, width), BF16),
                pltpu.VMEM((extended // LANES * extended, LANES), F32),
                pltpu.VMEM((batch * BLOCK * bond_count, LANES), F32),
                pltpu.VMEM((bond_count, BLOCK, LANES), jnp.int32),
                pltpu.VMEM((bond_count, BLOCK, LANES), F32),
                pltpu.VMEM((batch * BLOCK, extended), BF16),
                pltpu.VMEM((row_blocks // batch, batch, BLOCK, width), BF16),
                pltpu.VMEM((BLOCK, width), BF16),
                pltpu.VMEM((width, width), BF16),
                pltpu.SemaphoreType.DMA((slots,)),
                pltpu.SemaphoreType.DMA(()),
            ],
        ),
        out_shape=[pltpu.HBM((2 * half, BLOCK, width), BF16)] * 2,
        compiler_params=pltpu.CompilerParams(vmem_limit_bytes=44 * MB),
        cost_estimate=pl.CostEstimate(
            flops=40 * rows * width * width,
            bytes_accessed=30 * MB,
            transcendentals=rows * width,
        ),
        name="encode_rows",
    )(info, codes, atoms, low, high, hbm(weight), gain, pairs)
    return [rows.reshape(half, 2, BLOCK, width) for rows in blocks]


def head_kernel(scale, part_count, tokens, bit_ref, rows_ref, *refs):
    weight_refs = refs[:part_count]
    (
        back_ref, send_ref, keep_ref, x, weights, act, slope, err, grad, back, shares,
        in_sems, weight_sems, back_sems,
    ) = refs[part_count + tokens :]
    width = x.shape[-1]
    tile = x.shape[1] * x.shape[2]
    count = weights.shape[1]
    chunk = width // 4
    chunks = [slice(at, at + chunk) for at in range(0, width, chunk)]
    transposed = (((1,), (1,)), ((), ()))
    over_rows = (((0,), (0,)), ((), ()))
    bit = bit_ref[0]

    def rows_in(rank):
        return pltpu.make_async_copy(rows_ref.at[:, rank], x.at[rank], in_sems.at[rank])

    def weights_in(layer):
        copies = []
        at = 0
        for ref in weight_refs:
            depth = ref.shape[2]
            for i in range(count):
                place = weights.at[layer, i, pl.ds(at, depth)]
                sem = weight_sems.at[layer, len(copies)]
                copies.append(pltpu.make_async_copy(ref.at[i, layer], place, sem))
            at += depth
        return copies

    def back_out(rank):
        return pltpu.make_async_copy(back.at[rank], back_ref.at[:, rank], back_sems.at[rank])

    def matrix(layer):
        return weights[layer].reshape(width, width)

    def forward(rank, wait):
        inputs = x[rank].reshape(tile, width)
        low = matrix(0)
        for at in chunks:
            z = jnp.dot(inputs, low[:, at], preferred_element_type=F32)
            s = sigmoid(z)
            act[rank * tile : (rank + 1) * tile, at] = (z * s).astype(BF16)
            slope[rank, :, at] = s * (1.0 + z * (1.0 - s))
        if wait:
            for copy in weights_in(1):
                copy.wait()
        acts = act[rank * tile : (rank + 1) * tile, :]
        high = matrix(1)
        for at in chunks:
            value = jnp.dot(acts, high[:, at], preferred_element_type=F32)
            value = value - inputs[:, at].astype(F32)
            err[rank, :, at] = value
            grad[1, rank * tile : (rank + 1) * tile, at] = value.astype(BF16)

    def backward(rank):
        rows = slice(rank * tile, (rank + 1) * tile)
        grads = grad[1, rows, :]
        high = matrix(1)
        for at in chunks:
            up = lax.dot_general(grads, high[at, :], transposed, preferred_element_type=F32)
            grad[0, rows, at] = (up * slope[rank, :, at]).astype(BF16)
        grads = grad[0, rows, :]
        low = matrix(0)
        shape = x.shape[1:3] + (chunk,)
        for at in chunks:
            up = lax.dot_general(grads, low[at, :], transposed, preferred_element_type=F32)
            back[rank, :, :, at] = (up - err[rank, :, at]).astype(BF16).reshape(shape)

    def share(layer, acts, rows):
        value = lax.dot_general(
            acts, grad[layer, :rows, :], over_rows, preferred_element_type=F32
        )
        shares[...] = (value * scale).astype(BF16).reshape(shares.shape)
        for j in range(count // 2):
            keep_ref[layer, j] = shares[2 * j + bit]
            send_ref[layer, j] = shares[2 * j + 1 - bit]

    for rank in range(2):
        rows_in(rank).start()
    for layer in range(2):
        for copy in weights_in(layer):
            copy.start()
    rows_in(0).wait()
    for copy in weights_in(0):
        copy.wait()
    forward(0, True)
    rows_in(1).wait()
    some = jnp.max(jnp.abs(x[1].reshape(tile, width).astype(F32))) > 0
    none = jnp.logical_not(some)
    pl.when(some)(lambda: forward(1, False))
    pl.when(some)(lambda: share(1, act[...], 2 * tile))
    pl.when(none)(lambda: share(1, act[:tile, :], tile))
    backward(0)
    back_out(0).start()
    pl.when(some)(lambda: backward(1))

    @pl.when(none)
    def _():
        back[1] = jnp.zeros(back.shape[1:], BF16)

    back_out(1).start()
    pl.when(some)(lambda: share(0, x[...].reshape(2 * tile, width), 2 * tile))
    pl.when(none)(lambda: share(0, x[0].reshape(tile, width), tile))
    for rank in range(2):
        back_out(rank).wait()


def run_head(rows, parts, scale, name, *tokens):
    sources, ranks, _, width = rows.shape
    count = parts[0].shape[0]
    depth = width // count
    layers = 2
    tile = sources * BLOCK
    total = ranks * tile
    part = (layers, count // 2, depth, width)
    bit = lax.axis_index("dom").astype(jnp.int32) & 1
    return pl.pallas_call(
        functools.partial(head_kernel, scale, len(parts), len(tokens)),
        grid_spec=pltpu.PrefetchScalarGridSpec(
            num_scalar_prefetch=1,
            grid=(1,),
            in_specs=[ANY] * (1 + len(parts) + len(tokens)),
            out_specs=[ANY, IN_VMEM, IN_VMEM],
            scratch_shapes=[
                pltpu.VMEM((ranks, sources, BLOCK, width), BF16),
                pltpu.VMEM((layers, count, depth, width), BF16),
                pltpu.VMEM((total, width), BF16),
                pltpu.VMEM((ranks, tile, width), F32),
                pltpu.VMEM((ranks, tile, width), F32),
                pltpu.VMEM((layers, total, width), BF16),
                pltpu.VMEM((ranks, sources, BLOCK, width), BF16),
                pltpu.VMEM((count, depth, width), BF16),
                pltpu.SemaphoreType.DMA((ranks,)),
                pltpu.SemaphoreType.DMA((layers, count * len(parts))),
                pltpu.SemaphoreType.DMA((ranks,)),
            ],
        ),
        out_shape=[pltpu.HBM(rows.shape, BF16)] + [pltpu.VMEM(part, BF16)] * 2,
        compiler_params=pltpu.CompilerParams(vmem_limit_bytes=(20 + 28 * tile // 1024) * MB),
        cost_estimate=pl.CostEstimate(
            flops=24 * total * width * width,
            bytes_accessed=5 * total * width * 2 + width * width * 4,
            transcendentals=total * width,
        ),
        name=name,
    )(bit.reshape(1), rows, *map(hbm, parts), *tokens)


def place_kernel(half, info_ref, own_ref, mirror_ref, out_ref):
    dataset, _, place = block_place(info_ref, pl.program_id(0))
    is_own = dataset // half == place // half
    out_ref[0] = jnp.where(is_own, own_ref[0, 0], mirror_ref[0, 0])


def place_rows(info, own, mirror, row_blocks):
    half, _, _, width = own.shape
    shape = (1, 1, BLOCK, width)

    def index(of_own, block, info_ref):
        dataset, rank, place = block_place(info_ref, block)
        wanted = (dataset // half == place // half) == of_own
        return jnp.where(wanted, lax.rem(dataset, half), 0), jnp.where(wanted, rank, 0), 0, 0

    return pl.pallas_call(
        functools.partial(place_kernel, half),
        grid_spec=pltpu.PrefetchScalarGridSpec(
            num_scalar_prefetch=1,
            grid=(row_blocks,),
            in_specs=[
                pl.BlockSpec(shape, functools.partial(index, True)),
                pl.BlockSpec(shape, functools.partial(index, False)),
            ],
            out_specs=pl.BlockSpec((1, BLOCK, width), lambda block, *_: (block, 0, 0)),
        ),
        out_shape=jax.ShapeDtypeStruct((row_blocks, BLOCK, width), BF16),
        compiler_params=pltpu.CompilerParams(vmem_limit_bytes=16 * MB),
        name="place_rows",
    )(info, own, mirror)


def halo(cut_rows):
    count = lax.axis_size("dom")
    forward = [(i, i + 1) for i in range(count - 1)]
    backward = [(target, source) for source, target in forward]
    low = lax.ppermute(cut_rows, "dom", forward)
    high = lax.ppermute(cut_rows, "dom", backward)
    return low, high


def exchange(blocks, half):
    groups = [list(range(half)), list(range(half, 2 * half))]
    return lax.all_to_all(
        blocks, "head", split_axis=0, concat_axis=0, axis_index_groups=groups, tiled=True
    )


def across(array, half):
    return lax.ppermute(array, "head", [(i, (i + half) % (2 * half)) for i in range(2 * half)])


def after(array, *tokens):
    return pl.pallas_call(
        lambda *refs: None,
        in_specs=[ANY] * (1 + len(tokens)),
        out_specs=ANY,
        out_shape=pltpu.HBM(array.shape, array.dtype),
        input_output_aliases={0: 0},
        compiler_params=pltpu.CompilerParams(vmem_limit_bytes=48 * MB),
        name="after",
    )(hbm(array), *tokens)


def swap(array, bit):
    count = lax.axis_size("dom")
    return lax.ppermute(array, "dom", [(i, i ^ (1 << bit)) for i in range(count)])


def merge_kernel(first, tokens, bit_ref, keep_ref, got_ref, *refs):
    send_ref, kept_ref = refs[tokens:]
    bit = bit_ref[0]
    for layer in range(send_ref.shape[0]):
        for j in range(kept_ref.shape[1]):
            for out_ref, at in ((kept_ref, 2 * j + bit), (send_ref, 2 * j + 1 - bit)):
                keep = keep_ref[first + layer, at].astype(F32)
                out_ref[layer, j] = (keep + got_ref[first + layer, at].astype(F32)).astype(BF16)


def merge(keep, got, bit, first, layers, tokens):
    _, count, depth, width = keep.shape
    mine = (lax.axis_index("dom").astype(jnp.int32) >> bit) & 1
    shape = (layers, count // 2, depth, width)
    return pl.pallas_call(
        functools.partial(merge_kernel, first, len(tokens)),
        grid_spec=pltpu.PrefetchScalarGridSpec(
            num_scalar_prefetch=1,
            grid=(1,),
            in_specs=[IN_VMEM, IN_VMEM] + [ANY] * len(tokens),
            out_specs=[IN_VMEM] * 2,
        ),
        out_shape=[pltpu.VMEM(shape, BF16)] * 2,
        compiler_params=pltpu.CompilerParams(vmem_limit_bytes=16 * MB),
        name="merge_shares",
    )(mine.reshape(1), keep, got, *tokens)


def merge_whole_kernel(keep_ref, got_ref, out_ref):
    for layer in range(keep_ref.shape[0]):
        for j in range(keep_ref.shape[1]):
            keep = keep_ref[layer, j].astype(F32)
            out_ref[j, layer] = (keep + got_ref[layer, j].astype(F32)).astype(BF16)


def merge_whole(keep, got):
    layers, count, depth, width = keep.shape
    shape = (count, layers, depth, width)
    return pl.pallas_call(
        merge_whole_kernel,
        in_specs=[IN_VMEM, IN_VMEM],
        out_specs=resident(shape),
        grid=(1,),
        out_shape=pltpu.HBM(shape, BF16),
        compiler_params=pltpu.CompilerParams(vmem_limit_bytes=20 * MB),
        name="merge_whole",
    )(keep, got)


def sum_over_dom(keep, got, first, layers, *tokens):
    bits = lax.axis_size("dom").bit_length() - 1
    for bit in range(1, bits):
        send, keep = merge(keep, got, bit, first, layers, tokens)
        got = swap(send, bit)
        first = 0
    return keep[:, 0], got[:, 0], send


def add_kernel(keep_ref, got_ref, *refs):
    refs[-1][...] = (keep_ref[...].astype(F32) + got_ref[...].astype(F32)).astype(BF16)


def add(keep, got, *tokens):
    return pl.pallas_call(
        add_kernel,
        in_specs=[IN_VMEM, IN_VMEM] + [ANY] * len(tokens),
        out_specs=IN_VMEM,
        out_shape=pltpu.VMEM(keep.shape, BF16),
        compiler_params=pltpu.CompilerParams(vmem_limit_bytes=16 * MB),
        name="add_shares",
    )(keep, got, *tokens)


def total_kernel(sum_ref, far_ref, *refs):
    refs[-1][0] = sum_ref[0].astype(F32) + far_ref[0].astype(F32)


def total(own, far, layer, out=None, *tokens):
    _, depth, width = own.shape
    mine = pl.BlockSpec((1, depth, width), lambda t: (layer, 0, 0))
    came = pl.BlockSpec((1, depth, width), lambda t: (0, 0, 0))
    tokens = list(map(hbm, tokens if out is None else (out,) + tokens))
    return pl.pallas_call(
        total_kernel,
        grid=(1,),
        in_specs=[mine, came] + [ANY] * len(tokens),
        out_specs=mine,
        out_shape=pltpu.HBM(own.shape, F32),
        input_output_aliases={} if out is None else {2: 0},
        compiler_params=pltpu.CompilerParams(vmem_limit_bytes=16 * MB),
        name="total_share",
    )(own, far, *tokens)


def body(atoms, bonds, triplets, halo_ids, counts, enc_weight, gate_gain, head_weight):
    atom_rows = atoms[0]
    row_count, width = atom_rows.shape
    row_blocks = row_count // BLOCK
    half = lax.axis_size("head") // 2

    count = lax.axis_size("dom")

    def gather(shard):
        return lax.all_gather(shard, "dom", axis=0, tiled=False)

    own_weights = [gather(head_weight[0])]
    picked, *pieces = pick_rows(atom_rows, halo_ids, head_weight)
    far = [across(piece, half) for piece in pieces]
    low, high = halo(picked)
    extended = row_count + 2 * low.shape[0]
    codes = ((triplets[0] // LANES) * extended + bonds[0]).reshape(-1)
    pairs = (bonds[0] * LANES + triplets[0] % LANES).T
    place = lax.axis_index("head").astype(jnp.int32).reshape(1, 1)
    info = jnp.concatenate([counts, place], axis=1)
    own_blocks, mirror_blocks = encode(
        info, codes, atom_rows, low, high, enc_weight, gate_gain[None, :], pairs, half
    )
    near = after(far[0], hbm(own_blocks))
    own_rows = exchange(after(own_blocks, hbm(near)), half)
    mirror_weights = [gather(near), gather(after(far[1], own_rows))]
    mirror_rows = exchange(after(mirror_blocks, own_rows), half)

    scale = 1.0 / math.sqrt(count * row_count)
    back, send, keep = run_head(own_rows, own_weights, scale, "head_own")
    own_back = exchange(back, half)
    own_sum = merge_whole(keep, swap(send, 0))

    back, send, keep = run_head(mirror_rows, mirror_weights, scale, "head_mirror", hbm(own_sum))
    got = swap(send, 0)
    high_keep, high_got, high_sent = sum_over_dom(keep, got, 1, 1)
    high_sum = add(high_keep, high_got)
    high_part = across(high_sum, half)
    mirror_back = exchange(after(back, high_sum), half)
    low_keep, low_got, _ = sum_over_dom(keep, got, 0, 1, high_sum)
    low_sum = add(low_keep, low_got, high_part)
    low_part = across(low_sum, half)
    same_core = [[i for i in range(count) if i % 2 == core] for core in range(2)]
    own_sum = lax.psum_scatter(
        own_sum, "dom", scatter_dimension=0, axis_index_groups=same_core, tiled=False
    )
    row_part = place_rows(info, own_back, mirror_back, row_blocks)
    head_part = total(own_sum, high_part, 1, None, row_part)
    head_part = total(own_sum, low_part, 0, head_part)
    return row_part.reshape(1, row_count, width), head_part[None]


def solution(mesh):
    return jax.shard_map(
        body,
        mesh=mesh,
        in_specs=(
            P("dom", "head", None),
            P("dom", None, "head"),
            P("dom", None, "head"),
            P("dom", "head"),
            P("dom", "head"),
            P(),
            P(),
            P("head", None, "dom", None),
        ),
        out_specs=(P("dom", "head", None), P("head", None, "dom", None)),
        check_vma=False,
    )
```

```python
import functools
import math

import jax
import jax.numpy as jnp
from jax import lax
from jax.experimental import pallas as pl
from jax.experimental.pallas import tpu as pltpu
from jax.sharding import PartitionSpec as P

BLOCK = 128
LANES = 128
MB = 1 << 20
VMEM = 58 * MB
F32 = jnp.float32
BF16 = jnp.bfloat16
ANY = pl.BlockSpec(memory_space=pl.ANY)
IN_VMEM = pl.BlockSpec(memory_space=pltpu.VMEM)


def sigmoid(x):
    return 0.5 + 0.5 * jnp.tanh(0.5 * x)


def hbm(array):
    return pltpu.with_memory_space_constraint(array, pltpu.HBM)


def resident(shape):
    return pl.BlockSpec(shape, lambda *_: (0,) * len(shape))


def pick_kernel(ids_ref, rows_ref, shard_ref, out_ref, first_ref, last_ref, held, sems):
    cut = first_ref.shape[1]
    load = pltpu.make_async_copy(shard_ref.at[0], held, sems.at[0])
    stores = [
        pltpu.make_async_copy(held.at[:, pl.ds(at, ref.shape[1])], ref, sems.at[i])
        for i, ref, at in ((1, first_ref, 0), (2, last_ref, cut))
    ]
    load.start()
    count, total = out_ref.shape[0], rows_ref.shape[0]
    places = lax.broadcasted_iota(jnp.int32, (total, count), 0)
    ones = jnp.where(places == ids_ref[...], 1.0, 0.0).astype(BF16)
    out_ref[...] = lax.dot_general(
        ones, rows_ref[...], (((0,), (0,)), ((), ())), preferred_element_type=F32
    ).astype(BF16)
    load.wait()
    for store in stores:
        store.start()
    for store in stores:
        store.wait()


def pick_rows(rows, ids, shard):
    _, layers, depth, width = shard.shape
    cut = depth * 5 // 8
    return pl.pallas_call(
        pick_kernel,
        in_specs=[IN_VMEM, IN_VMEM, ANY],
        out_specs=[IN_VMEM, ANY, ANY],
        out_shape=[
            jax.ShapeDtypeStruct((ids.shape[1], rows.shape[1]), rows.dtype),
            pltpu.HBM((layers, cut, width), shard.dtype),
            pltpu.HBM((layers, depth - cut, width), shard.dtype),
        ],
        scratch_shapes=[pltpu.VMEM(shard.shape[1:], shard.dtype), pltpu.SemaphoreType.DMA((3,))],
        compiler_params=pltpu.CompilerParams(vmem_limit_bytes=16 * MB),
        name="pick_rows",
    )(ids, rows, hbm(shard))


def block_place(info_ref, block):
    sets = info_ref.shape[1] - 1
    start, dataset, rank = jnp.int32(0), jnp.int32(0), jnp.int32(0)
    for candidate in range(sets):
        blocks = info_ref[0, candidate] // BLOCK
        inside = jnp.logical_and(block >= start, block < start + blocks)
        dataset = jnp.where(inside, candidate, dataset)
        rank = jnp.where(inside, block - start, rank)
        start = start + blocks
    return dataset, rank, info_ref[0, sets]


def encode_kernel(
    half, batch, info_ref, codes_ref, atoms_ref, low_ref, high_ref, weight_ref, gain_ref,
    pairs_ref, own_ref, mirror_ref, gained, scores, partial, wanted, gates, gate_rows, staged,
    zeros, weight, sems, weight_sem,
):
    rows, width = atoms_ref.shape
    depth = low_ref.shape[0]
    bond_count = pairs_ref.shape[1]
    sets = 2 * half
    weight_in = pltpu.make_async_copy(weight_ref, weight, weight_sem)
    weight_in.start()
    home = info_ref[0, sets] // half * half
    tile = batch * BLOCK

    def leave(source, slot, act):
        def one(ref, at):
            act(pltpu.make_async_copy(source, ref.at[at], sems.at[slot]))

        pl.when(slot < sets)(lambda: one(own_ref, slot))
        pl.when(slot >= sets)(lambda: one(mirror_ref, slot - sets))

    zeros[...] = jnp.zeros_like(zeros)

    def blank(slot, carry):
        dataset = lax.rem(home + slot // 2, sets)
        empty = info_ref[0, dataset] // BLOCK <= lax.rem(slot, 2)
        pl.when(empty)(lambda: leave(zeros, slot, lambda copy: copy.start()))
        return carry

    lax.fori_loop(0, 2 * sets, blank, 0)

    extended = rows + 2 * depth
    parts = ((atoms_ref, 0), (low_ref, rows), (high_ref, rows + depth))
    for ref, at in parts:
        gained[at : at + ref.shape[0], :] = (ref[...].astype(F32) * gain_ref[...]).astype(BF16)
    for ref, base in parts:
        step = min(ref.shape[0], 2 * LANES)
        for at in range(0, ref.shape[0], step):
            value = lax.dot_general(
                gained[...], ref[at : at + step, :], (((1,), (1,)), ((), ())),
                preferred_element_type=F32,
            )
            for k in range(0, step, LANES):
                piece = (base + at + k) // LANES
                scores[piece * extended : (piece + 1) * extended, :] = value[:, k : k + LANES]

    def encode_tile(step, carry):
        base = pl.multiple_of(step * tile, tile)

        def score(group, carry):
            for bond in range(bond_count):
                at = bond * rows + base + group * 8
                place = pl.multiple_of(bond * tile + group * 8, 8)
                for j in range(8):
                    partial[pl.ds(place + j, 1), :] = scores[pl.ds(codes_ref[at + j], 1), :]
            return carry

        lax.fori_loop(0, tile // 8, score, 0)
        places = lax.broadcasted_iota(jnp.int32, (BLOCK, LANES), 1)
        for block in range(batch):
            pairs = pairs_ref[pl.ds(base + block * BLOCK, BLOCK), :]
            for bond in range(bond_count):
                at = bond * tile + block * BLOCK
                pair = jnp.broadcast_to(pairs[:, bond : bond + 1], (BLOCK, LANES))
                wanted[bond] = pair // LANES
                picked = places == pair % LANES
                logits = jnp.sum(
                    jnp.where(picked, partial[at : at + BLOCK, :], 0.0), axis=1, keepdims=True
                )
                gate = sigmoid(logits * (1.0 / math.sqrt(width)))
                gates[bond] = jnp.broadcast_to(gate, (BLOCK, LANES))
            for at in range(0, extended, LANES):
                acc = jnp.zeros((BLOCK, LANES), F32)
                for bond in range(bond_count):
                    acc = acc + jnp.where(wanted[bond] == places + at, gates[bond], 0.0)
                gate_rows[block * BLOCK : (block + 1) * BLOCK, at : at + LANES] = acc.astype(BF16)
        message = jnp.dot(gate_rows[:, :rows], atoms_ref[...], preferred_element_type=F32)
        for ref, at in ((low_ref, rows), (high_ref, rows + depth)):
            message += jnp.dot(
                gate_rows[:, at : at + depth], ref[...], preferred_element_type=F32
            )
        pl.when(step == 0)(lambda: weight_in.wait())
        update = jnp.dot(message.astype(BF16), weight[...], preferred_element_type=F32)
        own = atoms_ref[pl.ds(base, tile), :].astype(F32)
        staged[step] = (own + update * sigmoid(update)).astype(BF16).reshape(staged.shape[1:])
        for block in range(batch):
            dataset, rank, _ = block_place(info_ref, step * batch + block)
            slot = lax.rem(dataset - home + sets, sets) * 2 + rank
            leave(staged.at[step, block], slot, lambda copy: copy.start())
        return carry

    lax.fori_loop(0, rows // tile, encode_tile, 0)

    def settle(slot, carry):
        leave(zeros, slot, lambda copy: copy.wait())
        return carry

    lax.fori_loop(0, 2 * sets, settle, 0)


def encode(info, codes, atoms, low, high, weight, gain, pairs, half):
    rows, width = atoms.shape
    depth = low.shape[0]
    extended = rows + 2 * depth
    bond_count = pairs.shape[1]
    slots = 4 * half
    row_blocks = rows // BLOCK
    batch = 4 if row_blocks % 4 == 0 else 1
    blocks = pl.pallas_call(
        functools.partial(encode_kernel, half, batch),
        grid_spec=pltpu.PrefetchScalarGridSpec(
            num_scalar_prefetch=2,
            grid=(1,),
            in_specs=[
                resident((rows, width)),
                resident((depth, width)),
                resident((depth, width)),
                ANY,
                resident((1, width)),
                resident((rows, bond_count)),
            ],
            out_specs=[pl.BlockSpec(memory_space=pltpu.HBM)] * 2,
            scratch_shapes=[
                pltpu.VMEM((extended, width), BF16),
                pltpu.VMEM((extended // LANES * extended, LANES), F32),
                pltpu.VMEM((batch * BLOCK * bond_count, LANES), F32),
                pltpu.VMEM((bond_count, BLOCK, LANES), jnp.int32),
                pltpu.VMEM((bond_count, BLOCK, LANES), F32),
                pltpu.VMEM((batch * BLOCK, extended), BF16),
                pltpu.VMEM((row_blocks // batch, batch, BLOCK, width), BF16),
                pltpu.VMEM((BLOCK, width), BF16),
                pltpu.VMEM((width, width), BF16),
                pltpu.SemaphoreType.DMA((slots,)),
                pltpu.SemaphoreType.DMA(()),
            ],
        ),
        out_shape=[pltpu.HBM((2 * half, BLOCK, width), BF16)] * 2,
        compiler_params=pltpu.CompilerParams(vmem_limit_bytes=44 * MB),
        cost_estimate=pl.CostEstimate(
            flops=40 * rows * width * width,
            bytes_accessed=30 * MB,
            transcendentals=rows * width,
        ),
        name="encode_rows",
    )(info, codes, atoms, low, high, hbm(weight), gain, pairs)
    return [rows.reshape(half, 2, BLOCK, width) for rows in blocks]


def head_kernel(scale, offsets, tokens, table_ref, rows_ref, *refs):
    part_count = len(offsets)
    weight_refs = refs[:part_count]
    (
        back_ref, send_ref, keep_ref, x, weights, act, slope, err, grad, back, shares,
        in_sems, weight_sems, back_sems,
    ) = refs[part_count + tokens :]
    width = x.shape[-1]
    tile = x.shape[1] * x.shape[2]
    count = weights.shape[1]
    chunk = width // 4
    chunks = [slice(at, at + chunk) for at in range(0, width, chunk)]
    transposed = (((1,), (1,)), ((), ()))
    over_rows = (((0,), (0,)), ((), ()))
    bit = table_ref[0]

    def rows_in(rank):
        return pltpu.make_async_copy(rows_ref.at[:, rank], x.at[rank], in_sems.at[rank])

    def weights_in(layer):
        copies = []
        for ref, at in zip(weight_refs, offsets):
            for i in range(ref.shape[0]):
                owner = table_ref[1 + len(copies)]
                place = weights.at[layer, owner, pl.ds(at, ref.shape[2])]
                sem = weight_sems.at[layer, len(copies)]
                copies.append(pltpu.make_async_copy(ref.at[i, layer], place, sem))
        return copies

    def back_out(rank):
        return pltpu.make_async_copy(back.at[rank], back_ref.at[:, rank], back_sems.at[rank])

    def matrix(layer):
        return weights[layer].reshape(width, width)

    def forward(rank, wait):
        inputs = x[rank].reshape(tile, width)
        low = matrix(0)
        for at in chunks:
            z = jnp.dot(inputs, low[:, at], preferred_element_type=F32)
            s = sigmoid(z)
            act[rank * tile : (rank + 1) * tile, at] = (z * s).astype(BF16)
            slope[rank, :, at] = s * (1.0 + z * (1.0 - s))
        if wait:
            for copy in weights_in(1):
                copy.wait()
        acts = act[rank * tile : (rank + 1) * tile, :]
        high = matrix(1)
        for at in chunks:
            value = jnp.dot(acts, high[:, at], preferred_element_type=F32)
            value = value - inputs[:, at].astype(F32)
            err[rank, :, at] = value
            grad[1, rank * tile : (rank + 1) * tile, at] = value.astype(BF16)

    def backward(rank):
        rows = slice(rank * tile, (rank + 1) * tile)
        grads = grad[1, rows, :]
        high = matrix(1)
        for at in chunks:
            up = lax.dot_general(grads, high[at, :], transposed, preferred_element_type=F32)
            grad[0, rows, at] = (up * slope[rank, :, at]).astype(BF16)
        grads = grad[0, rows, :]
        low = matrix(0)
        shape = x.shape[1:3] + (chunk,)
        for at in chunks:
            up = lax.dot_general(grads, low[at, :], transposed, preferred_element_type=F32)
            back[rank, :, :, at] = (up - err[rank, :, at]).astype(BF16).reshape(shape)

    def share(layer, acts, rows):
        value = lax.dot_general(
            acts, grad[layer, :rows, :], over_rows, preferred_element_type=F32
        )
        shares[...] = (value * scale).astype(BF16).reshape(shares.shape)
        for j in range(count // 2):
            keep_ref[layer, j] = shares[2 * j + bit]
            send_ref[layer, j] = shares[2 * j + 1 - bit]

    for rank in range(2):
        rows_in(rank).start()
    for layer in range(2):
        for copy in weights_in(layer):
            copy.start()
    rows_in(0).wait()
    for copy in weights_in(0):
        copy.wait()
    forward(0, True)
    rows_in(1).wait()
    some = jnp.max(jnp.abs(x[1].reshape(tile, width).astype(F32))) > 0
    none = jnp.logical_not(some)
    pl.when(some)(lambda: forward(1, False))
    pl.when(some)(lambda: share(1, act[...], 2 * tile))
    pl.when(none)(lambda: share(1, act[:tile, :], tile))
    backward(0)
    back_out(0).start()
    pl.when(some)(lambda: backward(1))

    @pl.when(none)
    def _():
        back[1] = jnp.zeros(back.shape[1:], BF16)

    back_out(1).start()
    pl.when(some)(lambda: share(0, x[...].reshape(2 * tile, width), 2 * tile))
    pl.when(none)(lambda: share(0, x[0].reshape(tile, width), tile))
    for rank in range(2):
        back_out(rank).wait()


def run_head(rows, parts, scale, name, *tokens):
    sources, ranks, _, width = rows.shape
    count = lax.axis_size("dom")
    arrays, offsets, owners = zip(*parts)
    owners = [owner for group in owners for owner in group]
    depth = width // count
    layers = 2
    tile = sources * BLOCK
    total = ranks * tile
    part = (layers, count // 2, depth, width)
    bit = lax.axis_index("dom").astype(jnp.int32) & 1
    return pl.pallas_call(
        functools.partial(head_kernel, scale, offsets, len(tokens)),
        grid_spec=pltpu.PrefetchScalarGridSpec(
            num_scalar_prefetch=1,
            grid=(1,),
            in_specs=[ANY] * (1 + len(parts) + len(tokens)),
            out_specs=[ANY, IN_VMEM, IN_VMEM],
            scratch_shapes=[
                pltpu.VMEM((ranks, sources, BLOCK, width), BF16),
                pltpu.VMEM((layers, count, depth, width), BF16),
                pltpu.VMEM((total, width), BF16),
                pltpu.VMEM((ranks, tile, width), F32),
                pltpu.VMEM((ranks, tile, width), F32),
                pltpu.VMEM((layers, total, width), BF16),
                pltpu.VMEM((ranks, sources, BLOCK, width), BF16),
                pltpu.VMEM((count, depth, width), BF16),
                pltpu.SemaphoreType.DMA((ranks,)),
                pltpu.SemaphoreType.DMA((layers, len(owners))),
                pltpu.SemaphoreType.DMA((ranks,)),
            ],
        ),
        out_shape=[pltpu.HBM(rows.shape, BF16)] + [pltpu.VMEM(part, BF16)] * 2,
        compiler_params=pltpu.CompilerParams(vmem_limit_bytes=(20 + 28 * tile // 1024) * MB),
        cost_estimate=pl.CostEstimate(
            flops=24 * total * width * width,
            bytes_accessed=5 * total * width * 2 + width * width * 4,
            transcendentals=total * width,
        ),
        name=name,
    )(jnp.stack([bit] + owners), rows, *arrays, *tokens)


def place_kernel(half, info_ref, own_ref, mirror_ref, out_ref):
    dataset, _, place = block_place(info_ref, pl.program_id(0))
    is_own = dataset // half == place // half
    out_ref[0] = jnp.where(is_own, own_ref[0, 0], mirror_ref[0, 0])


def place_rows(info, own, mirror, row_blocks):
    half, _, _, width = own.shape
    shape = (1, 1, BLOCK, width)

    def index(of_own, block, info_ref):
        dataset, rank, place = block_place(info_ref, block)
        wanted = (dataset // half == place // half) == of_own
        return jnp.where(wanted, lax.rem(dataset, half), 0), jnp.where(wanted, rank, 0), 0, 0

    return pl.pallas_call(
        functools.partial(place_kernel, half),
        grid_spec=pltpu.PrefetchScalarGridSpec(
            num_scalar_prefetch=1,
            grid=(row_blocks,),
            in_specs=[
                pl.BlockSpec(shape, functools.partial(index, True)),
                pl.BlockSpec(shape, functools.partial(index, False)),
            ],
            out_specs=pl.BlockSpec((1, BLOCK, width), lambda block, *_: (block, 0, 0)),
        ),
        out_shape=jax.ShapeDtypeStruct((row_blocks, BLOCK, width), BF16),
        compiler_params=pltpu.CompilerParams(vmem_limit_bytes=16 * MB),
        name="place_rows",
    )(info, own, mirror)


def halo(cut_rows):
    count = lax.axis_size("dom")
    forward = [(i, i + 1) for i in range(count - 1)]
    backward = [(target, source) for source, target in forward]
    low = lax.ppermute(cut_rows, "dom", forward)
    high = lax.ppermute(cut_rows, "dom", backward)
    return low, high


def exchange(blocks, half):
    groups = [list(range(half)), list(range(half, 2 * half))]
    return lax.all_to_all(
        blocks, "head", split_axis=0, concat_axis=0, axis_index_groups=groups, tiled=True
    )


def across(array, half):
    return lax.ppermute(array, "head", [(i, (i + half) % (2 * half)) for i in range(2 * half)])


def after(array, *tokens):
    return pl.pallas_call(
        lambda *refs: None,
        in_specs=[ANY] * (1 + len(tokens)),
        out_specs=ANY,
        out_shape=pltpu.HBM(array.shape, array.dtype),
        input_output_aliases={0: 0},
        compiler_params=pltpu.CompilerParams(vmem_limit_bytes=48 * MB),
        name="after",
    )(hbm(array), *tokens)


def swap(array, bit):
    count = lax.axis_size("dom")
    return lax.ppermute(array, "dom", [(i, i ^ (1 << bit)) for i in range(count)])


def spread_over_dom(shard, offset):
    pieces = [shard]
    owners = [lax.axis_index("dom").astype(jnp.int32)]
    for bit in reversed(range(lax.axis_size("dom").bit_length() - 1)):
        pieces += [swap(piece, bit) for piece in pieces]
        owners += [owner ^ (1 << bit) for owner in owners]
    return [(piece[None], offset, [owner]) for piece, owner in zip(pieces, owners)]


def merge_kernel(first, tokens, bit_ref, keep_ref, got_ref, *refs):
    send_ref, kept_ref = refs[tokens:]
    bit = bit_ref[0]
    for layer in range(send_ref.shape[0]):
        for j in range(kept_ref.shape[1]):
            for out_ref, at in ((kept_ref, 2 * j + bit), (send_ref, 2 * j + 1 - bit)):
                keep = keep_ref[first + layer, at].astype(F32)
                out_ref[layer, j] = (keep + got_ref[first + layer, at].astype(F32)).astype(BF16)


def merge(keep, got, bit, first, layers, tokens):
    _, count, depth, width = keep.shape
    mine = (lax.axis_index("dom").astype(jnp.int32) >> bit) & 1
    shape = (layers, count // 2, depth, width)
    return pl.pallas_call(
        functools.partial(merge_kernel, first, len(tokens)),
        grid_spec=pltpu.PrefetchScalarGridSpec(
            num_scalar_prefetch=1,
            grid=(1,),
            in_specs=[IN_VMEM, IN_VMEM] + [ANY] * len(tokens),
            out_specs=[IN_VMEM] * 2,
        ),
        out_shape=[pltpu.VMEM(shape, BF16)] * 2,
        compiler_params=pltpu.CompilerParams(vmem_limit_bytes=16 * MB),
        name="merge_shares",
    )(mine.reshape(1), keep, got, *tokens)


def merge_whole_kernel(keep_ref, got_ref, out_ref):
    for layer in range(keep_ref.shape[0]):
        for j in range(keep_ref.shape[1]):
            keep = keep_ref[layer, j].astype(F32)
            out_ref[j, layer] = (keep + got_ref[layer, j].astype(F32)).astype(BF16)


def merge_whole(keep, got):
    layers, count, depth, width = keep.shape
    shape = (count, layers, depth, width)
    return pl.pallas_call(
        merge_whole_kernel,
        in_specs=[IN_VMEM, IN_VMEM],
        out_specs=resident(shape),
        grid=(1,),
        out_shape=pltpu.HBM(shape, BF16),
        compiler_params=pltpu.CompilerParams(vmem_limit_bytes=20 * MB),
        name="merge_whole",
    )(keep, got)


def sum_over_dom(keep, got, first, layers, *tokens):
    bits = lax.axis_size("dom").bit_length() - 1
    for bit in range(1, bits):
        send, keep = merge(keep, got, bit, first, layers, tokens)
        got = swap(send, bit)
        first = 0
    return keep[:, 0], got[:, 0], send


def add_kernel(keep_ref, got_ref, *refs):
    refs[-1][...] = (keep_ref[...].astype(F32) + got_ref[...].astype(F32)).astype(BF16)


def add(keep, got, *tokens):
    return pl.pallas_call(
        add_kernel,
        in_specs=[IN_VMEM, IN_VMEM] + [ANY] * len(tokens),
        out_specs=IN_VMEM,
        out_shape=pltpu.VMEM(keep.shape, BF16),
        compiler_params=pltpu.CompilerParams(vmem_limit_bytes=16 * MB),
        name="add_shares",
    )(keep, got, *tokens)


def total_kernel(sum_ref, far_ref, *refs):
    refs[-1][0] = sum_ref[0].astype(F32) + far_ref[0].astype(F32)


def total(own, far, layer, out=None, *tokens):
    _, depth, width = own.shape
    mine = pl.BlockSpec((1, depth, width), lambda t: (layer, 0, 0))
    came = pl.BlockSpec((1, depth, width), lambda t: (0, 0, 0))
    tokens = list(map(hbm, tokens if out is None else (out,) + tokens))
    return pl.pallas_call(
        total_kernel,
        grid=(1,),
        in_specs=[mine, came] + [ANY] * len(tokens),
        out_specs=mine,
        out_shape=pltpu.HBM(own.shape, F32),
        input_output_aliases={} if out is None else {2: 0},
        compiler_params=pltpu.CompilerParams(vmem_limit_bytes=16 * MB),
        name="total_share",
    )(own, far, *tokens)


def body(atoms, bonds, triplets, halo_ids, counts, enc_weight, gate_gain, head_weight):
    atom_rows = atoms[0]
    row_count, width = atom_rows.shape
    row_blocks = row_count // BLOCK
    half = lax.axis_size("head") // 2

    count = lax.axis_size("dom")

    gathered = lax.all_gather(head_weight[0], "dom", axis=0, tiled=False)
    own_parts = [(hbm(gathered), 0, [jnp.int32(i) for i in range(count)])]
    picked, *pieces = pick_rows(atom_rows, halo_ids, head_weight)
    far = across(pieces[0], half)
    low, high = halo(picked)
    extended = row_count + 2 * low.shape[0]
    codes = ((triplets[0] // LANES) * extended + bonds[0]).reshape(-1)
    pairs = (bonds[0] * LANES + triplets[0] % LANES).T
    place = lax.axis_index("head").astype(jnp.int32).reshape(1, 1)
    info = jnp.concatenate([counts, place], axis=1)
    own_blocks, mirror_blocks = encode(
        info, codes, atom_rows, low, high, enc_weight, gate_gain[None, :], pairs, half
    )
    near = after(far, hbm(own_blocks))
    mirror_rows = exchange(after(mirror_blocks, hbm(near), hbm(gathered)), half)
    rest = across(after(pieces[1], hbm(own_blocks)), half)
    cut = near.shape[1]
    mirror_parts = spread_over_dom(near, 0) + spread_over_dom(rest, cut)
    own_rows = exchange(after(own_blocks, mirror_rows), half)

    scale = 1.0 / math.sqrt(count * row_count)
    back, send, keep = run_head(mirror_rows, mirror_parts, scale, "head_mirror")
    got = swap(send, 0)
    high_keep, high_got, high_sent = sum_over_dom(keep, got, 1, 1)
    low_keep, low_got, low_sent = sum_over_dom(keep, got, 0, 1, high_sent)
    mirror_back = exchange(after(back, low_sent), half)

    back, send, keep = run_head(own_rows, own_parts, scale, "head_own", low_sent)
    own_back = exchange(back, half)
    high_sum = add(high_keep, high_got, send)
    low_sum = add(low_keep, low_got, send)
    high_part = across(high_sum, half)
    low_part = across(low_sum, half)
    own_sum = merge_whole(keep, swap(send, 0))
    same_core = [[i for i in range(count) if i % 2 == core] for core in range(2)]
    own_sum = lax.psum_scatter(
        own_sum, "dom", scatter_dimension=0, axis_index_groups=same_core, tiled=False
    )
    row_part = place_rows(info, own_back, mirror_back, row_blocks)
    head_part = total(own_sum, high_part, 1, None, row_part)
    head_part = total(own_sum, low_part, 0, head_part)
    return row_part.reshape(1, row_count, width), head_part[None]


def solution(mesh):
    return jax.shard_map(
        body,
        mesh=mesh,
        in_specs=(
            P("dom", "head", None),
            P("dom", None, "head"),
            P("dom", None, "head"),
            P("dom", "head"),
            P("dom", "head"),
            P(),
            P(),
            P("head", None, "dom", None),
        ),
        out_specs=(P("dom", "head", None), P("head", None, "dom", None)),
        check_vma=False,
    )
```

```python
import functools
import math

import jax
import jax.numpy as jnp
from jax import lax
from jax.experimental import pallas as pl
from jax.experimental.pallas import tpu as pltpu
from jax.sharding import PartitionSpec as P

BLOCK = 128
LANES = 128
MB = 1 << 20
VMEM = 58 * MB
F32 = jnp.float32
BF16 = jnp.bfloat16
ANY = pl.BlockSpec(memory_space=pl.ANY)
IN_VMEM = pl.BlockSpec(memory_space=pltpu.VMEM)


def sigmoid(x):
    return 0.5 + 0.5 * jnp.tanh(0.5 * x)


def hbm(array):
    return pltpu.with_memory_space_constraint(array, pltpu.HBM)


def resident(shape):
    return pl.BlockSpec(shape, lambda *_: (0,) * len(shape))


def pick_kernel(ids_ref, rows_ref, shard_ref, out_ref, first_ref, last_ref, held, sems):
    cut = first_ref.shape[1]
    load = pltpu.make_async_copy(shard_ref.at[0], held, sems.at[0])
    stores = [
        pltpu.make_async_copy(held.at[:, pl.ds(at, ref.shape[1])], ref, sems.at[i])
        for i, ref, at in ((1, first_ref, 0), (2, last_ref, cut))
    ]
    load.start()
    count, total = out_ref.shape[0], rows_ref.shape[0]
    places = lax.broadcasted_iota(jnp.int32, (total, count), 0)
    ones = jnp.where(places == ids_ref[...], 1.0, 0.0).astype(BF16)
    out_ref[...] = lax.dot_general(
        ones, rows_ref[...], (((0,), (0,)), ((), ())), preferred_element_type=F32
    ).astype(BF16)
    load.wait()
    for store in stores:
        store.start()
    for store in stores:
        store.wait()


def pick_rows(rows, ids, shard):
    _, layers, depth, width = shard.shape
    cut = depth * 3 // 4
    return pl.pallas_call(
        pick_kernel,
        in_specs=[IN_VMEM, IN_VMEM, ANY],
        out_specs=[IN_VMEM, ANY, ANY],
        out_shape=[
            jax.ShapeDtypeStruct((ids.shape[1], rows.shape[1]), rows.dtype),
            pltpu.HBM((layers, cut, width), shard.dtype),
            pltpu.HBM((layers, depth - cut, width), shard.dtype),
        ],
        scratch_shapes=[pltpu.VMEM(shard.shape[1:], shard.dtype), pltpu.SemaphoreType.DMA((3,))],
        compiler_params=pltpu.CompilerParams(vmem_limit_bytes=16 * MB),
        name="pick_rows",
    )(ids, rows, hbm(shard))


def block_place(info_ref, block):
    sets = info_ref.shape[1] - 1
    start, dataset, rank = jnp.int32(0), jnp.int32(0), jnp.int32(0)
    for candidate in range(sets):
        blocks = info_ref[0, candidate] // BLOCK
        inside = jnp.logical_and(block >= start, block < start + blocks)
        dataset = jnp.where(inside, candidate, dataset)
        rank = jnp.where(inside, block - start, rank)
        start = start + blocks
    return dataset, rank, info_ref[0, sets]


def encode_kernel(
    half, batch, info_ref, codes_ref, atoms_ref, low_ref, high_ref, weight_ref, gain_ref,
    pairs_ref, own_ref, mirror_ref, gained, scores, partial, wanted, gates, gate_rows, staged,
    zeros, weight, sems, weight_sem,
):
    rows, width = atoms_ref.shape
    depth = low_ref.shape[0]
    bond_count = pairs_ref.shape[1]
    sets = 2 * half
    weight_in = pltpu.make_async_copy(weight_ref, weight, weight_sem)
    weight_in.start()
    home = info_ref[0, sets] // half * half
    tile = batch * BLOCK

    def leave(source, slot, act):
        def one(ref, at):
            act(pltpu.make_async_copy(source, ref.at[at], sems.at[slot]))

        pl.when(slot < sets)(lambda: one(own_ref, slot))
        pl.when(slot >= sets)(lambda: one(mirror_ref, slot - sets))

    zeros[...] = jnp.zeros_like(zeros)

    def blank(slot, carry):
        dataset = lax.rem(home + slot // 2, sets)
        empty = info_ref[0, dataset] // BLOCK <= lax.rem(slot, 2)
        pl.when(empty)(lambda: leave(zeros, slot, lambda copy: copy.start()))
        return carry

    lax.fori_loop(0, 2 * sets, blank, 0)

    extended = rows + 2 * depth
    parts = ((atoms_ref, 0), (low_ref, rows), (high_ref, rows + depth))
    for ref, at in parts:
        gained[at : at + ref.shape[0], :] = (ref[...].astype(F32) * gain_ref[...]).astype(BF16)
    for ref, base in parts:
        step = min(ref.shape[0], 2 * LANES)
        for at in range(0, ref.shape[0], step):
            value = lax.dot_general(
                gained[...], ref[at : at + step, :], (((1,), (1,)), ((), ())),
                preferred_element_type=F32,
            )
            for k in range(0, step, LANES):
                piece = (base + at + k) // LANES
                scores[piece * extended : (piece + 1) * extended, :] = value[:, k : k + LANES]

    def encode_tile(step, carry):
        base = pl.multiple_of(step * tile, tile)

        eight = lax.broadcasted_iota(jnp.int32, (8, LANES), 0)

        def score(group, carry):
            for bond in range(bond_count):
                at = bond * rows + base + group * 8
                place = pl.multiple_of(bond * tile + group * 8, 8)
                found = scores[pl.ds(codes_ref[at], 8, stride=0), :]
                for j in range(1, 8):
                    row = scores[pl.ds(codes_ref[at + j], 8, stride=0), :]
                    found = jnp.where(eight == j, row, found)
                partial[pl.ds(place, 8), :] = found
            return carry

        lax.fori_loop(0, tile // 8, score, 0)
        places = lax.broadcasted_iota(jnp.int32, (BLOCK, LANES), 1)
        for block in range(batch):
            pairs = pairs_ref[pl.ds(base + block * BLOCK, BLOCK), :]
            for bond in range(bond_count):
                at = bond * tile + block * BLOCK
                pair = jnp.broadcast_to(pairs[:, bond : bond + 1], (BLOCK, LANES))
                wanted[bond] = pair // LANES
                picked = places == pair % LANES
                logits = jnp.sum(
                    jnp.where(picked, partial[at : at + BLOCK, :], 0.0), axis=1, keepdims=True
                )
                gate = sigmoid(logits * (1.0 / math.sqrt(width)))
                gates[bond] = jnp.broadcast_to(gate, (BLOCK, LANES))
            for at in range(0, extended, LANES):
                acc = jnp.zeros((BLOCK, LANES), F32)
                for bond in range(bond_count):
                    acc = acc + jnp.where(wanted[bond] == places + at, gates[bond], 0.0)
                gate_rows[block * BLOCK : (block + 1) * BLOCK, at : at + LANES] = acc.astype(BF16)
        message = jnp.dot(gate_rows[:, :rows], atoms_ref[...], preferred_element_type=F32)
        for ref, at in ((low_ref, rows), (high_ref, rows + depth)):
            message += jnp.dot(
                gate_rows[:, at : at + depth], ref[...], preferred_element_type=F32
            )
        pl.when(step == 0)(lambda: weight_in.wait())
        update = jnp.dot(message.astype(BF16), weight[...], preferred_element_type=F32)
        own = atoms_ref[pl.ds(base, tile), :].astype(F32)
        staged[step] = (own + update * sigmoid(update)).astype(BF16).reshape(staged.shape[1:])
        for block in range(batch):
            dataset, rank, _ = block_place(info_ref, step * batch + block)
            slot = lax.rem(dataset - home + sets, sets) * 2 + rank
            leave(staged.at[step, block], slot, lambda copy: copy.start())
        return carry

    lax.fori_loop(0, rows // tile, encode_tile, 0)

    def settle(slot, carry):
        leave(zeros, slot, lambda copy: copy.wait())
        return carry

    lax.fori_loop(0, 2 * sets, settle, 0)


def encode(info, codes, atoms, low, high, weight, gain, pairs, half):
    rows, width = atoms.shape
    extended = rows + 2 * low.shape[0]
    bond_count = pairs.shape[1]
    slots = 4 * half
    row_blocks = rows // BLOCK
    batch = 4 if row_blocks % 4 == 0 else 1
    blocks = pl.pallas_call(
        functools.partial(encode_kernel, half, batch),
        grid_spec=pltpu.PrefetchScalarGridSpec(
            num_scalar_prefetch=2,
            grid=(1,),
            in_specs=[IN_VMEM] * 3 + [ANY] + [IN_VMEM] * 2,
            out_specs=[pl.BlockSpec(memory_space=pltpu.HBM)] * 2,
            scratch_shapes=[
                pltpu.VMEM((extended, width), BF16),
                pltpu.VMEM((extended // LANES * extended, LANES), F32),
                pltpu.VMEM((batch * BLOCK * bond_count, LANES), F32),
                pltpu.VMEM((bond_count, BLOCK, LANES), jnp.int32),
                pltpu.VMEM((bond_count, BLOCK, LANES), F32),
                pltpu.VMEM((batch * BLOCK, extended), BF16),
                pltpu.VMEM((row_blocks // batch, batch, BLOCK, width), BF16),
                pltpu.VMEM((BLOCK, width), BF16),
                pltpu.VMEM((width, width), BF16),
                pltpu.SemaphoreType.DMA((slots,)),
                pltpu.SemaphoreType.DMA(()),
            ],
        ),
        out_shape=[pltpu.HBM((2 * half, BLOCK, width), BF16)] * 2,
        compiler_params=pltpu.CompilerParams(vmem_limit_bytes=44 * MB),
        cost_estimate=pl.CostEstimate(
            flops=40 * rows * width * width,
            bytes_accessed=30 * MB,
            transcendentals=rows * width,
        ),
        name="encode_rows",
    )(info, codes, atoms, low, high, hbm(weight), gain, pairs)
    return [rows.reshape(half, 2, BLOCK, width) for rows in blocks]


def head_kernel(scale, offsets, tokens, table_ref, rows_ref, *refs):
    part_count = len(offsets)
    weight_refs = refs[:part_count]
    (
        back_ref, send_ref, keep_ref, x, weights, act, slope, err, grad, back, shares,
        in_sems, weight_sems, back_sems,
    ) = refs[part_count + tokens :]
    width = x.shape[-1]
    tile = x.shape[1] * x.shape[2]
    count = weights.shape[1]
    chunk = width // 4
    chunks = [slice(at, at + chunk) for at in range(0, width, chunk)]
    transposed = (((1,), (1,)), ((), ()))
    over_rows = (((0,), (0,)), ((), ()))
    bit = table_ref[0]

    def rows_in(rank):
        return pltpu.make_async_copy(rows_ref.at[:, rank], x.at[rank], in_sems.at[rank])

    def weights_in(layer):
        copies = []
        for ref, at in zip(weight_refs, offsets):
            for i in range(ref.shape[0]):
                owner = table_ref[1 + len(copies)]
                place = weights.at[layer, owner, pl.ds(at, ref.shape[2])]
                sem = weight_sems.at[layer, len(copies)]
                copies.append(pltpu.make_async_copy(ref.at[i, layer], place, sem))
        return copies

    def back_out(rank):
        return pltpu.make_async_copy(back.at[rank], back_ref.at[:, rank], back_sems.at[rank])

    def matrix(layer):
        return weights[layer].reshape(width, width)

    def forward(rank, wait):
        inputs = x[rank].reshape(tile, width)
        low = matrix(0)
        for at in chunks:
            z = jnp.dot(inputs, low[:, at], preferred_element_type=F32)
            s = sigmoid(z)
            act[rank * tile : (rank + 1) * tile, at] = (z * s).astype(BF16)
            slope[rank, :, at] = s * (1.0 + z * (1.0 - s))
        if wait:
            for copy in weights_in(1):
                copy.wait()
        acts = act[rank * tile : (rank + 1) * tile, :]
        high = matrix(1)
        for at in chunks:
            value = jnp.dot(acts, high[:, at], preferred_element_type=F32)
            value = value - inputs[:, at].astype(F32)
            err[rank, :, at] = value
            grad[1, rank * tile : (rank + 1) * tile, at] = value.astype(BF16)

    def backward(rank):
        rows = slice(rank * tile, (rank + 1) * tile)
        grads = grad[1, rows, :]
        high = matrix(1)
        for at in chunks:
            up = lax.dot_general(grads, high[at, :], transposed, preferred_element_type=F32)
            grad[0, rows, at] = (up * slope[rank, :, at]).astype(BF16)
        grads = grad[0, rows, :]
        low = matrix(0)
        shape = x.shape[1:3] + (chunk,)
        for at in chunks:
            up = lax.dot_general(grads, low[at, :], transposed, preferred_element_type=F32)
            back[rank, :, :, at] = (up - err[rank, :, at]).astype(BF16).reshape(shape)

    def share(layer, acts, rows):
        value = lax.dot_general(
            acts, grad[layer, :rows, :], over_rows, preferred_element_type=F32
        )
        shares[...] = (value * scale).astype(BF16).reshape(shares.shape)
        for j in range(count // 2):
            keep_ref[layer, j] = shares[2 * j + bit]
            send_ref[layer, j] = shares[2 * j + 1 - bit]

    for rank in range(2):
        rows_in(rank).start()
    for layer in range(2):
        for copy in weights_in(layer):
            copy.start()
    rows_in(0).wait()
    for copy in weights_in(0):
        copy.wait()
    forward(0, True)
    rows_in(1).wait()
    some = jnp.max(jnp.abs(x[1].reshape(tile, width).astype(F32))) > 0
    none = jnp.logical_not(some)
    pl.when(some)(lambda: forward(1, False))
    pl.when(some)(lambda: share(1, act[...], 2 * tile))
    pl.when(none)(lambda: share(1, act[:tile, :], tile))
    backward(0)
    back_out(0).start()
    pl.when(some)(lambda: backward(1))

    @pl.when(none)
    def _():
        back[1] = jnp.zeros(back.shape[1:], BF16)

    back_out(1).start()
    pl.when(some)(lambda: share(0, x[...].reshape(2 * tile, width), 2 * tile))
    pl.when(none)(lambda: share(0, x[0].reshape(tile, width), tile))
    for rank in range(2):
        back_out(rank).wait()


def run_head(rows, parts, scale, name, *tokens):
    sources, ranks, _, width = rows.shape
    count = lax.axis_size("dom")
    arrays, offsets, owners = zip(*parts)
    owners = [owner for group in owners for owner in group]
    depth = width // count
    layers = 2
    tile = sources * BLOCK
    total = ranks * tile
    part = (layers, count // 2, depth, width)
    bit = lax.axis_index("dom").astype(jnp.int32) & 1
    return pl.pallas_call(
        functools.partial(head_kernel, scale, offsets, len(tokens)),
        grid_spec=pltpu.PrefetchScalarGridSpec(
            num_scalar_prefetch=1,
            grid=(1,),
            in_specs=[ANY] * (1 + len(parts) + len(tokens)),
            out_specs=[ANY, IN_VMEM, IN_VMEM],
            scratch_shapes=[
                pltpu.VMEM((ranks, sources, BLOCK, width), BF16),
                pltpu.VMEM((layers, count, depth, width), BF16),
                pltpu.VMEM((total, width), BF16),
                pltpu.VMEM((ranks, tile, width), F32),
                pltpu.VMEM((ranks, tile, width), F32),
                pltpu.VMEM((layers, total, width), BF16),
                pltpu.VMEM((ranks, sources, BLOCK, width), BF16),
                pltpu.VMEM((count, depth, width), BF16),
                pltpu.SemaphoreType.DMA((ranks,)),
                pltpu.SemaphoreType.DMA((layers, len(owners))),
                pltpu.SemaphoreType.DMA((ranks,)),
            ],
        ),
        out_shape=[pltpu.HBM(rows.shape, BF16)] + [pltpu.VMEM(part, BF16)] * 2,
        compiler_params=pltpu.CompilerParams(vmem_limit_bytes=(20 + 28 * tile // 1024) * MB),
        cost_estimate=pl.CostEstimate(
            flops=24 * total * width * width,
            bytes_accessed=5 * total * width * 2 + width * width * 4,
            transcendentals=total * width,
        ),
        name=name,
    )(jnp.stack([bit] + owners), rows, *arrays, *tokens)


def place_kernel(half, info_ref, own_ref, mirror_ref, out_ref):
    dataset, _, place = block_place(info_ref, pl.program_id(0))
    is_own = dataset // half == place // half
    out_ref[0] = jnp.where(is_own, own_ref[0, 0], mirror_ref[0, 0])


def place_rows(info, own, mirror, row_blocks):
    half, _, _, width = own.shape
    shape = (1, 1, BLOCK, width)

    def index(of_own, block, info_ref):
        dataset, rank, place = block_place(info_ref, block)
        wanted = (dataset // half == place // half) == of_own
        return jnp.where(wanted, lax.rem(dataset, half), 0), jnp.where(wanted, rank, 0), 0, 0

    return pl.pallas_call(
        functools.partial(place_kernel, half),
        grid_spec=pltpu.PrefetchScalarGridSpec(
            num_scalar_prefetch=1,
            grid=(row_blocks,),
            in_specs=[
                pl.BlockSpec(shape, functools.partial(index, True)),
                pl.BlockSpec(shape, functools.partial(index, False)),
            ],
            out_specs=pl.BlockSpec((1, BLOCK, width), lambda block, *_: (block, 0, 0)),
        ),
        out_shape=jax.ShapeDtypeStruct((row_blocks, BLOCK, width), BF16),
        compiler_params=pltpu.CompilerParams(vmem_limit_bytes=16 * MB),
        name="place_rows",
    )(info, own, mirror)


def halo(cut_rows):
    count = lax.axis_size("dom")
    forward = [(i, i + 1) for i in range(count - 1)]
    backward = [(target, source) for source, target in forward]
    low = lax.ppermute(cut_rows, "dom", forward)
    high = lax.ppermute(cut_rows, "dom", backward)
    return low, high


def exchange(blocks, half):
    groups = [list(range(half)), list(range(half, 2 * half))]
    return lax.all_to_all(
        blocks, "head", split_axis=0, concat_axis=0, axis_index_groups=groups, tiled=True
    )


def across(array, half):
    return lax.ppermute(array, "head", [(i, (i + half) % (2 * half)) for i in range(2 * half)])


def after(array, *tokens):
    return pl.pallas_call(
        lambda *refs: None,
        in_specs=[ANY] * (1 + len(tokens)),
        out_specs=ANY,
        out_shape=pltpu.HBM(array.shape, array.dtype),
        input_output_aliases={0: 0},
        compiler_params=pltpu.CompilerParams(vmem_limit_bytes=48 * MB),
        name="after",
    )(hbm(array), *tokens)


def swap(array, bit):
    count = lax.axis_size("dom")
    return lax.ppermute(array, "dom", [(i, i ^ (1 << bit)) for i in range(count)])


def spread_over_dom(shard, offset):
    pieces = [shard]
    owners = [lax.axis_index("dom").astype(jnp.int32)]
    for bit in reversed(range(lax.axis_size("dom").bit_length() - 1)):
        pieces += [swap(piece, bit) for piece in pieces]
        owners += [owner ^ (1 << bit) for owner in owners]
    return [(piece[None], offset, [owner]) for piece, owner in zip(pieces, owners)]


def merge_kernel(first, tokens, bit_ref, keep_ref, got_ref, *refs):
    send_ref, kept_ref = refs[tokens:]
    bit = bit_ref[0]
    for layer in range(send_ref.shape[0]):
        for j in range(kept_ref.shape[1]):
            for out_ref, at in ((kept_ref, 2 * j + bit), (send_ref, 2 * j + 1 - bit)):
                keep = keep_ref[first + layer, at].astype(F32)
                out_ref[layer, j] = (keep + got_ref[first + layer, at].astype(F32)).astype(BF16)


def merge(keep, got, bit, first, layers, tokens):
    _, count, depth, width = keep.shape
    mine = (lax.axis_index("dom").astype(jnp.int32) >> bit) & 1
    shape = (layers, count // 2, depth, width)
    return pl.pallas_call(
        functools.partial(merge_kernel, first, len(tokens)),
        grid_spec=pltpu.PrefetchScalarGridSpec(
            num_scalar_prefetch=1,
            grid=(1,),
            in_specs=[IN_VMEM, IN_VMEM] + [ANY] * len(tokens),
            out_specs=[IN_VMEM] * 2,
        ),
        out_shape=[pltpu.VMEM(shape, BF16)] * 2,
        compiler_params=pltpu.CompilerParams(vmem_limit_bytes=16 * MB),
        name="merge_shares",
    )(mine.reshape(1), keep, got, *tokens)


def sum_over_dom(keep, got, first, layers, *tokens):
    bits = lax.axis_size("dom").bit_length() - 1
    for bit in range(1, bits):
        send, keep = merge(keep, got, bit, first, layers, tokens)
        got = swap(send, bit)
        first = 0
    return keep[:, 0], got[:, 0], send


def add_kernel(keep_ref, got_ref, *refs):
    refs[-1][...] = (keep_ref[...].astype(F32) + got_ref[...].astype(F32)).astype(BF16)


def add(keep, got, *tokens):
    return pl.pallas_call(
        add_kernel,
        in_specs=[IN_VMEM, IN_VMEM] + [ANY] * len(tokens),
        out_specs=IN_VMEM,
        out_shape=pltpu.VMEM(keep.shape, BF16),
        compiler_params=pltpu.CompilerParams(vmem_limit_bytes=16 * MB),
        name="add_shares",
    )(keep, got, *tokens)


def total_kernel(keep_ref, got_ref, far_ref, *refs):
    total = keep_ref[0].astype(F32) + got_ref[0].astype(F32) + far_ref[0].astype(F32)
    refs[-1][0] = total


def total(keep, got, far, layer, out=None, *tokens):
    _, depth, width = keep.shape
    mine = pl.BlockSpec((1, depth, width), lambda t: (layer, 0, 0))
    came = pl.BlockSpec((1, depth, width), lambda t: (0, 0, 0))
    tokens = list(map(hbm, tokens if out is None else (out,) + tokens))
    return pl.pallas_call(
        total_kernel,
        grid=(1,),
        in_specs=[mine, mine, came] + [ANY] * len(tokens),
        out_specs=mine,
        out_shape=pltpu.HBM(keep.shape, F32),
        input_output_aliases={} if out is None else {3: 0},
        compiler_params=pltpu.CompilerParams(vmem_limit_bytes=16 * MB),
        name="total_share",
    )(keep, got, far, *tokens)


def body(atoms, bonds, triplets, halo_ids, counts, enc_weight, gate_gain, head_weight):
    atom_rows = atoms[0]
    row_count, width = atom_rows.shape
    row_blocks = row_count // BLOCK
    half = lax.axis_size("head") // 2

    count = lax.axis_size("dom")

    gathered = lax.all_gather(head_weight[0], "dom", axis=0, tiled=False)
    own_parts = [(hbm(gathered), 0, [jnp.int32(i) for i in range(count)])]
    picked, *pieces = pick_rows(atom_rows, halo_ids, head_weight)
    far = across(pieces[0], half)
    low, high = halo(picked)
    extended = row_count + 2 * low.shape[0]
    codes = ((triplets[0] // LANES) * extended + bonds[0]).reshape(-1)
    pairs = (bonds[0] * LANES + triplets[0] % LANES).T
    place = lax.axis_index("head").astype(jnp.int32).reshape(1, 1)
    info = jnp.concatenate([counts, place], axis=1)
    own_blocks, mirror_blocks = encode(
        info, codes, atom_rows, low, high, enc_weight, gate_gain[None, :], pairs, half
    )
    near = after(far, hbm(own_blocks))
    mirror_rows = exchange(after(mirror_blocks, hbm(near), hbm(gathered)), half)
    rest = across(after(pieces[1], hbm(own_blocks)), half)
    cut = near.shape[1]
    mirror_parts = spread_over_dom(near, 0) + spread_over_dom(rest, cut)
    own_rows = exchange(after(own_blocks, mirror_rows), half)

    scale = 1.0 / math.sqrt(count * row_count)
    back, send, keep = run_head(mirror_rows, mirror_parts, scale, "head_mirror")
    got = swap(send, 0)
    high_keep, high_got, high_sent = sum_over_dom(keep, got, 1, 1)
    low_keep, low_got, low_sent = sum_over_dom(keep, got, 0, 1, high_sent)
    mirror_back = exchange(after(back, low_sent), half)

    high_sum = add(high_keep, high_got)
    high_part = across(high_sum, half)
    back, send, keep = run_head(own_rows, own_parts, scale, "head_own", high_sum)
    own_back = exchange(after(back, high_part, low_got), half)
    low_part = across(add(low_keep, low_got, send), half)
    own_keep, own_got, _ = sum_over_dom(keep, swap(send, 0), 0, 2)
    row_part = place_rows(info, own_back, mirror_back, row_blocks)
    head_part = total(own_keep, own_got, high_part, 1, None, row_part)
    head_part = total(own_keep, own_got, low_part, 0, head_part)
    return row_part.reshape(1, row_count, width), head_part[None]


def solution(mesh):
    return jax.shard_map(
        body,
        mesh=mesh,
        in_specs=(
            P("dom", "head", None),
            P("dom", None, "head"),
            P("dom", None, "head"),
            P("dom", "head"),
            P("dom", "head"),
            P(),
            P(),
            P("head", None, "dom", None),
        ),
        out_specs=(P("dom", "head", None), P("head", None, "dom", None)),
        check_vma=False,
    )
```

```python
import functools
import math

import jax
import jax.numpy as jnp
from jax import lax
from jax.experimental import pallas as pl
from jax.experimental.pallas import tpu as pltpu
from jax.sharding import PartitionSpec as P

BLOCK = 128
LANES = 128
MB = 1 << 20
VMEM = 58 * MB
F32 = jnp.float32
BF16 = jnp.bfloat16
ANY = pl.BlockSpec(memory_space=pl.ANY)
IN_VMEM = pl.BlockSpec(memory_space=pltpu.VMEM)


def sigmoid(x):
    return 0.5 + 0.5 * jnp.tanh(0.5 * x)


def hbm(array):
    return pltpu.with_memory_space_constraint(array, pltpu.HBM)


def resident(shape):
    return pl.BlockSpec(shape, lambda *_: (0,) * len(shape))


def pick_kernel(ids_ref, rows_ref, out_ref):
    count, total = out_ref.shape[0], rows_ref.shape[0]
    places = lax.broadcasted_iota(jnp.int32, (total, count), 0)
    ones = jnp.where(places == ids_ref[...], 1.0, 0.0).astype(BF16)
    out_ref[...] = lax.dot_general(
        ones, rows_ref[...], (((0,), (0,)), ((), ())), preferred_element_type=F32
    ).astype(BF16)


def pick_rows(rows, ids):
    return pl.pallas_call(
        pick_kernel,
        in_specs=[IN_VMEM, IN_VMEM],
        out_specs=IN_VMEM,
        out_shape=jax.ShapeDtypeStruct((ids.shape[1], rows.shape[1]), rows.dtype),
        compiler_params=pltpu.CompilerParams(vmem_limit_bytes=16 * MB),
        name="pick_rows",
    )(ids, rows)


def block_place(info_ref, block):
    sets = info_ref.shape[1] - 1
    start, dataset, rank = jnp.int32(0), jnp.int32(0), jnp.int32(0)
    for candidate in range(sets):
        blocks = info_ref[0, candidate] // BLOCK
        inside = jnp.logical_and(block >= start, block < start + blocks)
        dataset = jnp.where(inside, candidate, dataset)
        rank = jnp.where(inside, block - start, rank)
        start = start + blocks
    return dataset, rank, info_ref[0, sets]


def encode_kernel(
    half, batch, info_ref, codes_ref, atoms_ref, low_ref, high_ref, weight_ref, gain_ref,
    pairs_ref, own_ref, mirror_ref, gained, scores, partial, wanted, gates, gate_rows, staged,
    zeros, weight, sems, weight_sem,
):
    rows, width = atoms_ref.shape
    depth = low_ref.shape[0]
    bond_count = pairs_ref.shape[1]
    sets = 2 * half
    weight_in = pltpu.make_async_copy(weight_ref, weight, weight_sem)
    weight_in.start()
    home = info_ref[0, sets] // half * half
    tile = batch * BLOCK

    def leave(source, slot, act):
        def one(ref, at):
            act(pltpu.make_async_copy(source, ref.at[at], sems.at[slot]))

        pl.when(slot < sets)(lambda: one(own_ref, slot))
        pl.when(slot >= sets)(lambda: one(mirror_ref, slot - sets))

    zeros[...] = jnp.zeros_like(zeros)

    def blank(slot, carry):
        dataset = lax.rem(home + slot // 2, sets)
        empty = info_ref[0, dataset] // BLOCK <= lax.rem(slot, 2)
        pl.when(empty)(lambda: leave(zeros, slot, lambda copy: copy.start()))
        return carry

    lax.fori_loop(0, 2 * sets, blank, 0)

    extended = rows + 2 * depth
    parts = ((atoms_ref, 0), (low_ref, rows), (high_ref, rows + depth))
    for ref, at in parts:
        gained[at : at + ref.shape[0], :] = (ref[...].astype(F32) * gain_ref[...]).astype(BF16)
    for ref, base in parts:
        step = min(ref.shape[0], 2 * LANES)
        for at in range(0, ref.shape[0], step):
            value = lax.dot_general(
                gained[...], ref[at : at + step, :], (((1,), (1,)), ((), ())),
                preferred_element_type=F32,
            )
            for k in range(0, step, LANES):
                piece = (base + at + k) // LANES
                scores[piece * extended : (piece + 1) * extended, :] = value[:, k : k + LANES]

    def encode_tile(step, carry):
        base = pl.multiple_of(step * tile, tile)

        eight = lax.broadcasted_iota(jnp.int32, (8, LANES), 0)

        def score(group, carry):
            for bond in range(bond_count):
                at = bond * rows + base + group * 8
                place = pl.multiple_of(bond * tile + group * 8, 8)
                found = scores[pl.ds(codes_ref[at], 8, stride=0), :]
                for j in range(1, 8):
                    row = scores[pl.ds(codes_ref[at + j], 8, stride=0), :]
                    found = jnp.where(eight == j, row, found)
                partial[pl.ds(place, 8), :] = found
            return carry

        lax.fori_loop(0, tile // 8, score, 0, unroll=4)
        places = lax.broadcasted_iota(jnp.int32, (BLOCK, LANES), 1)
        for block in range(batch):
            pairs = pairs_ref[pl.ds(base + block * BLOCK, BLOCK), :]
            for bond in range(bond_count):
                at = bond * tile + block * BLOCK
                pair = jnp.broadcast_to(pairs[:, bond : bond + 1], (BLOCK, LANES))
                wanted[bond] = pair // LANES
                picked = places == pair % LANES
                logits = jnp.sum(
                    jnp.where(picked, partial[at : at + BLOCK, :], 0.0), axis=1, keepdims=True
                )
                gate = sigmoid(logits * (1.0 / math.sqrt(width)))
                gates[bond] = jnp.broadcast_to(gate, (BLOCK, LANES))
            for at in range(0, extended, LANES):
                acc = jnp.zeros((BLOCK, LANES), F32)
                for bond in range(bond_count):
                    acc = acc + jnp.where(wanted[bond] == places + at, gates[bond], 0.0)
                gate_rows[block * BLOCK : (block + 1) * BLOCK, at : at + LANES] = acc.astype(BF16)
        message = jnp.dot(gate_rows[:, :rows], atoms_ref[...], preferred_element_type=F32)
        for ref, at in ((low_ref, rows), (high_ref, rows + depth)):
            message += jnp.dot(
                gate_rows[:, at : at + depth], ref[...], preferred_element_type=F32
            )
        pl.when(step == 0)(lambda: weight_in.wait())
        update = jnp.dot(message.astype(BF16), weight[...], preferred_element_type=F32)
        own = atoms_ref[pl.ds(base, tile), :].astype(F32)
        staged[step] = (own + update * sigmoid(update)).astype(BF16).reshape(staged.shape[1:])
        for block in range(batch):
            dataset, rank, _ = block_place(info_ref, step * batch + block)
            slot = lax.rem(dataset - home + sets, sets) * 2 + rank
            leave(staged.at[step, block], slot, lambda copy: copy.start())
        return carry

    lax.fori_loop(0, rows // tile, encode_tile, 0)

    def settle(slot, carry):
        leave(zeros, slot, lambda copy: copy.wait())
        return carry

    lax.fori_loop(0, 2 * sets, settle, 0)


def encode(info, codes, atoms, low, high, weight, gain, pairs, half):
    rows, width = atoms.shape
    extended = rows + 2 * low.shape[0]
    bond_count = pairs.shape[1]
    slots = 4 * half
    row_blocks = rows // BLOCK
    batch = 4 if row_blocks % 4 == 0 else 1
    blocks = pl.pallas_call(
        functools.partial(encode_kernel, half, batch),
        grid_spec=pltpu.PrefetchScalarGridSpec(
            num_scalar_prefetch=2,
            grid=(1,),
            in_specs=[IN_VMEM] * 3 + [ANY] + [IN_VMEM] * 2,
            out_specs=[pl.BlockSpec(memory_space=pltpu.HBM)] * 2,
            scratch_shapes=[
                pltpu.VMEM((extended, width), BF16),
                pltpu.VMEM((extended // LANES * extended, LANES), F32),
                pltpu.VMEM((batch * BLOCK * bond_count, LANES), F32),
                pltpu.VMEM((bond_count, BLOCK, LANES), jnp.int32),
                pltpu.VMEM((bond_count, BLOCK, LANES), F32),
                pltpu.VMEM((batch * BLOCK, extended), BF16),
                pltpu.VMEM((row_blocks // batch, batch, BLOCK, width), BF16),
                pltpu.VMEM((BLOCK, width), BF16),
                pltpu.VMEM((width, width), BF16),
                pltpu.SemaphoreType.DMA((slots,)),
                pltpu.SemaphoreType.DMA(()),
            ],
        ),
        out_shape=[pltpu.HBM((2 * half, BLOCK, width), BF16)] * 2,
        compiler_params=pltpu.CompilerParams(vmem_limit_bytes=44 * MB),
        cost_estimate=pl.CostEstimate(
            flops=3 * rows * width * width,
            bytes_accessed=10 * MB,
            transcendentals=rows * width,
        ),
        name="encode_rows",
    )(info, codes, atoms, low, high, hbm(weight), gain, pairs)
    return [rows.reshape(half, 2, BLOCK, width) for rows in blocks]


def head_kernel(scale, offsets, tokens, table_ref, rows_ref, *refs):
    part_count = len(offsets)
    weight_refs = refs[:part_count]
    (
        back_ref, send_ref, keep_ref, x, weights, act, slope, err, grad, back, shares,
        in_sems, weight_sems, back_sems,
    ) = refs[part_count + tokens :]
    width = x.shape[-1]
    tile = x.shape[1] * x.shape[2]
    count = weights.shape[1]
    chunk = width // 4
    chunks = [slice(at, at + chunk) for at in range(0, width, chunk)]
    transposed = (((1,), (1,)), ((), ()))
    over_rows = (((0,), (0,)), ((), ()))
    bit = table_ref[0]

    def rows_in(rank):
        return pltpu.make_async_copy(rows_ref.at[:, rank], x.at[rank], in_sems.at[rank])

    def weights_in(layer):
        copies = []
        for ref, at in zip(weight_refs, offsets):
            for i in range(ref.shape[0]):
                owner = table_ref[1 + len(copies)]
                place = weights.at[layer, owner, pl.ds(at, ref.shape[2])]
                sem = weight_sems.at[layer, len(copies)]
                copies.append(pltpu.make_async_copy(ref.at[i, layer], place, sem))
        return copies

    def back_out(rank):
        return pltpu.make_async_copy(back.at[rank], back_ref.at[:, rank], back_sems.at[rank])

    def matrix(layer):
        return weights[layer].reshape(width, width)

    def forward(rank, wait):
        inputs = x[rank].reshape(tile, width)
        low = matrix(0)
        for at in chunks:
            z = jnp.dot(inputs, low[:, at], preferred_element_type=F32)
            s = sigmoid(z)
            act[rank * tile : (rank + 1) * tile, at] = (z * s).astype(BF16)
            slope[rank, :, at] = s * (1.0 + z * (1.0 - s))
        if wait:
            for copy in weights_in(1):
                copy.wait()
        acts = act[rank * tile : (rank + 1) * tile, :]
        high = matrix(1)
        for at in chunks:
            value = jnp.dot(acts, high[:, at], preferred_element_type=F32)
            value = value - inputs[:, at].astype(F32)
            err[rank, :, at] = value
            grad[1, rank * tile : (rank + 1) * tile, at] = value.astype(BF16)

    def backward(rank):
        rows = slice(rank * tile, (rank + 1) * tile)
        grads = grad[1, rows, :]
        high = matrix(1)
        for at in chunks:
            up = lax.dot_general(grads, high[at, :], transposed, preferred_element_type=F32)
            grad[0, rows, at] = (up * slope[rank, :, at]).astype(BF16)
        grads = grad[0, rows, :]
        low = matrix(0)
        shape = x.shape[1:3] + (chunk,)
        for at in chunks:
            up = lax.dot_general(grads, low[at, :], transposed, preferred_element_type=F32)
            back[rank, :, :, at] = (up - err[rank, :, at]).astype(BF16).reshape(shape)

    def share(layer, acts, rows):
        value = lax.dot_general(
            acts, grad[layer, :rows, :], over_rows, preferred_element_type=F32
        )
        shares[...] = (value * scale).astype(BF16).reshape(shares.shape)
        for j in range(count // 2):
            keep_ref[layer, j] = shares[2 * j + bit]
            send_ref[layer, j] = shares[2 * j + 1 - bit]

    for rank in range(2):
        rows_in(rank).start()
    for layer in range(2):
        for copy in weights_in(layer):
            copy.start()
    rows_in(0).wait()
    for copy in weights_in(0):
        copy.wait()
    forward(0, True)
    rows_in(1).wait()
    some = jnp.max(jnp.abs(x[1].reshape(tile, width).astype(F32))) > 0
    none = jnp.logical_not(some)
    pl.when(some)(lambda: forward(1, False))
    pl.when(some)(lambda: share(1, act[...], 2 * tile))
    pl.when(none)(lambda: share(1, act[:tile, :], tile))
    backward(0)
    back_out(0).start()
    pl.when(some)(lambda: backward(1))

    @pl.when(none)
    def _():
        back[1] = jnp.zeros(back.shape[1:], BF16)

    back_out(1).start()
    pl.when(some)(lambda: share(0, x[...].reshape(2 * tile, width), 2 * tile))
    pl.when(none)(lambda: share(0, x[0].reshape(tile, width), tile))
    for rank in range(2):
        back_out(rank).wait()


def run_head(rows, parts, scale, name, *tokens):
    sources, ranks, _, width = rows.shape
    count = lax.axis_size("dom")
    arrays, offsets, owners = zip(*parts)
    owners = [owner for group in owners for owner in group]
    depth = width // count
    layers = 2
    tile = sources * BLOCK
    total = ranks * tile
    part = (layers, count // 2, depth, width)
    bit = lax.axis_index("dom").astype(jnp.int32) & 1
    return pl.pallas_call(
        functools.partial(head_kernel, scale, offsets, len(tokens)),
        grid_spec=pltpu.PrefetchScalarGridSpec(
            num_scalar_prefetch=1,
            grid=(1,),
            in_specs=[ANY] * (1 + len(parts) + len(tokens)),
            out_specs=[ANY, IN_VMEM, IN_VMEM],
            scratch_shapes=[
                pltpu.VMEM((ranks, sources, BLOCK, width), BF16),
                pltpu.VMEM((layers, count, depth, width), BF16),
                pltpu.VMEM((total, width), BF16),
                pltpu.VMEM((ranks, tile, width), F32),
                pltpu.VMEM((ranks, tile, width), F32),
                pltpu.VMEM((layers, total, width), BF16),
                pltpu.VMEM((ranks, sources, BLOCK, width), BF16),
                pltpu.VMEM((count, depth, width), BF16),
                pltpu.SemaphoreType.DMA((ranks,)),
                pltpu.SemaphoreType.DMA((layers, len(owners))),
                pltpu.SemaphoreType.DMA((ranks,)),
            ],
        ),
        out_shape=[pltpu.HBM(rows.shape, BF16)] + [pltpu.VMEM(part, BF16)] * 2,
        compiler_params=pltpu.CompilerParams(vmem_limit_bytes=(20 + 28 * tile // 1024) * MB),
        cost_estimate=pl.CostEstimate(
            flops=24 * total * width * width,
            bytes_accessed=5 * total * width * 2 + width * width * 4,
            transcendentals=total * width,
        ),
        name=name,
    )(jnp.stack([bit] + owners), rows, *arrays, *tokens)


def place_kernel(half, info_ref, own_ref, mirror_ref, out_ref):
    dataset, _, place = block_place(info_ref, pl.program_id(0))
    is_own = dataset // half == place // half
    out_ref[0] = jnp.where(is_own, own_ref[0, 0], mirror_ref[0, 0])


def place_rows(info, own, mirror, row_blocks):
    half, _, _, width = own.shape
    shape = (1, 1, BLOCK, width)

    def index(of_own, block, info_ref):
        dataset, rank, place = block_place(info_ref, block)
        wanted = (dataset // half == place // half) == of_own
        return jnp.where(wanted, lax.rem(dataset, half), 0), jnp.where(wanted, rank, 0), 0, 0

    return pl.pallas_call(
        functools.partial(place_kernel, half),
        grid_spec=pltpu.PrefetchScalarGridSpec(
            num_scalar_prefetch=1,
            grid=(row_blocks,),
            in_specs=[
                pl.BlockSpec(shape, functools.partial(index, True)),
                pl.BlockSpec(shape, functools.partial(index, False)),
            ],
            out_specs=pl.BlockSpec((1, BLOCK, width), lambda block, *_: (block, 0, 0)),
        ),
        out_shape=jax.ShapeDtypeStruct((row_blocks, BLOCK, width), BF16),
        compiler_params=pltpu.CompilerParams(vmem_limit_bytes=16 * MB),
        name="place_rows",
    )(info, own, mirror)


def halo(cut_rows):
    count = lax.axis_size("dom")
    forward = [(i, i + 1) for i in range(count - 1)]
    backward = [(target, source) for source, target in forward]
    low = lax.ppermute(cut_rows, "dom", forward)
    high = lax.ppermute(cut_rows, "dom", backward)
    return low, high


def exchange(blocks, half):
    groups = [list(range(half)), list(range(half, 2 * half))]
    return lax.all_to_all(
        blocks, "head", split_axis=0, concat_axis=0, axis_index_groups=groups, tiled=True
    )


def across(array, half):
    return lax.ppermute(array, "head", [(i, (i + half) % (2 * half)) for i in range(2 * half)])


def after(array, *tokens):
    return pl.pallas_call(
        lambda *refs: None,
        in_specs=[ANY] * (1 + len(tokens)),
        out_specs=ANY,
        out_shape=pltpu.HBM(array.shape, array.dtype),
        input_output_aliases={0: 0},
        compiler_params=pltpu.CompilerParams(vmem_limit_bytes=4 * MB),
        name="after",
    )(hbm(array), *tokens)


def swap(array, bit):
    count = lax.axis_size("dom")
    return lax.ppermute(array, "dom", [(i, i ^ (1 << bit)) for i in range(count)])


def spread_over_dom(shard, token):
    pieces = [shard]
    owners = [lax.axis_index("dom").astype(jnp.int32)]
    for bit in reversed(range(lax.axis_size("dom").bit_length() - 1)):
        pieces = pieces if bit else [after(piece, token) for piece in pieces]
        pieces += [swap(piece, bit) for piece in pieces]
        owners += [owner ^ (1 << bit) for owner in owners]
    return [(piece[None], 0, [owner]) for piece, owner in zip(pieces, owners)]


def merge_kernel(first, tokens, bit_ref, keep_ref, got_ref, *refs):
    send_ref, kept_ref = refs[tokens:]
    bit = bit_ref[0]
    for layer in range(send_ref.shape[0]):
        for j in range(kept_ref.shape[1]):
            for out_ref, at in ((kept_ref, 2 * j + bit), (send_ref, 2 * j + 1 - bit)):
                keep = keep_ref[first + layer, at].astype(F32)
                out_ref[layer, j] = (keep + got_ref[first + layer, at].astype(F32)).astype(BF16)


def merge(keep, got, bit, first, layers, tokens):
    _, count, depth, width = keep.shape
    mine = (lax.axis_index("dom").astype(jnp.int32) >> bit) & 1
    shape = (layers, count // 2, depth, width)
    return pl.pallas_call(
        functools.partial(merge_kernel, first, len(tokens)),
        grid_spec=pltpu.PrefetchScalarGridSpec(
            num_scalar_prefetch=1,
            grid=(1,),
            in_specs=[IN_VMEM, IN_VMEM] + [ANY] * len(tokens),
            out_specs=[IN_VMEM] * 2,
        ),
        out_shape=[pltpu.VMEM(shape, BF16)] * 2,
        compiler_params=pltpu.CompilerParams(vmem_limit_bytes=16 * MB),
        name="merge_shares",
    )(mine.reshape(1), keep, got, *tokens)


def sum_over_dom(keep, got, first, layers, *tokens):
    bits = lax.axis_size("dom").bit_length() - 1
    for bit in range(1, bits):
        send, keep = merge(keep, got, bit, first, layers, tokens)
        got = swap(send, bit)
        first = 0
    return keep[:, 0], got[:, 0], send


def add_kernel(keep_ref, got_ref, *refs):
    refs[-1][...] = (keep_ref[...].astype(F32) + got_ref[...].astype(F32)).astype(BF16)


def add(keep, got, *tokens):
    return pl.pallas_call(
        add_kernel,
        in_specs=[IN_VMEM, IN_VMEM] + [ANY] * len(tokens),
        out_specs=IN_VMEM,
        out_shape=pltpu.VMEM(keep.shape, BF16),
        compiler_params=pltpu.CompilerParams(vmem_limit_bytes=16 * MB),
        name="add_shares",
    )(keep, got, *tokens)


def total_kernel(keep_ref, got_ref, far_ref, *refs):
    total = keep_ref[0].astype(F32) + got_ref[0].astype(F32) + far_ref[0].astype(F32)
    refs[-1][0] = total


def total(keep, got, far, layer, out=None, *tokens):
    _, depth, width = keep.shape
    mine = pl.BlockSpec((1, depth, width), lambda t: (layer, 0, 0))
    came = pl.BlockSpec((1, depth, width), lambda t: (0, 0, 0))
    tokens = list(map(hbm, tokens if out is None else (out,) + tokens))
    return pl.pallas_call(
        total_kernel,
        grid=(1,),
        in_specs=[mine, mine, came] + [ANY] * len(tokens),
        out_specs=mine,
        out_shape=pltpu.HBM(keep.shape, F32),
        input_output_aliases={} if out is None else {3: 0},
        compiler_params=pltpu.CompilerParams(vmem_limit_bytes=16 * MB),
        name="total_share",
    )(keep, got, far, *tokens)


def body(atoms, bonds, triplets, halo_ids, counts, enc_weight, gate_gain, head_weight):
    atom_rows = atoms[0]
    row_count, width = atom_rows.shape
    row_blocks = row_count // BLOCK
    half = lax.axis_size("head") // 2

    count = lax.axis_size("dom")

    gathered = lax.all_gather(head_weight[0], "dom", axis=0, tiled=False)
    own_parts = [(hbm(gathered), 0, [jnp.int32(i) for i in range(count)])]
    far = across(head_weight, half)[0]
    low, high = halo(pick_rows(atom_rows, halo_ids))
    extended = row_count + 2 * low.shape[0]
    codes = ((triplets[0] // LANES) * extended + bonds[0]).reshape(-1)
    pairs = lax.optimization_barrier(bonds[0] * LANES + triplets[0] % LANES).T
    place = lax.axis_index("head").astype(jnp.int32).reshape(1, 1)
    info = jnp.concatenate([counts, place], axis=1)
    own_blocks, mirror_blocks = encode(
        info, codes, atom_rows, low, high, enc_weight, gate_gain[None, :], pairs, half
    )
    near = after(far, hbm(own_blocks))
    mirror_rows = exchange(after(mirror_blocks, hbm(near), hbm(gathered)), half)
    mirror_parts = spread_over_dom(near, mirror_rows)
    own_rows = exchange(after(own_blocks, mirror_rows), half)

    scale = 1.0 / math.sqrt(count * row_count)
    back, send, keep = run_head(mirror_rows, mirror_parts, scale, "head_mirror")
    got = swap(send, 0)
    high_keep, high_got, high_sent = sum_over_dom(keep, got, 1, 1)
    low_keep, low_got, low_sent = sum_over_dom(keep, got, 0, 1, high_sent)
    mirror_back = exchange(after(back, low_sent), half)

    back, send, keep = run_head(own_rows, own_parts, scale, "head_own", low_sent)
    own_back = exchange(after(back, high_got, low_got), half)
    high_part = across(add(high_keep, high_got, send), half)
    low_part = across(add(low_keep, low_got, send), half)
    own_keep, own_got, _ = sum_over_dom(keep, swap(send, 0), 0, 2)
    row_part = place_rows(info, own_back, mirror_back, row_blocks)
    head_part = total(own_keep, own_got, high_part, 1, None, row_part)
    head_part = total(own_keep, own_got, low_part, 0, head_part)
    return row_part.reshape(1, row_count, width), head_part[None]


def solution(mesh):
    return jax.shard_map(
        body,
        mesh=mesh,
        in_specs=(
            P("dom", "head", None),
            P("dom", None, "head"),
            P("dom", None, "head"),
            P("dom", "head"),
            P("dom", "head"),
            P(),
            P(),
            P("head", None, "dom", None),
        ),
        out_specs=(P("dom", "head", None), P("head", None, "dom", None)),
        check_vma=False,
    )
```

```python
import functools
import math

import jax
import jax.numpy as jnp
from jax import lax
from jax.experimental import pallas as pl
from jax.experimental.pallas import tpu as pltpu
from jax.sharding import PartitionSpec as P

BLOCK = 128
LANES = 128
MB = 1 << 20
VMEM = 58 * MB
F32 = jnp.float32
BF16 = jnp.bfloat16
ANY = pl.BlockSpec(memory_space=pl.ANY)
IN_VMEM = pl.BlockSpec(memory_space=pltpu.VMEM)


def sigmoid(x):
    return 0.5 + 0.5 * jnp.tanh(0.5 * x)


def hbm(array):
    return pltpu.with_memory_space_constraint(array, pltpu.HBM)


def resident(shape):
    return pl.BlockSpec(shape, lambda *_: (0,) * len(shape))


def pick_kernel(ids_ref, rows_ref, out_ref):
    count, total = out_ref.shape[0], rows_ref.shape[0]
    places = lax.broadcasted_iota(jnp.int32, (total, count), 0)
    ones = jnp.where(places == ids_ref[...], 1.0, 0.0).astype(BF16)
    out_ref[...] = lax.dot_general(
        ones, rows_ref[...], (((0,), (0,)), ((), ())), preferred_element_type=F32
    ).astype(BF16)


def pick_rows(rows, ids):
    return pl.pallas_call(
        pick_kernel,
        in_specs=[IN_VMEM, IN_VMEM],
        out_specs=IN_VMEM,
        out_shape=jax.ShapeDtypeStruct((ids.shape[1], rows.shape[1]), rows.dtype),
        compiler_params=pltpu.CompilerParams(vmem_limit_bytes=16 * MB),
        name="pick_rows",
    )(ids, rows)


def block_place(info_ref, block):
    sets = info_ref.shape[1] - 1
    start, dataset, rank = jnp.int32(0), jnp.int32(0), jnp.int32(0)
    for candidate in range(sets):
        blocks = info_ref[0, candidate] // BLOCK
        inside = jnp.logical_and(block >= start, block < start + blocks)
        dataset = jnp.where(inside, candidate, dataset)
        rank = jnp.where(inside, block - start, rank)
        start = start + blocks
    return dataset, rank, info_ref[0, sets]


def encode_kernel(
    half, batch, info_ref, codes_ref, atoms_ref, low_ref, high_ref, weight_ref, gain_ref,
    pairs_ref, own_ref, mirror_ref, gained, scores, partial, wanted, gates, gate_rows, staged,
    zeros, weight, sems, weight_sem,
):
    rows, width = atoms_ref.shape
    depth = low_ref.shape[0]
    bond_count = pairs_ref.shape[1]
    sets = 2 * half
    weight_in = pltpu.make_async_copy(weight_ref, weight, weight_sem)
    weight_in.start()
    home = info_ref[0, sets] // half * half
    tile = batch * BLOCK

    def leave(source, slot, act):
        def one(ref, at):
            act(pltpu.make_async_copy(source, ref.at[at], sems.at[slot]))

        pl.when(slot < sets)(lambda: one(own_ref, slot))
        pl.when(slot >= sets)(lambda: one(mirror_ref, slot - sets))

    zeros[...] = jnp.zeros_like(zeros)

    def blank(slot, carry):
        dataset = lax.rem(home + slot // 2, sets)
        empty = info_ref[0, dataset] // BLOCK <= lax.rem(slot, 2)
        pl.when(empty)(lambda: leave(zeros, slot, lambda copy: copy.start()))
        return carry

    lax.fori_loop(0, 2 * sets, blank, 0)

    extended = rows + 2 * depth
    parts = ((atoms_ref, 0), (low_ref, rows), (high_ref, rows + depth))
    for ref, at in parts:
        gained[at : at + ref.shape[0], :] = (ref[...].astype(F32) * gain_ref[...]).astype(BF16)
    for ref, base in parts:
        step = min(ref.shape[0], 2 * LANES)
        for at in range(0, ref.shape[0], step):
            value = lax.dot_general(
                gained[...], ref[at : at + step, :], (((1,), (1,)), ((), ())),
                preferred_element_type=F32,
            )
            for k in range(0, step, LANES):
                piece = (base + at + k) // LANES
                scores[piece * extended : (piece + 1) * extended, :] = value[:, k : k + LANES]

    def encode_tile(step, carry):
        base = pl.multiple_of(step * tile, tile)

        eight = lax.broadcasted_iota(jnp.int32, (8, LANES), 0)

        def score(group, carry):
            for bond in range(bond_count):
                at = bond * rows + base + group * 8
                place = pl.multiple_of(bond * tile + group * 8, 8)
                found = scores[pl.ds(codes_ref[at], 8, stride=0), :]
                for j in range(1, 8):
                    row = scores[pl.ds(codes_ref[at + j], 8, stride=0), :]
                    found = jnp.where(eight == j, row, found)
                partial[pl.ds(place, 8), :] = found
            return carry

        lax.fori_loop(0, tile // 8, score, 0, unroll=4)
        places = lax.broadcasted_iota(jnp.int32, (BLOCK, LANES), 1)
        for block in range(batch):
            pairs = pairs_ref[pl.ds(base + block * BLOCK, BLOCK), :]
            for bond in range(bond_count):
                at = bond * tile + block * BLOCK
                pair = jnp.broadcast_to(pairs[:, bond : bond + 1], (BLOCK, LANES))
                wanted[bond] = pair // LANES
                picked = places == pair % LANES
                logits = jnp.sum(
                    jnp.where(picked, partial[at : at + BLOCK, :], 0.0), axis=1, keepdims=True
                )
                gate = sigmoid(logits * (1.0 / math.sqrt(width)))
                gates[bond] = jnp.broadcast_to(gate, (BLOCK, LANES))
            for at in range(0, extended, LANES):
                acc = jnp.zeros((BLOCK, LANES), F32)
                for bond in range(bond_count):
                    acc = acc + jnp.where(wanted[bond] == places + at, gates[bond], 0.0)
                gate_rows[block * BLOCK : (block + 1) * BLOCK, at : at + LANES] = acc.astype(BF16)
        message = jnp.dot(gate_rows[:, :rows], atoms_ref[...], preferred_element_type=F32)
        for ref, at in ((low_ref, rows), (high_ref, rows + depth)):
            message += jnp.dot(
                gate_rows[:, at : at + depth], ref[...], preferred_element_type=F32
            )
        pl.when(step == 0)(lambda: weight_in.wait())
        update = jnp.dot(message.astype(BF16), weight[...], preferred_element_type=F32)
        own = atoms_ref[pl.ds(base, tile), :].astype(F32)
        staged[step] = (own + update * sigmoid(update)).astype(BF16).reshape(staged.shape[1:])
        for block in range(batch):
            dataset, rank, _ = block_place(info_ref, step * batch + block)
            slot = lax.rem(dataset - home + sets, sets) * 2 + rank
            leave(staged.at[step, block], slot, lambda copy: copy.start())
        return carry

    lax.fori_loop(0, rows // tile, encode_tile, 0)

    def settle(slot, carry):
        leave(zeros, slot, lambda copy: copy.wait())
        return carry

    lax.fori_loop(0, 2 * sets, settle, 0)


def encode(info, codes, atoms, low, high, weight, gain, pairs, half):
    rows, width = atoms.shape
    extended = rows + 2 * low.shape[0]
    bond_count = pairs.shape[1]
    slots = 4 * half
    row_blocks = rows // BLOCK
    batch = 4 if row_blocks % 4 == 0 else 1
    blocks = pl.pallas_call(
        functools.partial(encode_kernel, half, batch),
        grid_spec=pltpu.PrefetchScalarGridSpec(
            num_scalar_prefetch=2,
            grid=(1,),
            in_specs=[IN_VMEM] * 3 + [ANY] + [IN_VMEM] * 2,
            out_specs=[pl.BlockSpec(memory_space=pltpu.HBM)] * 2,
            scratch_shapes=[
                pltpu.VMEM((extended, width), BF16),
                pltpu.VMEM((extended // LANES * extended, LANES), F32),
                pltpu.VMEM((batch * BLOCK * bond_count, LANES), F32),
                pltpu.VMEM((bond_count, BLOCK, LANES), jnp.int32),
                pltpu.VMEM((bond_count, BLOCK, LANES), F32),
                pltpu.VMEM((batch * BLOCK, extended), BF16),
                pltpu.VMEM((row_blocks // batch, batch, BLOCK, width), BF16),
                pltpu.VMEM((BLOCK, width), BF16),
                pltpu.VMEM((width, width), BF16),
                pltpu.SemaphoreType.DMA((slots,)),
                pltpu.SemaphoreType.DMA(()),
            ],
        ),
        out_shape=[pltpu.HBM((2 * half, BLOCK, width), BF16)] * 2,
        compiler_params=pltpu.CompilerParams(vmem_limit_bytes=44 * MB),
        cost_estimate=pl.CostEstimate(
            flops=3 * rows * width * width,
            bytes_accessed=10 * MB,
            transcendentals=rows * width,
        ),
        name="encode_rows",
    )(info, codes, atoms, low, high, hbm(weight), gain, pairs)
    return [rows.reshape(half, 2, BLOCK, width) for rows in blocks]


def head_kernel(scale, offsets, tokens, table_ref, rows_ref, *refs):
    part_count = len(offsets)
    weight_refs = refs[:part_count]
    (
        back_ref, send_ref, keep_ref, x, weights, act, slope, err, grad, back, shares,
        in_sems, weight_sems, back_sems, keep_sems,
    ) = refs[part_count + tokens :]
    width = x.shape[-1]
    tile = x.shape[1] * x.shape[2]
    count = weights.shape[1]
    chunk = width // 4
    chunks = [slice(at, at + chunk) for at in range(0, width, chunk)]
    transposed = (((1,), (1,)), ((), ()))
    over_rows = (((0,), (0,)), ((), ()))
    bit = table_ref[0]

    def rows_in(rank):
        return pltpu.make_async_copy(rows_ref.at[:, rank], x.at[rank], in_sems.at[rank])

    def weights_in(layer):
        copies = []
        for ref, at in zip(weight_refs, offsets):
            for i in range(ref.shape[0]):
                owner = table_ref[1 + len(copies)]
                place = weights.at[layer, owner, pl.ds(at, ref.shape[2])]
                sem = weight_sems.at[layer, len(copies)]
                copies.append(pltpu.make_async_copy(ref.at[i, layer], place, sem))
        return copies

    def back_out(rank):
        return pltpu.make_async_copy(back.at[rank], back_ref.at[:, rank], back_sems.at[rank])

    def keep_out(layer):
        return [
            pltpu.make_async_copy(
                shares.at[layer, 2 * j + bit], keep_ref.at[layer, j], keep_sems.at[layer, j]
            )
            for j in range(count // 2)
        ]

    def matrix(layer):
        return weights[layer].reshape(width, width)

    def forward(rank, wait):
        inputs = x[rank].reshape(tile, width)
        low = matrix(0)
        for at in chunks:
            z = jnp.dot(inputs, low[:, at], preferred_element_type=F32)
            s = sigmoid(z)
            act[rank * tile : (rank + 1) * tile, at] = (z * s).astype(BF16)
            slope[rank, :, at] = s * (1.0 + z * (1.0 - s))
        if wait:
            for copy in weights_in(1):
                copy.wait()
        acts = act[rank * tile : (rank + 1) * tile, :]
        high = matrix(1)
        for at in chunks:
            value = jnp.dot(acts, high[:, at], preferred_element_type=F32)
            value = value - inputs[:, at].astype(F32)
            err[rank, :, at] = value
            grad[1, rank * tile : (rank + 1) * tile, at] = value.astype(BF16)

    def backward(rank):
        rows = slice(rank * tile, (rank + 1) * tile)
        grads = grad[1, rows, :]
        high = matrix(1)
        for at in chunks:
            up = lax.dot_general(grads, high[at, :], transposed, preferred_element_type=F32)
            grad[0, rows, at] = (up * slope[rank, :, at]).astype(BF16)
        grads = grad[0, rows, :]
        low = matrix(0)
        shape = x.shape[1:3] + (chunk,)
        for at in chunks:
            up = lax.dot_general(grads, low[at, :], transposed, preferred_element_type=F32)
            back[rank, :, :, at] = (up - err[rank, :, at]).astype(BF16).reshape(shape)

    def share(layer, acts, rows):
        value = lax.dot_general(
            acts, grad[layer, :rows, :], over_rows, preferred_element_type=F32
        )
        shares[layer] = (value * scale).astype(BF16).reshape(shares.shape[1:])
        for j in range(count // 2):
            send_ref[layer, j] = shares[layer, 2 * j + 1 - bit]

    for rank in range(2):
        rows_in(rank).start()
    for layer in range(2):
        for copy in weights_in(layer):
            copy.start()
    rows_in(0).wait()
    for copy in weights_in(0):
        copy.wait()
    forward(0, True)
    rows_in(1).wait()
    some = jnp.max(jnp.abs(x[1].reshape(tile, width).astype(F32))) > 0
    none = jnp.logical_not(some)
    pl.when(some)(lambda: forward(1, False))
    pl.when(some)(lambda: share(1, act[...], 2 * tile))
    pl.when(none)(lambda: share(1, act[:tile, :], tile))
    for copy in keep_out(1):
        copy.start()
    backward(0)
    back_out(0).start()
    pl.when(some)(lambda: backward(1))

    @pl.when(none)
    def _():
        back[1] = jnp.zeros(back.shape[1:], BF16)

    back_out(1).start()
    pl.when(some)(lambda: share(0, x[...].reshape(2 * tile, width), 2 * tile))
    pl.when(none)(lambda: share(0, x[0].reshape(tile, width), tile))
    for copy in keep_out(0):
        copy.start()
    for rank in range(2):
        back_out(rank).wait()
    for layer in range(2):
        for copy in keep_out(layer):
            copy.wait()


def run_head(rows, parts, scale, name, *tokens):
    sources, ranks, _, width = rows.shape
    count = lax.axis_size("dom")
    arrays, offsets, owners = zip(*parts)
    owners = [owner for group in owners for owner in group]
    depth = width // count
    layers = 2
    tile = sources * BLOCK
    total = ranks * tile
    part = (layers, count // 2, depth, width)
    bit = lax.axis_index("dom").astype(jnp.int32) & 1
    return pl.pallas_call(
        functools.partial(head_kernel, scale, offsets, len(tokens)),
        grid_spec=pltpu.PrefetchScalarGridSpec(
            num_scalar_prefetch=1,
            grid=(1,),
            in_specs=[ANY] * (1 + len(parts) + len(tokens)),
            out_specs=[ANY, IN_VMEM, ANY],
            scratch_shapes=[
                pltpu.VMEM((ranks, sources, BLOCK, width), BF16),
                pltpu.VMEM((layers, count, depth, width), BF16),
                pltpu.VMEM((total, width), BF16),
                pltpu.VMEM((ranks, tile, width), F32),
                pltpu.VMEM((ranks, tile, width), F32),
                pltpu.VMEM((layers, total, width), BF16),
                pltpu.VMEM((ranks, sources, BLOCK, width), BF16),
                pltpu.VMEM((layers, count, depth, width), BF16),
                pltpu.SemaphoreType.DMA((ranks,)),
                pltpu.SemaphoreType.DMA((layers, len(owners))),
                pltpu.SemaphoreType.DMA((ranks,)),
                pltpu.SemaphoreType.DMA((layers, count // 2)),
            ],
        ),
        out_shape=[pltpu.HBM(rows.shape, BF16), pltpu.VMEM(part, BF16), pltpu.HBM(part, BF16)],
        compiler_params=pltpu.CompilerParams(vmem_limit_bytes=(22 + 28 * tile // 1024) * MB),
        cost_estimate=pl.CostEstimate(
            flops=24 * total * width * width,
            bytes_accessed=5 * total * width * 2 + width * width * 4,
            transcendentals=total * width,
        ),
        name=name,
    )(jnp.stack([bit] + owners), rows, *arrays, *tokens)


def place_kernel(half, info_ref, own_ref, mirror_ref, out_ref, held, sems):
    blocks = out_ref.shape[0]

    def load(block, act):
        dataset, rank, place = block_place(info_ref, block)
        is_own = dataset // half == place // half

        def one(ref):
            source = ref.at[lax.rem(dataset, half), rank]
            act(pltpu.make_async_copy(source, held.at[block], sems.at[0, block]))

        pl.when(is_own)(lambda: one(own_ref))
        pl.when(jnp.logical_not(is_own))(lambda: one(mirror_ref))

    def store(block):
        return pltpu.make_async_copy(held.at[block], out_ref.at[block], sems.at[1, block])

    for block in range(blocks):
        load(block, lambda copy: copy.start())
    for block in range(blocks):
        load(block, lambda copy: copy.wait())
        store(block).start()
    for block in range(blocks):
        store(block).wait()


def place_rows(info, own, mirror, row_blocks):
    width = own.shape[-1]
    shape = (row_blocks, BLOCK, width)
    return pl.pallas_call(
        functools.partial(place_kernel, own.shape[0]),
        grid_spec=pltpu.PrefetchScalarGridSpec(
            num_scalar_prefetch=1,
            grid=(1,),
            in_specs=[ANY, ANY],
            out_specs=ANY,
            scratch_shapes=[pltpu.VMEM(shape, BF16), pltpu.SemaphoreType.DMA((2, row_blocks))],
        ),
        out_shape=pltpu.HBM(shape, BF16),
        compiler_params=pltpu.CompilerParams(vmem_limit_bytes=16 * MB),
        name="place_rows",
    )(info, own, mirror)


def halo(cut_rows):
    count = lax.axis_size("dom")
    forward = [(i, i + 1) for i in range(count - 1)]
    backward = [(target, source) for source, target in forward]
    low = lax.ppermute(cut_rows, "dom", forward)
    high = lax.ppermute(cut_rows, "dom", backward)
    return low, high


def exchange(blocks, half):
    groups = [list(range(half)), list(range(half, 2 * half))]
    return lax.all_to_all(
        blocks, "head", split_axis=0, concat_axis=0, axis_index_groups=groups, tiled=True
    )


def across(array, half):
    return lax.ppermute(array, "head", [(i, (i + half) % (2 * half)) for i in range(2 * half)])


def after(array, *tokens):
    return pl.pallas_call(
        lambda *refs: None,
        in_specs=[ANY] * (1 + len(tokens)),
        out_specs=ANY,
        out_shape=pltpu.HBM(array.shape, array.dtype),
        input_output_aliases={0: 0},
        compiler_params=pltpu.CompilerParams(vmem_limit_bytes=4 * MB),
        name="after",
    )(hbm(array), *tokens)


def swap(array, bit):
    count = lax.axis_size("dom")
    return lax.ppermute(array, "dom", [(i, i ^ (1 << bit)) for i in range(count)])


def spread_over_dom(shard, token):
    pieces = [shard]
    owners = [lax.axis_index("dom").astype(jnp.int32)]
    for bit in reversed(range(lax.axis_size("dom").bit_length() - 1)):
        pieces = pieces if bit else [after(piece, token) for piece in pieces]
        pieces += [swap(piece, bit) for piece in pieces]
        owners += [owner ^ (1 << bit) for owner in owners]
    return [(piece[None], 0, [owner]) for piece, owner in zip(pieces, owners)]


def merge_kernel(first, tokens, bit_ref, keep_ref, got_ref, *refs):
    send_ref, kept_ref = refs[tokens:]
    bit = bit_ref[0]
    for layer in range(send_ref.shape[0]):
        for j in range(kept_ref.shape[1]):
            for out_ref, at in ((kept_ref, 2 * j + bit), (send_ref, 2 * j + 1 - bit)):
                keep = keep_ref[first + layer, at].astype(F32)
                out_ref[layer, j] = (keep + got_ref[first + layer, at].astype(F32)).astype(BF16)


def merge(keep, got, bit, first, layers, tokens):
    _, count, depth, width = keep.shape
    mine = (lax.axis_index("dom").astype(jnp.int32) >> bit) & 1
    shape = (layers, count // 2, depth, width)
    return pl.pallas_call(
        functools.partial(merge_kernel, first, len(tokens)),
        grid_spec=pltpu.PrefetchScalarGridSpec(
            num_scalar_prefetch=1,
            grid=(1,),
            in_specs=[IN_VMEM, IN_VMEM] + [ANY] * len(tokens),
            out_specs=[IN_VMEM] * 2,
        ),
        out_shape=[pltpu.VMEM(shape, BF16)] * 2,
        compiler_params=pltpu.CompilerParams(vmem_limit_bytes=16 * MB),
        name="merge_shares",
    )(mine.reshape(1), keep, got, *tokens)


def sum_over_dom(keep, got, first, layers, *tokens):
    bits = lax.axis_size("dom").bit_length() - 1
    for bit in range(1, bits):
        send, keep = merge(keep, got, bit, first, layers, tokens)
        got = swap(send, bit)
        first = 0
    return keep[:, 0], got[:, 0], send


def add_kernel(keep_ref, got_ref, *refs):
    refs[-1][...] = (keep_ref[...].astype(F32) + got_ref[...].astype(F32)).astype(BF16)


def add(keep, got, *tokens):
    return pl.pallas_call(
        add_kernel,
        in_specs=[IN_VMEM, IN_VMEM] + [ANY] * len(tokens),
        out_specs=IN_VMEM,
        out_shape=pltpu.VMEM(keep.shape, BF16),
        compiler_params=pltpu.CompilerParams(vmem_limit_bytes=16 * MB),
        name="add_shares",
    )(keep, got, *tokens)


def total_kernel(keep_ref, got_ref, far_ref, *refs):
    total = keep_ref[0].astype(F32) + got_ref[0].astype(F32) + far_ref[0].astype(F32)
    refs[-1][0] = total


def total(keep, got, far, layer, out=None, *tokens):
    _, depth, width = keep.shape
    mine = pl.BlockSpec((1, depth, width), lambda t: (layer, 0, 0))
    came = pl.BlockSpec((1, depth, width), lambda t: (0, 0, 0))
    tokens = list(map(hbm, tokens if out is None else (out,) + tokens))
    return pl.pallas_call(
        total_kernel,
        grid=(1,),
        in_specs=[mine, mine, came] + [ANY] * len(tokens),
        out_specs=mine,
        out_shape=pltpu.HBM(keep.shape, F32),
        input_output_aliases={} if out is None else {3: 0},
        compiler_params=pltpu.CompilerParams(vmem_limit_bytes=16 * MB),
        name="total_share",
    )(keep, got, far, *tokens)


def body(atoms, bonds, triplets, halo_ids, counts, enc_weight, gate_gain, head_weight):
    atom_rows = atoms[0]
    row_count, width = atom_rows.shape
    row_blocks = row_count // BLOCK
    half = lax.axis_size("head") // 2

    count = lax.axis_size("dom")

    gathered = lax.all_gather(head_weight[0], "dom", axis=0, tiled=False)
    own_parts = [(hbm(gathered), 0, [jnp.int32(i) for i in range(count)])]
    far = across(head_weight, half)[0]
    low, high = halo(pick_rows(atom_rows, halo_ids))
    extended = row_count + 2 * low.shape[0]
    codes = ((triplets[0] // LANES) * extended + bonds[0]).reshape(-1)
    pairs = lax.optimization_barrier(bonds[0] * LANES + triplets[0] % LANES).T
    place = lax.axis_index("head").astype(jnp.int32).reshape(1, 1)
    info = jnp.concatenate([counts, place], axis=1)
    own_blocks, mirror_blocks = encode(
        info, codes, atom_rows, low, high, enc_weight, gate_gain[None, :], pairs, half
    )
    near = after(far, hbm(own_blocks))
    mirror_rows = exchange(after(mirror_blocks, hbm(near), hbm(gathered)), half)
    mirror_parts = spread_over_dom(near, mirror_rows)
    own_rows = exchange(after(own_blocks, mirror_rows), half)

    scale = 1.0 / math.sqrt(count * row_count)
    back, send, keep = run_head(mirror_rows, mirror_parts, scale, "head_mirror")
    got = swap(send, 0)
    high_keep, high_got, high_sent = sum_over_dom(keep, got, 1, 1)
    low_keep, low_got, low_sent = sum_over_dom(keep, got, 0, 1, high_sent)
    mirror_back = exchange(after(back, low_sent), half)

    back, send, keep = run_head(own_rows, own_parts, scale, "head_own", low_sent)
    high_sum = add(high_keep, high_got, send)
    low_sum = add(low_keep, low_got, send)
    high_part = across(high_sum, half)
    low_part = across(low_sum, half)
    own_back = exchange(after(back, high_sum, low_sum), half)
    own_keep, own_got, _ = sum_over_dom(keep, swap(send, 0), 0, 2, low_sum)
    row_part = place_rows(info, own_back, mirror_back, row_blocks)
    head_part = total(own_keep, own_got, high_part, 1)
    head_part = total(own_keep, own_got, low_part, 0, head_part)
    return row_part.reshape(1, row_count, width), head_part[None]


def solution(mesh):
    return jax.shard_map(
        body,
        mesh=mesh,
        in_specs=(
            P("dom", "head", None),
            P("dom", None, "head"),
            P("dom", None, "head"),
            P("dom", "head"),
            P("dom", "head"),
            P(),
            P(),
            P("head", None, "dom", None),
        ),
        out_specs=(P("dom", "head", None), P("head", None, "dom", None)),
        check_vma=False,
    )
```

```python
import functools
import math

import jax
import jax.numpy as jnp
from jax import lax
from jax.experimental import pallas as pl
from jax.experimental.pallas import tpu as pltpu
from jax.sharding import PartitionSpec as P

BLOCK = 128
LANES = 128
MB = 1 << 20
VMEM = 58 * MB
F32 = jnp.float32
BF16 = jnp.bfloat16
ANY = pl.BlockSpec(memory_space=pl.ANY)
IN_VMEM = pl.BlockSpec(memory_space=pltpu.VMEM)


def sigmoid(x):
    return 0.5 + 0.5 * jnp.tanh(0.5 * x)


def hbm(array):
    return pltpu.with_memory_space_constraint(array, pltpu.HBM)


def resident(shape):
    return pl.BlockSpec(shape, lambda *_: (0,) * len(shape))


def pick_kernel(ids_ref, rows_ref, out_ref):
    count, total = out_ref.shape[0], rows_ref.shape[0]
    places = lax.broadcasted_iota(jnp.int32, (total, count), 0)
    ones = jnp.where(places == ids_ref[...], 1.0, 0.0).astype(BF16)
    out_ref[...] = lax.dot_general(
        ones, rows_ref[...], (((0,), (0,)), ((), ())), preferred_element_type=F32
    ).astype(BF16)


def pick_rows(rows, ids):
    return pl.pallas_call(
        pick_kernel,
        in_specs=[IN_VMEM, IN_VMEM],
        out_specs=IN_VMEM,
        out_shape=jax.ShapeDtypeStruct((ids.shape[1], rows.shape[1]), rows.dtype),
        compiler_params=pltpu.CompilerParams(vmem_limit_bytes=16 * MB),
        name="pick_rows",
    )(ids, rows)


def block_place(info_ref, block):
    sets = info_ref.shape[1] - 1
    start, dataset, rank = jnp.int32(0), jnp.int32(0), jnp.int32(0)
    for candidate in range(sets):
        blocks = info_ref[0, candidate] // BLOCK
        inside = jnp.logical_and(block >= start, block < start + blocks)
        dataset = jnp.where(inside, candidate, dataset)
        rank = jnp.where(inside, block - start, rank)
        start = start + blocks
    return dataset, rank, info_ref[0, sets]


def encode_kernel(
    half, batch, info_ref, codes_ref, atoms_ref, low_ref, high_ref, weight_ref, gain_ref,
    pairs_ref, own_ref, mirror_ref, gained, scores, partial, wanted, gates, gate_rows, staged,
    zeros, weight, sems, weight_sem,
):
    rows, width = atoms_ref.shape
    depth = low_ref.shape[0]
    bond_count = pairs_ref.shape[1]
    sets = 2 * half
    weight_in = pltpu.make_async_copy(weight_ref, weight, weight_sem)
    weight_in.start()
    home = info_ref[0, sets] // half * half
    tile = batch * BLOCK

    def leave(source, slot, act):
        def one(ref, at):
            act(pltpu.make_async_copy(source, ref.at[at], sems.at[slot]))

        pl.when(slot < sets)(lambda: one(own_ref, slot))
        pl.when(slot >= sets)(lambda: one(mirror_ref, slot - sets))

    zeros[...] = jnp.zeros_like(zeros)

    def blank(slot, carry):
        dataset = lax.rem(home + slot // 2, sets)
        empty = info_ref[0, dataset] // BLOCK <= lax.rem(slot, 2)
        pl.when(empty)(lambda: leave(zeros, slot, lambda copy: copy.start()))
        return carry

    lax.fori_loop(0, 2 * sets, blank, 0)

    extended = rows + 2 * depth
    parts = ((atoms_ref, 0), (low_ref, rows), (high_ref, rows + depth))
    for ref, at in parts:
        gained[at : at + ref.shape[0], :] = (ref[...].astype(F32) * gain_ref[...]).astype(BF16)
    for ref, base in parts:
        step = min(ref.shape[0], 2 * LANES)
        for at in range(0, ref.shape[0], step):
            value = lax.dot_general(
                gained[...], ref[at : at + step, :], (((1,), (1,)), ((), ())),
                preferred_element_type=F32,
            )
            for k in range(0, step, LANES):
                piece = (base + at + k) // LANES
                scores[piece * extended : (piece + 1) * extended, :] = value[:, k : k + LANES]

    def encode_tile(step, carry):
        base = pl.multiple_of(step * tile, tile)

        eight = lax.broadcasted_iota(jnp.int32, (8, LANES), 0)

        def score(group, carry):
            for bond in range(bond_count):
                at = bond * rows + base + group * 8
                place = pl.multiple_of(bond * tile + group * 8, 8)
                found = scores[pl.ds(codes_ref[at], 8, stride=0), :]
                for j in range(1, 8):
                    row = scores[pl.ds(codes_ref[at + j], 8, stride=0), :]
                    found = jnp.where(eight == j, row, found)
                partial[pl.ds(place, 8), :] = found
            return carry

        lax.fori_loop(0, tile // 8, score, 0, unroll=4)
        places = lax.broadcasted_iota(jnp.int32, (BLOCK, LANES), 1)
        for block in range(batch):
            pairs = pairs_ref[pl.ds(base + block * BLOCK, BLOCK), :]
            for bond in range(bond_count):
                at = bond * tile + block * BLOCK
                pair = jnp.broadcast_to(pairs[:, bond : bond + 1], (BLOCK, LANES))
                wanted[bond] = pair // LANES
                picked = places == pair % LANES
                logits = jnp.sum(
                    jnp.where(picked, partial[at : at + BLOCK, :], 0.0), axis=1, keepdims=True
                )
                gate = sigmoid(logits * (1.0 / math.sqrt(width)))
                gates[bond] = jnp.broadcast_to(gate, (BLOCK, LANES))
            for at in range(0, extended, LANES):
                acc = jnp.zeros((BLOCK, LANES), F32)
                for bond in range(bond_count):
                    acc = acc + jnp.where(wanted[bond] == places + at, gates[bond], 0.0)
                gate_rows[block * BLOCK : (block + 1) * BLOCK, at : at + LANES] = acc.astype(BF16)
        message = jnp.dot(gate_rows[:, :rows], atoms_ref[...], preferred_element_type=F32)
        for ref, at in ((low_ref, rows), (high_ref, rows + depth)):
            message += jnp.dot(
                gate_rows[:, at : at + depth], ref[...], preferred_element_type=F32
            )
        pl.when(step == 0)(lambda: weight_in.wait())
        update = jnp.dot(message.astype(BF16), weight[...], preferred_element_type=F32)
        own = atoms_ref[pl.ds(base, tile), :].astype(F32)
        staged[step] = (own + update * sigmoid(update)).astype(BF16).reshape(staged.shape[1:])
        for block in range(batch):
            dataset, rank, _ = block_place(info_ref, step * batch + block)
            slot = lax.rem(dataset - home + sets, sets) * 2 + rank
            leave(staged.at[step, block], slot, lambda copy: copy.start())
        return carry

    lax.fori_loop(0, rows // tile, encode_tile, 0)

    def settle(slot, carry):
        leave(zeros, slot, lambda copy: copy.wait())
        return carry

    lax.fori_loop(0, 2 * sets, settle, 0)


def encode(info, codes, atoms, low, high, weight, gain, pairs, half):
    rows, width = atoms.shape
    extended = rows + 2 * low.shape[0]
    bond_count = pairs.shape[1]
    slots = 4 * half
    row_blocks = rows // BLOCK
    batch = 4 if row_blocks % 4 == 0 else 1
    blocks = pl.pallas_call(
        functools.partial(encode_kernel, half, batch),
        grid_spec=pltpu.PrefetchScalarGridSpec(
            num_scalar_prefetch=2,
            grid=(1,),
            in_specs=[IN_VMEM] * 3 + [ANY] + [IN_VMEM] * 2,
            out_specs=[pl.BlockSpec(memory_space=pltpu.HBM)] * 2,
            scratch_shapes=[
                pltpu.VMEM((extended, width), BF16),
                pltpu.VMEM((extended // LANES * extended, LANES), F32),
                pltpu.VMEM((batch * BLOCK * bond_count, LANES), F32),
                pltpu.VMEM((bond_count, BLOCK, LANES), jnp.int32),
                pltpu.VMEM((bond_count, BLOCK, LANES), F32),
                pltpu.VMEM((batch * BLOCK, extended), BF16),
                pltpu.VMEM((row_blocks // batch, batch, BLOCK, width), BF16),
                pltpu.VMEM((BLOCK, width), BF16),
                pltpu.VMEM((width, width), BF16),
                pltpu.SemaphoreType.DMA((slots,)),
                pltpu.SemaphoreType.DMA(()),
            ],
        ),
        out_shape=[pltpu.HBM((2 * half, BLOCK, width), BF16)] * 2,
        compiler_params=pltpu.CompilerParams(vmem_limit_bytes=44 * MB),
        cost_estimate=pl.CostEstimate(
            flops=3 * rows * width * width,
            bytes_accessed=10 * MB,
            transcendentals=rows * width,
        ),
        name="encode_rows",
    )(info, codes, atoms, low, high, hbm(weight), gain, pairs)
    return [rows.reshape(half, 2, BLOCK, width) for rows in blocks]


def head_kernel(scale, offsets, tokens, table_ref, rows_ref, *refs):
    part_count = len(offsets)
    weight_refs = refs[:part_count]
    (
        back_ref, send_ref, keep_ref, x, weights, act, slope, err, grad, back, shares,
        in_sems, weight_sems, back_sems, keep_sems,
    ) = refs[part_count + tokens :]
    width = x.shape[-1]
    tile = x.shape[1] * x.shape[2]
    count = weights.shape[1]
    chunk = width // 4
    chunks = [slice(at, at + chunk) for at in range(0, width, chunk)]
    transposed = (((1,), (1,)), ((), ()))
    over_rows = (((0,), (0,)), ((), ()))
    bit = table_ref[0]

    def rows_in(rank):
        return pltpu.make_async_copy(rows_ref.at[:, rank], x.at[rank], in_sems.at[rank])

    def weights_in(layer):
        copies = []
        for ref, at in zip(weight_refs, offsets):
            for i in range(ref.shape[0]):
                owner = table_ref[1 + len(copies)]
                place = weights.at[layer, owner, pl.ds(at, ref.shape[2])]
                sem = weight_sems.at[layer, len(copies)]
                copies.append(pltpu.make_async_copy(ref.at[i, layer], place, sem))
        return copies

    def back_out(rank):
        return pltpu.make_async_copy(back.at[rank], back_ref.at[:, rank], back_sems.at[rank])

    def keep_out(layer):
        return [
            pltpu.make_async_copy(
                shares.at[layer, 2 * j + bit], keep_ref.at[layer, j], keep_sems.at[layer, j]
            )
            for j in range(count // 2)
        ]

    def matrix(layer):
        return weights[layer].reshape(width, width)

    def forward(rank, wait):
        inputs = x[rank].reshape(tile, width)
        low = matrix(0)
        for at in chunks:
            z = jnp.dot(inputs, low[:, at], preferred_element_type=F32)
            s = sigmoid(z)
            act[rank * tile : (rank + 1) * tile, at] = (z * s).astype(BF16)
            slope[rank, :, at] = s * (1.0 + z * (1.0 - s))
        if wait:
            for copy in weights_in(1):
                copy.wait()
        acts = act[rank * tile : (rank + 1) * tile, :]
        high = matrix(1)
        for at in chunks:
            value = jnp.dot(acts, high[:, at], preferred_element_type=F32)
            value = value - inputs[:, at].astype(F32)
            err[rank, :, at] = value
            grad[1, rank * tile : (rank + 1) * tile, at] = value.astype(BF16)

    def backward(rank):
        rows = slice(rank * tile, (rank + 1) * tile)
        grads = grad[1, rows, :]
        high = matrix(1)
        for at in chunks:
            up = lax.dot_general(grads, high[at, :], transposed, preferred_element_type=F32)
            grad[0, rows, at] = (up * slope[rank, :, at]).astype(BF16)
        grads = grad[0, rows, :]
        low = matrix(0)
        shape = x.shape[1:3] + (chunk,)
        for at in chunks:
            up = lax.dot_general(grads, low[at, :], transposed, preferred_element_type=F32)
            back[rank, :, :, at] = (up - err[rank, :, at]).astype(BF16).reshape(shape)

    def share(layer, acts, rows):
        value = lax.dot_general(
            acts, grad[layer, :rows, :], over_rows, preferred_element_type=F32
        )
        shares[layer] = (value * scale).astype(BF16).reshape(shares.shape[1:])
        for j in range(count // 2):
            send_ref[layer, j] = shares[layer, 2 * j + 1 - bit]

    for rank in range(2):
        rows_in(rank).start()
    for layer in range(2):
        for copy in weights_in(layer):
            copy.start()
    rows_in(0).wait()
    for copy in weights_in(0):
        copy.wait()
    forward(0, True)
    rows_in(1).wait()
    some = jnp.max(jnp.abs(x[1].reshape(tile, width).astype(F32))) > 0
    none = jnp.logical_not(some)
    pl.when(some)(lambda: forward(1, False))
    pl.when(some)(lambda: share(1, act[...], 2 * tile))
    pl.when(none)(lambda: share(1, act[:tile, :], tile))
    for copy in keep_out(1):
        copy.start()
    backward(0)
    back_out(0).start()
    pl.when(some)(lambda: backward(1))

    @pl.when(none)
    def _():
        back[1] = jnp.zeros(back.shape[1:], BF16)

    back_out(1).start()
    pl.when(some)(lambda: share(0, x[...].reshape(2 * tile, width), 2 * tile))
    pl.when(none)(lambda: share(0, x[0].reshape(tile, width), tile))
    for copy in keep_out(0):
        copy.start()
    for rank in range(2):
        back_out(rank).wait()
    for layer in range(2):
        for copy in keep_out(layer):
            copy.wait()


def run_head(rows, parts, scale, name, *tokens):
    sources, ranks, _, width = rows.shape
    count = lax.axis_size("dom")
    arrays, offsets, owners = zip(*parts)
    owners = [owner for group in owners for owner in group]
    depth = width // count
    layers = 2
    tile = sources * BLOCK
    total = ranks * tile
    part = (layers, count // 2, depth, width)
    bit = lax.axis_index("dom").astype(jnp.int32) & 1
    return pl.pallas_call(
        functools.partial(head_kernel, scale, offsets, len(tokens)),
        grid_spec=pltpu.PrefetchScalarGridSpec(
            num_scalar_prefetch=1,
            grid=(1,),
            in_specs=[ANY] * (1 + len(parts) + len(tokens)),
            out_specs=[ANY, IN_VMEM, ANY],
            scratch_shapes=[
                pltpu.VMEM((ranks, sources, BLOCK, width), BF16),
                pltpu.VMEM((layers, count, depth, width), BF16),
                pltpu.VMEM((total, width), BF16),
                pltpu.VMEM((ranks, tile, width), F32),
                pltpu.VMEM((ranks, tile, width), F32),
                pltpu.VMEM((layers, total, width), BF16),
                pltpu.VMEM((ranks, sources, BLOCK, width), BF16),
                pltpu.VMEM((layers, count, depth, width), BF16),
                pltpu.SemaphoreType.DMA((ranks,)),
                pltpu.SemaphoreType.DMA((layers, len(owners))),
                pltpu.SemaphoreType.DMA((ranks,)),
                pltpu.SemaphoreType.DMA((layers, count // 2)),
            ],
        ),
        out_shape=[pltpu.HBM(rows.shape, BF16), pltpu.VMEM(part, BF16), pltpu.HBM(part, BF16)],
        compiler_params=pltpu.CompilerParams(vmem_limit_bytes=(22 + 28 * tile // 1024) * MB),
        cost_estimate=pl.CostEstimate(
            flops=24 * total * width * width,
            bytes_accessed=5 * total * width * 2 + width * width * 4,
            transcendentals=total * width,
        ),
        name=name,
    )(jnp.stack([bit] + owners), rows, *arrays, *tokens)


def place_kernel(half, info_ref, own_ref, mirror_ref, out_ref, held, sems):
    blocks = out_ref.shape[0]

    def load(block, act):
        dataset, rank, place = block_place(info_ref, block)
        is_own = dataset // half == place // half

        def one(ref):
            source = ref.at[lax.rem(dataset, half), rank]
            act(pltpu.make_async_copy(source, held.at[block], sems.at[0, block]))

        pl.when(is_own)(lambda: one(own_ref))
        pl.when(jnp.logical_not(is_own))(lambda: one(mirror_ref))

    def store(block):
        return pltpu.make_async_copy(held.at[block], out_ref.at[block], sems.at[1, block])

    for block in range(blocks):
        load(block, lambda copy: copy.start())
    for block in range(blocks):
        load(block, lambda copy: copy.wait())
        store(block).start()
    for block in range(blocks):
        store(block).wait()


def place_rows(info, own, mirror, row_blocks):
    width = own.shape[-1]
    shape = (row_blocks, BLOCK, width)
    return pl.pallas_call(
        functools.partial(place_kernel, own.shape[0]),
        grid_spec=pltpu.PrefetchScalarGridSpec(
            num_scalar_prefetch=1,
            grid=(1,),
            in_specs=[ANY, ANY],
            out_specs=ANY,
            scratch_shapes=[pltpu.VMEM(shape, BF16), pltpu.SemaphoreType.DMA((2, row_blocks))],
        ),
        out_shape=pltpu.HBM(shape, BF16),
        compiler_params=pltpu.CompilerParams(vmem_limit_bytes=16 * MB),
        name="place_rows",
    )(info, own, mirror)


def halo(cut_rows):
    count = lax.axis_size("dom")
    forward = [(i, i + 1) for i in range(count - 1)]
    backward = [(target, source) for source, target in forward]
    low = lax.ppermute(cut_rows, "dom", forward)
    high = lax.ppermute(cut_rows, "dom", backward)
    return low, high


def exchange(blocks, half):
    groups = [list(range(half)), list(range(half, 2 * half))]
    return lax.all_to_all(
        blocks, "head", split_axis=0, concat_axis=0, axis_index_groups=groups, tiled=True
    )


def across(array, half):
    return lax.ppermute(array, "head", [(i, (i + half) % (2 * half)) for i in range(2 * half)])


def after(array, *tokens):
    return pl.pallas_call(
        lambda *refs: None,
        in_specs=[ANY] * (1 + len(tokens)),
        out_specs=ANY,
        out_shape=pltpu.HBM(array.shape, array.dtype),
        input_output_aliases={0: 0},
        compiler_params=pltpu.CompilerParams(vmem_limit_bytes=4 * MB),
        name="after",
    )(hbm(array), *tokens)


def swap(array, bit):
    count = lax.axis_size("dom")
    return lax.ppermute(array, "dom", [(i, i ^ (1 << bit)) for i in range(count)])


def spread_over_dom(shard, token):
    pieces = [shard]
    owners = [lax.axis_index("dom").astype(jnp.int32)]
    for bit in reversed(range(lax.axis_size("dom").bit_length() - 1)):
        pieces = pieces if bit else [after(piece, token) for piece in pieces]
        pieces += [swap(piece, bit) for piece in pieces]
        owners += [owner ^ (1 << bit) for owner in owners]
    return [(piece[None], 0, [owner]) for piece, owner in zip(pieces, owners)]


def merge_kernel(first, tokens, bit_ref, keep_ref, got_ref, *refs):
    send_ref, kept_ref = refs[tokens:]
    bit = bit_ref[0]
    for layer in range(send_ref.shape[0]):
        for j in range(kept_ref.shape[1]):
            for out_ref, at in ((kept_ref, 2 * j + bit), (send_ref, 2 * j + 1 - bit)):
                keep = keep_ref[first + layer, at].astype(F32)
                out_ref[layer, j] = (keep + got_ref[first + layer, at].astype(F32)).astype(BF16)


def merge(keep, got, bit, first, layers, tokens):
    _, count, depth, width = keep.shape
    mine = (lax.axis_index("dom").astype(jnp.int32) >> bit) & 1
    shape = (layers, count // 2, depth, width)
    return pl.pallas_call(
        functools.partial(merge_kernel, first, len(tokens)),
        grid_spec=pltpu.PrefetchScalarGridSpec(
            num_scalar_prefetch=1,
            grid=(1,),
            in_specs=[IN_VMEM, IN_VMEM] + [ANY] * len(tokens),
            out_specs=[IN_VMEM] * 2,
        ),
        out_shape=[pltpu.VMEM(shape, BF16)] * 2,
        compiler_params=pltpu.CompilerParams(vmem_limit_bytes=16 * MB),
        name="merge_shares",
    )(mine.reshape(1), keep, got, *tokens)


def sum_over_dom(keep, got, first, layers, *tokens):
    bits = lax.axis_size("dom").bit_length() - 1
    for bit in range(1, bits):
        send, keep = merge(keep, got, bit, first, layers, tokens)
        got = swap(send, bit)
        first = 0
    return keep[:, 0], got[:, 0], send


def add_kernel(keep_ref, got_ref, *refs):
    refs[-1][...] = (keep_ref[...].astype(F32) + got_ref[...].astype(F32)).astype(BF16)


def add(keep, got, *tokens):
    return pl.pallas_call(
        add_kernel,
        in_specs=[IN_VMEM, IN_VMEM] + [ANY] * len(tokens),
        out_specs=IN_VMEM,
        out_shape=pltpu.VMEM(keep.shape, BF16),
        compiler_params=pltpu.CompilerParams(vmem_limit_bytes=16 * MB),
        name="add_shares",
    )(keep, got, *tokens)


def total_kernel(keep_ref, got_ref, far_ref, *refs):
    total = keep_ref[0].astype(F32) + got_ref[0].astype(F32) + far_ref[0].astype(F32)
    refs[-1][0] = total


def total(keep, got, far, layer, out=None, *tokens):
    _, depth, width = keep.shape
    mine = pl.BlockSpec((1, depth, width), lambda t: (layer, 0, 0))
    came = pl.BlockSpec((1, depth, width), lambda t: (0, 0, 0))
    tokens = list(map(hbm, tokens if out is None else (out,) + tokens))
    return pl.pallas_call(
        total_kernel,
        grid=(1,),
        in_specs=[mine, mine, came] + [ANY] * len(tokens),
        out_specs=mine,
        out_shape=pltpu.HBM(keep.shape, F32),
        input_output_aliases={} if out is None else {3: 0},
        compiler_params=pltpu.CompilerParams(vmem_limit_bytes=16 * MB),
        name="total_share",
    )(keep, got, far, *tokens)


def body(atoms, bonds, triplets, halo_ids, counts, enc_weight, gate_gain, head_weight):
    atom_rows = atoms[0]
    row_count, width = atom_rows.shape
    row_blocks = row_count // BLOCK
    half = lax.axis_size("head") // 2

    count = lax.axis_size("dom")

    gathered = lax.all_gather(head_weight[0], "dom", axis=0, tiled=False)
    own_parts = [(hbm(gathered), 0, [jnp.int32(i) for i in range(count)])]
    far = across(head_weight, half)[0]
    low, high = halo(pick_rows(atom_rows, halo_ids))
    extended = row_count + 2 * low.shape[0]
    codes = ((triplets[0] // LANES) * extended + bonds[0]).reshape(-1)
    pairs = lax.optimization_barrier(bonds[0] * LANES + triplets[0] % LANES).T
    place = lax.axis_index("head").astype(jnp.int32).reshape(1, 1)
    info = jnp.concatenate([counts, place], axis=1)
    own_blocks, mirror_blocks = encode(
        info, codes, atom_rows, low, high, enc_weight, gate_gain[None, :], pairs, half
    )
    near = after(far, hbm(own_blocks))
    mirror_rows = exchange(after(mirror_blocks, hbm(near), hbm(gathered)), half)
    mirror_parts = spread_over_dom(near, mirror_rows)
    own_rows = exchange(after(own_blocks, mirror_rows), half)

    scale = 1.0 / math.sqrt(count * row_count)
    back, send, keep = run_head(mirror_rows, mirror_parts, scale, "head_mirror")
    got = swap(send, 0)
    high_keep, high_got, high_sent = sum_over_dom(keep, got, 1, 1)
    mirror_back = exchange(after(back, high_sent), half)
    high_sum = add(high_keep, high_got)
    high_part = across(high_sum, half)
    low_keep, low_got, low_sent = sum_over_dom(keep, got, 0, 1, high_got)

    back, send, keep = run_head(own_rows, own_parts, scale, "head_own", high_sum, low_sent)
    low_sum = add(low_keep, low_got, send)
    low_part = across(low_sum, half)
    own_back = exchange(after(back, high_part, low_sum), half)
    own_keep, own_got, _ = sum_over_dom(keep, swap(send, 0), 0, 2, low_sum)
    row_part = place_rows(info, own_back, mirror_back, row_blocks)
    head_part = total(own_keep, own_got, high_part, 1)
    head_part = total(own_keep, own_got, low_part, 0, head_part, row_part)
    return row_part.reshape(1, row_count, width), head_part[None]


def solution(mesh):
    return jax.shard_map(
        body,
        mesh=mesh,
        in_specs=(
            P("dom", "head", None),
            P("dom", None, "head"),
            P("dom", None, "head"),
            P("dom", "head"),
            P("dom", "head"),
            P(),
            P(),
            P("head", None, "dom", None),
        ),
        out_specs=(P("dom", "head", None), P("head", None, "dom", None)),
        check_vma=False,
    )
```

```python
import functools
import math

import jax
import jax.numpy as jnp
from jax import lax
from jax.experimental import pallas as pl
from jax.experimental.pallas import tpu as pltpu
from jax.sharding import PartitionSpec as P

BLOCK = 128
LANES = 128
MB = 1 << 20
VMEM = 58 * MB
F32 = jnp.float32
BF16 = jnp.bfloat16
ANY = pl.BlockSpec(memory_space=pl.ANY)
IN_VMEM = pl.BlockSpec(memory_space=pltpu.VMEM)


def sigmoid(x):
    return 0.5 + 0.5 * jnp.tanh(0.5 * x)


def hbm(array):
    return pltpu.with_memory_space_constraint(array, pltpu.HBM)


def resident(shape):
    return pl.BlockSpec(shape, lambda *_: (0,) * len(shape))


def pick_kernel(ids_ref, rows_ref, out_ref):
    count, total = out_ref.shape[0], rows_ref.shape[0]
    places = lax.broadcasted_iota(jnp.int32, (total, count), 0)
    ones = jnp.where(places == ids_ref[...], 1.0, 0.0).astype(BF16)
    out_ref[...] = lax.dot_general(
        ones, rows_ref[...], (((0,), (0,)), ((), ())), preferred_element_type=F32
    ).astype(BF16)


def pick_rows(rows, ids):
    return pl.pallas_call(
        pick_kernel,
        in_specs=[IN_VMEM, IN_VMEM],
        out_specs=IN_VMEM,
        out_shape=jax.ShapeDtypeStruct((ids.shape[1], rows.shape[1]), rows.dtype),
        compiler_params=pltpu.CompilerParams(vmem_limit_bytes=16 * MB),
        name="pick_rows",
    )(ids, rows)


def block_place(info_ref, block):
    sets = info_ref.shape[1] - 1
    start, dataset, rank = jnp.int32(0), jnp.int32(0), jnp.int32(0)
    for candidate in range(sets):
        blocks = info_ref[0, candidate] // BLOCK
        inside = jnp.logical_and(block >= start, block < start + blocks)
        dataset = jnp.where(inside, candidate, dataset)
        rank = jnp.where(inside, block - start, rank)
        start = start + blocks
    return dataset, rank, info_ref[0, sets]


def encode_kernel(
    half, batch, info_ref, codes_ref, atoms_ref, low_ref, high_ref, weight_ref, gain_ref,
    pairs_ref, own_ref, mirror_ref, gained, scores, partial, wanted, gates, gate_rows, staged,
    zeros, weight, sems, weight_sem,
):
    rows, width = atoms_ref.shape
    depth = low_ref.shape[0]
    bond_count = pairs_ref.shape[1]
    sets = 2 * half
    weight_in = pltpu.make_async_copy(weight_ref, weight, weight_sem)
    weight_in.start()
    home = info_ref[0, sets] // half * half
    tile = batch * BLOCK

    def leave(source, slot, act):
        def one(ref, at):
            act(pltpu.make_async_copy(source, ref.at[at], sems.at[slot]))

        pl.when(slot < sets)(lambda: one(own_ref, slot))
        pl.when(slot >= sets)(lambda: one(mirror_ref, slot - sets))

    zeros[...] = jnp.zeros_like(zeros)

    def blank(slot, carry):
        dataset = lax.rem(home + slot // 2, sets)
        empty = info_ref[0, dataset] // BLOCK <= lax.rem(slot, 2)
        pl.when(empty)(lambda: leave(zeros, slot, lambda copy: copy.start()))
        return carry

    lax.fori_loop(0, 2 * sets, blank, 0)

    extended = rows + 2 * depth
    parts = ((atoms_ref, 0), (low_ref, rows), (high_ref, rows + depth))
    for ref, at in parts:
        gained[at : at + ref.shape[0], :] = (ref[...].astype(F32) * gain_ref[...]).astype(BF16)
    for ref, base in parts:
        step = min(ref.shape[0], 2 * LANES)
        for at in range(0, ref.shape[0], step):
            value = lax.dot_general(
                gained[...], ref[at : at + step, :], (((1,), (1,)), ((), ())),
                preferred_element_type=F32,
            )
            for k in range(0, step, LANES):
                piece = (base + at + k) // LANES
                scores[piece * extended : (piece + 1) * extended, :] = value[:, k : k + LANES]

    def encode_tile(step, carry):
        base = pl.multiple_of(step * tile, tile)

        eight = lax.broadcasted_iota(jnp.int32, (8, LANES), 0)

        def score(group, carry):
            for bond in range(bond_count):
                at = bond * rows + base + group * 8
                place = pl.multiple_of(bond * tile + group * 8, 8)
                found = scores[pl.ds(codes_ref[at], 8, stride=0), :]
                for j in range(1, 8):
                    row = scores[pl.ds(codes_ref[at + j], 8, stride=0), :]
                    found = jnp.where(eight == j, row, found)
                partial[pl.ds(place, 8), :] = found
            return carry

        lax.fori_loop(0, tile // 8, score, 0, unroll=4)
        places = lax.broadcasted_iota(jnp.int32, (BLOCK, LANES), 1)
        for block in range(batch):
            pairs = pairs_ref[pl.ds(base + block * BLOCK, BLOCK), :]
            for bond in range(bond_count):
                at = bond * tile + block * BLOCK
                pair = jnp.broadcast_to(pairs[:, bond : bond + 1], (BLOCK, LANES))
                wanted[bond] = pair // LANES
                picked = places == pair % LANES
                logits = jnp.sum(
                    jnp.where(picked, partial[at : at + BLOCK, :], 0.0), axis=1, keepdims=True
                )
                gate = sigmoid(logits * (1.0 / math.sqrt(width)))
                gates[bond] = jnp.broadcast_to(gate, (BLOCK, LANES))
            for at in range(0, extended, LANES):
                acc = jnp.zeros((BLOCK, LANES), F32)
                for bond in range(bond_count):
                    acc = acc + jnp.where(wanted[bond] == places + at, gates[bond], 0.0)
                gate_rows[block * BLOCK : (block + 1) * BLOCK, at : at + LANES] = acc.astype(BF16)
        message = jnp.dot(gate_rows[:, :rows], atoms_ref[...], preferred_element_type=F32)
        for ref, at in ((low_ref, rows), (high_ref, rows + depth)):
            message += jnp.dot(
                gate_rows[:, at : at + depth], ref[...], preferred_element_type=F32
            )
        pl.when(step == 0)(lambda: weight_in.wait())
        update = jnp.dot(message.astype(BF16), weight[...], preferred_element_type=F32)
        own = atoms_ref[pl.ds(base, tile), :].astype(F32)
        staged[step] = (own + update * sigmoid(update)).astype(BF16).reshape(staged.shape[1:])
        for block in range(batch):
            dataset, rank, _ = block_place(info_ref, step * batch + block)
            slot = lax.rem(dataset - home + sets, sets) * 2 + rank
            leave(staged.at[step, block], slot, lambda copy: copy.start())
        return carry

    lax.fori_loop(0, rows // tile, encode_tile, 0)

    def settle(slot, carry):
        leave(zeros, slot, lambda copy: copy.wait())
        return carry

    lax.fori_loop(0, 2 * sets, settle, 0)


def encode(info, codes, atoms, low, high, weight, gain, pairs, half):
    rows, width = atoms.shape
    extended = rows + 2 * low.shape[0]
    bond_count = pairs.shape[1]
    slots = 4 * half
    row_blocks = rows // BLOCK
    batch = 4 if row_blocks % 4 == 0 else 1
    blocks = pl.pallas_call(
        functools.partial(encode_kernel, half, batch),
        grid_spec=pltpu.PrefetchScalarGridSpec(
            num_scalar_prefetch=2,
            grid=(1,),
            in_specs=[IN_VMEM] * 3 + [ANY] + [IN_VMEM] * 2,
            out_specs=[pl.BlockSpec(memory_space=pltpu.HBM)] * 2,
            scratch_shapes=[
                pltpu.VMEM((extended, width), BF16),
                pltpu.VMEM((extended // LANES * extended, LANES), F32),
                pltpu.VMEM((batch * BLOCK * bond_count, LANES), F32),
                pltpu.VMEM((bond_count, BLOCK, LANES), jnp.int32),
                pltpu.VMEM((bond_count, BLOCK, LANES), F32),
                pltpu.VMEM((batch * BLOCK, extended), BF16),
                pltpu.VMEM((row_blocks // batch, batch, BLOCK, width), BF16),
                pltpu.VMEM((BLOCK, width), BF16),
                pltpu.VMEM((width, width), BF16),
                pltpu.SemaphoreType.DMA((slots,)),
                pltpu.SemaphoreType.DMA(()),
            ],
        ),
        out_shape=[pltpu.HBM((2 * half, BLOCK, width), BF16)] * 2,
        compiler_params=pltpu.CompilerParams(vmem_limit_bytes=44 * MB),
        cost_estimate=pl.CostEstimate(
            flops=3 * rows * width * width,
            bytes_accessed=10 * MB,
            transcendentals=rows * width,
        ),
        name="encode_rows",
    )(info, codes, atoms, low, high, hbm(weight), gain, pairs)
    return [rows.reshape(half, 2, BLOCK, width) for rows in blocks]


def head_kernel(scale, offsets, tokens, table_ref, rows_ref, *refs):
    part_count = len(offsets)
    weight_refs = refs[:part_count]
    (
        back_ref, send_ref, keep_ref, x, weights, act, slope, err, grad, back, shares,
        in_sems, weight_sems, back_sems, keep_sems,
    ) = refs[part_count + tokens :]
    width = x.shape[-1]
    tile = x.shape[1] * x.shape[2]
    count = weights.shape[1]
    chunk = width // 4
    chunks = [slice(at, at + chunk) for at in range(0, width, chunk)]
    transposed = (((1,), (1,)), ((), ()))
    over_rows = (((0,), (0,)), ((), ()))
    bit = table_ref[0]

    def rows_in(rank):
        return pltpu.make_async_copy(rows_ref.at[:, rank], x.at[rank], in_sems.at[rank])

    def weights_in(layer):
        copies = []
        for ref, at in zip(weight_refs, offsets):
            for i in range(ref.shape[0]):
                owner = table_ref[1 + len(copies)]
                place = weights.at[layer, owner, pl.ds(at, ref.shape[2])]
                sem = weight_sems.at[layer, len(copies)]
                copies.append(pltpu.make_async_copy(ref.at[i, layer], place, sem))
        return copies

    def back_out(rank):
        return pltpu.make_async_copy(back.at[rank], back_ref.at[:, rank], back_sems.at[rank])

    def keep_out(layer):
        return [
            pltpu.make_async_copy(
                shares.at[layer, 2 * j + bit], keep_ref.at[layer, j], keep_sems.at[layer, j]
            )
            for j in range(count // 2)
        ]

    def matrix(layer):
        return weights[layer].reshape(width, width)

    def forward(rank, wait):
        inputs = x[rank].reshape(tile, width)
        low = matrix(0)
        for at in chunks:
            z = jnp.dot(inputs, low[:, at], preferred_element_type=F32)
            s = sigmoid(z)
            act[rank * tile : (rank + 1) * tile, at] = (z * s).astype(BF16)
            slope[rank, :, at] = s * (1.0 + z * (1.0 - s))
        if wait:
            for copy in weights_in(1):
                copy.wait()
        acts = act[rank * tile : (rank + 1) * tile, :]
        high = matrix(1)
        for at in chunks:
            value = jnp.dot(acts, high[:, at], preferred_element_type=F32)
            value = value - inputs[:, at].astype(F32)
            err[rank, :, at] = value
            grad[1, rank * tile : (rank + 1) * tile, at] = value.astype(BF16)

    def backward(rank):
        rows = slice(rank * tile, (rank + 1) * tile)
        grads = grad[1, rows, :]
        high = matrix(1)
        for at in chunks:
            up = lax.dot_general(grads, high[at, :], transposed, preferred_element_type=F32)
            grad[0, rows, at] = (up * slope[rank, :, at]).astype(BF16)
        grads = grad[0, rows, :]
        low = matrix(0)
        shape = x.shape[1:3] + (chunk,)
        for at in chunks:
            up = lax.dot_general(grads, low[at, :], transposed, preferred_element_type=F32)
            back[rank, :, :, at] = (up - err[rank, :, at]).astype(BF16).reshape(shape)

    def share(layer, acts, rows):
        value = lax.dot_general(
            acts, grad[layer, :rows, :], over_rows, preferred_element_type=F32
        )
        shares[layer] = (value * scale).astype(BF16).reshape(shares.shape[1:])
        for j in range(count // 2):
            send_ref[layer, j] = shares[layer, 2 * j + 1 - bit]

    for rank in range(2):
        rows_in(rank).start()
    for layer in range(2):
        for copy in weights_in(layer):
            copy.start()
    rows_in(0).wait()
    for copy in weights_in(0):
        copy.wait()
    forward(0, True)
    rows_in(1).wait()
    some = jnp.max(jnp.abs(x[1].reshape(tile, width).astype(F32))) > 0
    none = jnp.logical_not(some)
    pl.when(some)(lambda: forward(1, False))
    pl.when(some)(lambda: share(1, act[...], 2 * tile))
    pl.when(none)(lambda: share(1, act[:tile, :], tile))
    for copy in keep_out(1):
        copy.start()
    backward(0)
    back_out(0).start()
    pl.when(some)(lambda: backward(1))

    @pl.when(none)
    def _():
        back[1] = jnp.zeros(back.shape[1:], BF16)

    back_out(1).start()
    pl.when(some)(lambda: share(0, x[...].reshape(2 * tile, width), 2 * tile))
    pl.when(none)(lambda: share(0, x[0].reshape(tile, width), tile))
    for copy in keep_out(0):
        copy.start()
    for rank in range(2):
        back_out(rank).wait()
    for layer in range(2):
        for copy in keep_out(layer):
            copy.wait()


def run_head(rows, parts, scale, name, *tokens):
    sources, ranks, _, width = rows.shape
    count = lax.axis_size("dom")
    arrays, offsets, owners = zip(*parts)
    owners = [owner for group in owners for owner in group]
    depth = width // count
    layers = 2
    tile = sources * BLOCK
    total = ranks * tile
    part = (layers, count // 2, depth, width)
    bit = lax.axis_index("dom").astype(jnp.int32) & 1
    return pl.pallas_call(
        functools.partial(head_kernel, scale, offsets, len(tokens)),
        grid_spec=pltpu.PrefetchScalarGridSpec(
            num_scalar_prefetch=1,
            grid=(1,),
            in_specs=[ANY] * (1 + len(parts) + len(tokens)),
            out_specs=[ANY, IN_VMEM, ANY],
            scratch_shapes=[
                pltpu.VMEM((ranks, sources, BLOCK, width), BF16),
                pltpu.VMEM((layers, count, depth, width), BF16),
                pltpu.VMEM((total, width), BF16),
                pltpu.VMEM((ranks, tile, width), F32),
                pltpu.VMEM((ranks, tile, width), F32),
                pltpu.VMEM((layers, total, width), BF16),
                pltpu.VMEM((ranks, sources, BLOCK, width), BF16),
                pltpu.VMEM((layers, count, depth, width), BF16),
                pltpu.SemaphoreType.DMA((ranks,)),
                pltpu.SemaphoreType.DMA((layers, len(owners))),
                pltpu.SemaphoreType.DMA((ranks,)),
                pltpu.SemaphoreType.DMA((layers, count // 2)),
            ],
        ),
        out_shape=[pltpu.HBM(rows.shape, BF16), pltpu.VMEM(part, BF16), pltpu.HBM(part, BF16)],
        compiler_params=pltpu.CompilerParams(vmem_limit_bytes=(22 + 28 * tile // 1024) * MB),
        cost_estimate=pl.CostEstimate(
            flops=24 * total * width * width,
            bytes_accessed=5 * total * width * 2 + width * width * 4,
            transcendentals=total * width,
        ),
        name=name,
    )(jnp.stack([bit] + owners), rows, *arrays, *tokens)


def place_kernel(half, info_ref, own_ref, mirror_ref, out_ref, held, sems):
    blocks = out_ref.shape[0]

    def load(block, act):
        dataset, rank, place = block_place(info_ref, block)
        is_own = dataset // half == place // half

        def one(ref):
            source = ref.at[lax.rem(dataset, half), rank]
            act(pltpu.make_async_copy(source, held.at[block], sems.at[0, block]))

        pl.when(is_own)(lambda: one(own_ref))
        pl.when(jnp.logical_not(is_own))(lambda: one(mirror_ref))

    def store(block):
        return pltpu.make_async_copy(held.at[block], out_ref.at[block], sems.at[1, block])

    for block in range(blocks):
        load(block, lambda copy: copy.start())
    for block in range(blocks):
        load(block, lambda copy: copy.wait())
        store(block).start()
    for block in range(blocks):
        store(block).wait()


def place_rows(info, own, mirror, row_blocks):
    width = own.shape[-1]
    shape = (row_blocks, BLOCK, width)
    return pl.pallas_call(
        functools.partial(place_kernel, own.shape[0]),
        grid_spec=pltpu.PrefetchScalarGridSpec(
            num_scalar_prefetch=1,
            grid=(1,),
            in_specs=[ANY, ANY],
            out_specs=ANY,
            scratch_shapes=[pltpu.VMEM(shape, BF16), pltpu.SemaphoreType.DMA((2, row_blocks))],
        ),
        out_shape=pltpu.HBM(shape, BF16),
        compiler_params=pltpu.CompilerParams(vmem_limit_bytes=16 * MB),
        name="place_rows",
    )(info, own, mirror)


def halo(cut_rows):
    count = lax.axis_size("dom")
    forward = [(i, i + 1) for i in range(count - 1)]
    backward = [(target, source) for source, target in forward]
    low = lax.ppermute(cut_rows, "dom", forward)
    high = lax.ppermute(cut_rows, "dom", backward)
    return low, high


def exchange(blocks, half):
    groups = [list(range(half)), list(range(half, 2 * half))]
    return lax.all_to_all(
        blocks, "head", split_axis=0, concat_axis=0, axis_index_groups=groups, tiled=True
    )


def across(array, half):
    return lax.ppermute(array, "head", [(i, (i + half) % (2 * half)) for i in range(2 * half)])


def after(array, *tokens):
    return pl.pallas_call(
        lambda *refs: None,
        in_specs=[ANY] * (1 + len(tokens)),
        out_specs=ANY,
        out_shape=pltpu.HBM(array.shape, array.dtype),
        input_output_aliases={0: 0},
        compiler_params=pltpu.CompilerParams(vmem_limit_bytes=4 * MB),
        name="after",
    )(hbm(array), *tokens)


def swap(array, bit):
    count = lax.axis_size("dom")
    return lax.ppermute(array, "dom", [(i, i ^ (1 << bit)) for i in range(count)])


def spread_over_dom(shard, token):
    pieces = [shard]
    owners = [lax.axis_index("dom").astype(jnp.int32)]
    for bit in reversed(range(lax.axis_size("dom").bit_length() - 1)):
        pieces = pieces if bit else [after(piece, token) for piece in pieces]
        pieces += [swap(piece, bit) for piece in pieces]
        owners += [owner ^ (1 << bit) for owner in owners]
    return [(piece[None], 0, [owner]) for piece, owner in zip(pieces, owners)]


def merge_kernel(tokens, bit_ref, keep_ref, got_ref, *refs):
    send_ref, kept_ref = refs[tokens:]
    bit = bit_ref[0]
    for layer in range(send_ref.shape[0]):
        for j in range(kept_ref.shape[1]):
            for out_ref, at in ((kept_ref, 2 * j + bit), (send_ref, 2 * j + 1 - bit)):
                keep = keep_ref[layer, at].astype(F32)
                out_ref[layer, j] = (keep + got_ref[layer, at].astype(F32)).astype(BF16)


def merge(keep, got, bit, tokens):
    layers, count, depth, width = keep.shape
    mine = (lax.axis_index("dom").astype(jnp.int32) >> bit) & 1
    shape = (layers, count // 2, depth, width)
    return pl.pallas_call(
        functools.partial(merge_kernel, len(tokens)),
        grid_spec=pltpu.PrefetchScalarGridSpec(
            num_scalar_prefetch=1,
            grid=(1,),
            in_specs=[IN_VMEM, IN_VMEM] + [ANY] * len(tokens),
            out_specs=[IN_VMEM] * 2,
        ),
        out_shape=[pltpu.VMEM(shape, BF16)] * 2,
        compiler_params=pltpu.CompilerParams(vmem_limit_bytes=16 * MB),
        name="merge_shares",
    )(mine.reshape(1), keep, got, *tokens)


def sum_over_dom(keep, got, *tokens):
    bits = lax.axis_size("dom").bit_length() - 1
    for bit in range(1, bits):
        send, keep = merge(keep, got, bit, tokens)
        got = swap(send, bit)
    return keep[:, 0], got[:, 0], send


def add_kernel(keep_ref, got_ref, *refs):
    refs[-1][...] = (keep_ref[...].astype(F32) + got_ref[...].astype(F32)).astype(BF16)


def add(keep, got, *tokens):
    return pl.pallas_call(
        add_kernel,
        in_specs=[IN_VMEM, IN_VMEM] + [ANY] * len(tokens),
        out_specs=IN_VMEM,
        out_shape=pltpu.VMEM(keep.shape, BF16),
        compiler_params=pltpu.CompilerParams(vmem_limit_bytes=16 * MB),
        name="add_shares",
    )(keep, got, *tokens)


def total_kernel(keep_ref, got_ref, far_ref, *refs):
    total = keep_ref[...].astype(F32) + got_ref[...].astype(F32) + far_ref[...].astype(F32)
    refs[-1][...] = total


def total(keep, got, far, *tokens):
    layers, depth, width = keep.shape
    block = pl.BlockSpec((1, depth, width), lambda t: (t, 0, 0))
    return pl.pallas_call(
        total_kernel,
        grid=(layers,),
        in_specs=[block] * 3 + [ANY] * len(tokens),
        out_specs=block,
        out_shape=pltpu.HBM(keep.shape, F32),
        compiler_params=pltpu.CompilerParams(vmem_limit_bytes=16 * MB),
        name="total_shares",
    )(keep, got, far, *map(hbm, tokens))


def body(atoms, bonds, triplets, halo_ids, counts, enc_weight, gate_gain, head_weight):
    atom_rows = atoms[0]
    row_count, width = atom_rows.shape
    row_blocks = row_count // BLOCK
    half = lax.axis_size("head") // 2

    count = lax.axis_size("dom")

    gathered = lax.all_gather(head_weight[0], "dom", axis=0, tiled=False)
    own_parts = [(hbm(gathered), 0, [jnp.int32(i) for i in range(count)])]
    far = across(head_weight, half)[0]
    low, high = halo(pick_rows(atom_rows, halo_ids))
    extended = row_count + 2 * low.shape[0]
    codes = ((triplets[0] // LANES) * extended + bonds[0]).reshape(-1)
    pairs = lax.optimization_barrier(bonds[0] * LANES + triplets[0] % LANES).T
    place = lax.axis_index("head").astype(jnp.int32).reshape(1, 1)
    info = jnp.concatenate([counts, place], axis=1)
    own_blocks, mirror_blocks = encode(
        info, codes, atom_rows, low, high, enc_weight, gate_gain[None, :], pairs, half
    )
    near = after(far, hbm(own_blocks))
    mirror_rows = exchange(after(mirror_blocks, hbm(near), hbm(gathered)), half)
    mirror_parts = spread_over_dom(near, mirror_rows)
    own_rows = exchange(after(own_blocks, mirror_rows), half)

    scale = 1.0 / math.sqrt(count * row_count)
    back, send, keep = run_head(mirror_rows, mirror_parts, scale, "head_mirror")
    got = swap(send, 0)
    mirror_keep, mirror_got, sent = sum_over_dom(keep, got)
    mirror_back = exchange(after(back, sent), half)

    back, send, keep = run_head(own_rows, own_parts, scale, "head_own", sent)
    mirror_sum = add(mirror_keep, mirror_got, send)
    far_sum = across(mirror_sum, half)
    own_back = exchange(after(back, mirror_sum), half)
    own_keep, own_got, _ = sum_over_dom(keep, swap(send, 0), mirror_sum)
    row_part = place_rows(info, own_back, mirror_back, row_blocks)
    head_part = total(own_keep, own_got, far_sum, row_part)
    return row_part.reshape(1, row_count, width), head_part[None]


def solution(mesh):
    return jax.shard_map(
        body,
        mesh=mesh,
        in_specs=(
            P("dom", "head", None),
            P("dom", None, "head"),
            P("dom", None, "head"),
            P("dom", "head"),
            P("dom", "head"),
            P(),
            P(),
            P("head", None, "dom", None),
        ),
        out_specs=(P("dom", "head", None), P("head", None, "dom", None)),
        check_vma=False,
    )
```

```python
import functools
import math

import jax
import jax.numpy as jnp
from jax import lax
from jax.experimental import pallas as pl
from jax.experimental.pallas import tpu as pltpu
from jax.sharding import PartitionSpec as P

BLOCK = 128
LANES = 128
MB = 1 << 20
VMEM = 58 * MB
F32 = jnp.float32
BF16 = jnp.bfloat16
ANY = pl.BlockSpec(memory_space=pl.ANY)
IN_VMEM = pl.BlockSpec(memory_space=pltpu.VMEM)


def sigmoid(x):
    return 0.5 + 0.5 * jnp.tanh(0.5 * x)


def hbm(array):
    return pltpu.with_memory_space_constraint(array, pltpu.HBM)


def vmem(array):
    return pltpu.with_memory_space_constraint(array, pltpu.VMEM)


def resident(shape):
    return pl.BlockSpec(shape, lambda *_: (0,) * len(shape))


def pick_kernel(ids_ref, rows_ref, out_ref):
    count, total = out_ref.shape[0], rows_ref.shape[0]
    places = lax.broadcasted_iota(jnp.int32, (total, count), 0)
    ones = jnp.where(places == ids_ref[...], 1.0, 0.0).astype(BF16)
    out_ref[...] = lax.dot_general(
        ones, rows_ref[...], (((0,), (0,)), ((), ())), preferred_element_type=F32
    ).astype(BF16)


def pick_rows(rows, ids):
    return pl.pallas_call(
        pick_kernel,
        in_specs=[IN_VMEM, IN_VMEM],
        out_specs=IN_VMEM,
        out_shape=jax.ShapeDtypeStruct((ids.shape[1], rows.shape[1]), rows.dtype),
        compiler_params=pltpu.CompilerParams(vmem_limit_bytes=16 * MB),
        name="pick_rows",
    )(ids, rows)


def block_place(info_ref, block):
    sets = info_ref.shape[1] - 1
    start, dataset, rank = jnp.int32(0), jnp.int32(0), jnp.int32(0)
    for candidate in range(sets):
        blocks = info_ref[0, candidate] // BLOCK
        inside = jnp.logical_and(block >= start, block < start + blocks)
        dataset = jnp.where(inside, candidate, dataset)
        rank = jnp.where(inside, block - start, rank)
        start = start + blocks
    return dataset, rank, info_ref[0, sets]


def encode_kernel(
    half, batch, info_ref, codes_ref, atoms_ref, low_ref, high_ref, weight_ref, gain_ref,
    pairs_ref, own_ref, mirror_ref, gained, scores, partial, wanted, gates, gate_rows, staged,
    zeros, weight, sems, weight_sem,
):
    rows, width = atoms_ref.shape
    depth = low_ref.shape[0]
    bond_count = pairs_ref.shape[1]
    sets = 2 * half
    weight_in = pltpu.make_async_copy(weight_ref, weight, weight_sem)
    weight_in.start()
    home = info_ref[0, sets] // half * half
    tile = batch * BLOCK

    def leave(source, slot, act):
        def one(ref, at):
            act(pltpu.make_async_copy(source, ref.at[at], sems.at[slot]))

        pl.when(slot < sets)(lambda: one(own_ref, slot))
        pl.when(slot >= sets)(lambda: one(mirror_ref, slot - sets))

    zeros[...] = jnp.zeros_like(zeros)

    def blank(slot, carry):
        dataset = lax.rem(home + slot // 2, sets)
        empty = info_ref[0, dataset] // BLOCK <= lax.rem(slot, 2)
        pl.when(empty)(lambda: leave(zeros, slot, lambda copy: copy.start()))
        return carry

    lax.fori_loop(0, 2 * sets, blank, 0)

    extended = rows + 2 * depth
    parts = ((atoms_ref, 0), (low_ref, rows), (high_ref, rows + depth))
    for ref, at in parts:
        gained[at : at + ref.shape[0], :] = (ref[...].astype(F32) * gain_ref[...]).astype(BF16)
    for ref, base in parts:
        step = min(ref.shape[0], 2 * LANES)
        for at in range(0, ref.shape[0], step):
            value = lax.dot_general(
                gained[...], ref[at : at + step, :], (((1,), (1,)), ((), ())),
                preferred_element_type=F32,
            )
            for k in range(0, step, LANES):
                piece = (base + at + k) // LANES
                scores[piece * extended : (piece + 1) * extended, :] = value[:, k : k + LANES]

    def encode_tile(step, carry):
        base = pl.multiple_of(step * tile, tile)

        eight = lax.broadcasted_iota(jnp.int32, (8, LANES), 0)

        def score(group, carry):
            for bond in range(bond_count):
                at = bond * rows + base + group * 8
                place = pl.multiple_of(bond * tile + group * 8, 8)
                found = scores[pl.ds(codes_ref[at], 8, stride=0), :]
                for j in range(1, 8):
                    row = scores[pl.ds(codes_ref[at + j], 8, stride=0), :]
                    found = jnp.where(eight == j, row, found)
                partial[pl.ds(place, 8), :] = found
            return carry

        lax.fori_loop(0, tile // 8, score, 0, unroll=4)
        places = lax.broadcasted_iota(jnp.int32, (BLOCK, LANES), 1)
        for block in range(batch):
            pairs = pairs_ref[pl.ds(base + block * BLOCK, BLOCK), :]
            for bond in range(bond_count):
                at = bond * tile + block * BLOCK
                pair = jnp.broadcast_to(pairs[:, bond : bond + 1], (BLOCK, LANES))
                wanted[bond] = pair // LANES
                picked = places == pair % LANES
                logits = jnp.sum(
                    jnp.where(picked, partial[at : at + BLOCK, :], 0.0), axis=1, keepdims=True
                )
                gate = sigmoid(logits * (1.0 / math.sqrt(width)))
                gates[bond] = jnp.broadcast_to(gate, (BLOCK, LANES))
            for at in range(0, extended, LANES):
                acc = jnp.zeros((BLOCK, LANES), F32)
                for bond in range(bond_count):
                    acc = acc + jnp.where(wanted[bond] == places + at, gates[bond], 0.0)
                gate_rows[block * BLOCK : (block + 1) * BLOCK, at : at + LANES] = acc.astype(BF16)
        message = jnp.dot(gate_rows[:, :rows], atoms_ref[...], preferred_element_type=F32)
        for ref, at in ((low_ref, rows), (high_ref, rows + depth)):
            message += jnp.dot(
                gate_rows[:, at : at + depth], ref[...], preferred_element_type=F32
            )
        pl.when(step == 0)(lambda: weight_in.wait())
        update = jnp.dot(message.astype(BF16), weight[...], preferred_element_type=F32)
        own = atoms_ref[pl.ds(base, tile), :].astype(F32)
        staged[step] = (own + update * sigmoid(update)).astype(BF16).reshape(staged.shape[1:])
        for block in range(batch):
            dataset, rank, _ = block_place(info_ref, step * batch + block)
            slot = lax.rem(dataset - home + sets, sets) * 2 + rank
            leave(staged.at[step, block], slot, lambda copy: copy.start())
        return carry

    lax.fori_loop(0, rows // tile, encode_tile, 0)

    def settle(slot, carry):
        leave(zeros, slot, lambda copy: copy.wait())
        return carry

    lax.fori_loop(0, 2 * sets, settle, 0)


def encode(info, codes, atoms, low, high, weight, gain, pairs, half):
    rows, width = atoms.shape
    extended = rows + 2 * low.shape[0]
    bond_count = pairs.shape[1]
    slots = 4 * half
    row_blocks = rows // BLOCK
    batch = 4 if row_blocks % 4 == 0 else 1
    blocks = pl.pallas_call(
        functools.partial(encode_kernel, half, batch),
        grid_spec=pltpu.PrefetchScalarGridSpec(
            num_scalar_prefetch=2,
            grid=(1,),
            in_specs=[IN_VMEM] * 3 + [ANY] + [IN_VMEM] * 2,
            out_specs=[pl.BlockSpec(memory_space=pltpu.HBM)] * 2,
            scratch_shapes=[
                pltpu.VMEM((extended, width), BF16),
                pltpu.VMEM((extended // LANES * extended, LANES), F32),
                pltpu.VMEM((batch * BLOCK * bond_count, LANES), F32),
                pltpu.VMEM((bond_count, BLOCK, LANES), jnp.int32),
                pltpu.VMEM((bond_count, BLOCK, LANES), F32),
                pltpu.VMEM((batch * BLOCK, extended), BF16),
                pltpu.VMEM((row_blocks // batch, batch, BLOCK, width), BF16),
                pltpu.VMEM((BLOCK, width), BF16),
                pltpu.VMEM((width, width), BF16),
                pltpu.SemaphoreType.DMA((slots,)),
                pltpu.SemaphoreType.DMA(()),
            ],
        ),
        out_shape=[pltpu.HBM((2 * half, BLOCK, width), BF16)] * 2,
        compiler_params=pltpu.CompilerParams(vmem_limit_bytes=44 * MB),
        cost_estimate=pl.CostEstimate(
            flops=3 * rows * width * width,
            bytes_accessed=10 * MB,
            transcendentals=rows * width,
        ),
        name="encode_rows",
    )(info, codes, atoms, low, high, hbm(weight), gain, pairs)
    return [rows.reshape(half, 2, BLOCK, width) for rows in blocks]


def head_kernel(scale, offsets, tokens, table_ref, rows_ref, *refs):
    part_count = len(offsets)
    weight_refs = refs[:part_count]
    (
        back_ref, send_ref, keep_ref, x, weights, act, slope, err, grad, back, shares,
        in_sems, weight_sems, back_sems,
    ) = refs[part_count + tokens :]
    width = x.shape[-1]
    tile = x.shape[1] * x.shape[2]
    count = weights.shape[1]
    chunk = width // 4
    chunks = [slice(at, at + chunk) for at in range(0, width, chunk)]
    transposed = (((1,), (1,)), ((), ()))
    over_rows = (((0,), (0,)), ((), ()))
    bit = table_ref[0]

    def rows_in(rank):
        return pltpu.make_async_copy(rows_ref.at[:, rank], x.at[rank], in_sems.at[rank])

    def weights_in(layer):
        copies = []
        for ref, at in zip(weight_refs, offsets):
            for i in range(ref.shape[0]):
                owner = table_ref[1 + len(copies)]
                place = weights.at[layer, owner, pl.ds(at, ref.shape[2])]
                sem = weight_sems.at[layer, len(copies)]
                copies.append(pltpu.make_async_copy(ref.at[i, layer], place, sem))
        return copies

    def back_out(rank):
        return pltpu.make_async_copy(back.at[rank], back_ref.at[:, rank], back_sems.at[rank])

    def matrix(layer):
        return weights[layer].reshape(width, width)

    def forward(rank, wait):
        inputs = x[rank].reshape(tile, width)
        low = matrix(0)
        for at in chunks:
            z = jnp.dot(inputs, low[:, at], preferred_element_type=F32)
            s = sigmoid(z)
            act[rank * tile : (rank + 1) * tile, at] = (z * s).astype(BF16)
            slope[rank, :, at] = s * (1.0 + z * (1.0 - s))
        if wait:
            for copy in weights_in(1):
                copy.wait()
        acts = act[rank * tile : (rank + 1) * tile, :]
        high = matrix(1)
        for at in chunks:
            value = jnp.dot(acts, high[:, at], preferred_element_type=F32)
            value = value - inputs[:, at].astype(F32)
            err[rank, :, at] = value
            grad[1, rank * tile : (rank + 1) * tile, at] = value.astype(BF16)

    def backward(rank):
        rows = slice(rank * tile, (rank + 1) * tile)
        grads = grad[1, rows, :]
        high = matrix(1)
        for at in chunks:
            up = lax.dot_general(grads, high[at, :], transposed, preferred_element_type=F32)
            grad[0, rows, at] = (up * slope[rank, :, at]).astype(BF16)
        grads = grad[0, rows, :]
        low = matrix(0)
        shape = x.shape[1:3] + (chunk,)
        for at in chunks:
            up = lax.dot_general(grads, low[at, :], transposed, preferred_element_type=F32)
            back[rank, :, :, at] = (up - err[rank, :, at]).astype(BF16).reshape(shape)

    def share(layer, acts, rows):
        value = lax.dot_general(
            acts, grad[layer, :rows, :], over_rows, preferred_element_type=F32
        )
        shares[...] = (value * scale).astype(BF16).reshape(shares.shape)
        for j in range(count // 2):
            keep_ref[layer, j] = shares[2 * j + bit]
            send_ref[layer, j] = shares[2 * j + 1 - bit]

    for rank in range(2):
        rows_in(rank).start()
    for layer in range(2):
        for copy in weights_in(layer):
            copy.start()
    rows_in(0).wait()
    for copy in weights_in(0):
        copy.wait()
    forward(0, True)
    rows_in(1).wait()
    some = jnp.max(jnp.abs(x[1].reshape(tile, width).astype(F32))) > 0
    none = jnp.logical_not(some)
    pl.when(some)(lambda: forward(1, False))
    pl.when(some)(lambda: share(1, act[...], 2 * tile))
    pl.when(none)(lambda: share(1, act[:tile, :], tile))
    backward(0)
    back_out(0).start()
    pl.when(some)(lambda: backward(1))

    @pl.when(none)
    def _():
        back[1] = jnp.zeros(back.shape[1:], BF16)

    back_out(1).start()
    pl.when(some)(lambda: share(0, x[...].reshape(2 * tile, width), 2 * tile))
    pl.when(none)(lambda: share(0, x[0].reshape(tile, width), tile))
    for rank in range(2):
        back_out(rank).wait()


def run_head(rows, parts, scale, name, *tokens):
    sources, ranks, _, width = rows.shape
    count = lax.axis_size("dom")
    arrays, offsets, owners = zip(*parts)
    owners = [owner for group in owners for owner in group]
    depth = width // count
    layers = 2
    tile = sources * BLOCK
    total = ranks * tile
    part = (layers, count // 2, depth, width)
    bit = lax.axis_index("dom").astype(jnp.int32) & 1
    return pl.pallas_call(
        functools.partial(head_kernel, scale, offsets, len(tokens)),
        grid_spec=pltpu.PrefetchScalarGridSpec(
            num_scalar_prefetch=1,
            grid=(1,),
            in_specs=[ANY] * (1 + len(parts) + len(tokens)),
            out_specs=[ANY, IN_VMEM, IN_VMEM],
            scratch_shapes=[
                pltpu.VMEM((ranks, sources, BLOCK, width), BF16),
                pltpu.VMEM((layers, count, depth, width), BF16),
                pltpu.VMEM((total, width), BF16),
                pltpu.VMEM((ranks, tile, width), F32),
                pltpu.VMEM((ranks, tile, width), F32),
                pltpu.VMEM((layers, total, width), BF16),
                pltpu.VMEM((ranks, sources, BLOCK, width), BF16),
                pltpu.VMEM((count, depth, width), BF16),
                pltpu.SemaphoreType.DMA((ranks,)),
                pltpu.SemaphoreType.DMA((layers, len(owners))),
                pltpu.SemaphoreType.DMA((ranks,)),
            ],
        ),
        out_shape=[pltpu.HBM(rows.shape, BF16)] + [pltpu.VMEM(part, BF16)] * 2,
        compiler_params=pltpu.CompilerParams(vmem_limit_bytes=(20 + 28 * tile // 1024) * MB),
        cost_estimate=pl.CostEstimate(
            flops=24 * total * width * width,
            bytes_accessed=5 * total * width * 2 + width * width * 4,
            transcendentals=total * width,
        ),
        name=name,
    )(jnp.stack([bit] + owners), rows, *arrays, *tokens)


def place_kernel(half, info_ref, own_ref, mirror_ref, out_ref, held, sems):
    blocks = out_ref.shape[0]

    def load(block, act):
        dataset, rank, place = block_place(info_ref, block)
        is_own = dataset // half == place // half

        def one(ref):
            source = ref.at[lax.rem(dataset, half), rank]
            act(pltpu.make_async_copy(source, held.at[block], sems.at[0, block]))

        pl.when(is_own)(lambda: one(own_ref))
        pl.when(jnp.logical_not(is_own))(lambda: one(mirror_ref))

    def store(block):
        return pltpu.make_async_copy(held.at[block], out_ref.at[block], sems.at[1, block])

    for block in range(blocks):
        load(block, lambda copy: copy.start())
    for block in range(blocks):
        load(block, lambda copy: copy.wait())
        store(block).start()
    for block in range(blocks):
        store(block).wait()


def place_rows(info, own, mirror, row_blocks):
    width = own.shape[-1]
    shape = (row_blocks, BLOCK, width)
    return pl.pallas_call(
        functools.partial(place_kernel, own.shape[0]),
        grid_spec=pltpu.PrefetchScalarGridSpec(
            num_scalar_prefetch=1,
            grid=(1,),
            in_specs=[ANY, ANY],
            out_specs=ANY,
            scratch_shapes=[pltpu.VMEM(shape, BF16), pltpu.SemaphoreType.DMA((2, row_blocks))],
        ),
        out_shape=pltpu.HBM(shape, BF16),
        compiler_params=pltpu.CompilerParams(vmem_limit_bytes=16 * MB),
        name="place_rows",
    )(info, own, mirror)


def halo(cut_rows):
    count = lax.axis_size("dom")
    forward = [(i, i + 1) for i in range(count - 1)]
    backward = [(target, source) for source, target in forward]
    low = lax.ppermute(cut_rows, "dom", forward)
    high = lax.ppermute(cut_rows, "dom", backward)
    return low, high


def exchange(blocks, half):
    groups = [list(range(half)), list(range(half, 2 * half))]
    return lax.all_to_all(
        blocks, "head", split_axis=0, concat_axis=0, axis_index_groups=groups, tiled=True
    )


def across(array, half):
    return lax.ppermute(array, "head", [(i, (i + half) % (2 * half)) for i in range(2 * half)])


def after(array, *tokens, anywhere=False):
    shape = jax.ShapeDtypeStruct(array.shape, array.dtype)
    return pl.pallas_call(
        lambda *refs: None,
        in_specs=[ANY] * (1 + len(tokens)),
        out_specs=ANY,
        out_shape=shape if anywhere else pltpu.HBM(array.shape, array.dtype),
        input_output_aliases={0: 0},
        compiler_params=pltpu.CompilerParams(vmem_limit_bytes=4 * MB),
        name="after",
    )(array if anywhere else hbm(array), *tokens)


def swap(array, bit):
    count = lax.axis_size("dom")
    return lax.ppermute(array, "dom", [(i, i ^ (1 << bit)) for i in range(count)])


def spread_over_dom(shard, token):
    pieces = [shard]
    owners = [lax.axis_index("dom").astype(jnp.int32)]
    for bit in reversed(range(lax.axis_size("dom").bit_length() - 1)):
        pieces = pieces if bit else [after(piece, token, anywhere=True) for piece in pieces]
        pieces += [swap(piece, bit) for piece in pieces]
        owners += [owner ^ (1 << bit) for owner in owners]
    return [(piece[None], 0, [owner]) for piece, owner in zip(pieces, owners)]


def merge_kernel(tokens, bit_ref, keep_ref, got_ref, *refs):
    send_ref, kept_ref, mark_ref = refs[tokens:]
    bit = bit_ref[0]
    mark_ref[...] = jnp.zeros_like(mark_ref)
    for layer in range(send_ref.shape[0]):
        for j in range(kept_ref.shape[1]):
            for out_ref, at in ((kept_ref, 2 * j + bit), (send_ref, 2 * j + 1 - bit)):
                keep = keep_ref[layer, at].astype(F32)
                out_ref[layer, j] = (keep + got_ref[layer, at].astype(F32)).astype(BF16)


def merge(keep, got, bit, tokens):
    layers, count, depth, width = keep.shape
    mine = (lax.axis_index("dom").astype(jnp.int32) >> bit) & 1
    shape = (layers, count // 2, depth, width)
    return pl.pallas_call(
        functools.partial(merge_kernel, len(tokens)),
        grid_spec=pltpu.PrefetchScalarGridSpec(
            num_scalar_prefetch=1,
            grid=(1,),
            in_specs=[IN_VMEM, IN_VMEM] + [ANY] * len(tokens),
            out_specs=[IN_VMEM] * 3,
        ),
        out_shape=[pltpu.VMEM(shape, BF16)] * 2 + [jax.ShapeDtypeStruct((8, LANES), F32)],
        compiler_params=pltpu.CompilerParams(vmem_limit_bytes=16 * MB),
        name="merge_shares",
    )(mine.reshape(1), vmem(keep), vmem(got), *tokens)


def sum_over_dom(keep, got, *tokens):
    bits = lax.axis_size("dom").bit_length() - 1
    for bit in range(1, bits):
        send, keep, mark = merge(keep, got, bit, tokens)
        got = swap(send, bit)
    return keep[:, 0], got[:, 0], mark


def add_kernel(keep_ref, got_ref, *refs):
    refs[-1][...] = (keep_ref[...].astype(F32) + got_ref[...].astype(F32)).astype(BF16)


def add(keep, got, *tokens):
    return pl.pallas_call(
        add_kernel,
        in_specs=[IN_VMEM, IN_VMEM] + [ANY] * len(tokens),
        out_specs=IN_VMEM,
        out_shape=pltpu.VMEM(keep.shape, BF16),
        compiler_params=pltpu.CompilerParams(vmem_limit_bytes=16 * MB),
        name="add_shares",
    )(keep, got, *tokens)


def total_kernel(keep_ref, got_ref, far_ref, *refs):
    total = keep_ref[...].astype(F32) + got_ref[...].astype(F32) + far_ref[...].astype(F32)
    refs[-1][...] = total


def total(keep, got, far, *tokens):
    layers, depth, width = keep.shape
    block = pl.BlockSpec((1, depth, width), lambda t: (t, 0, 0))
    return pl.pallas_call(
        total_kernel,
        grid=(layers,),
        in_specs=[block] * 3 + [ANY] * len(tokens),
        out_specs=block,
        out_shape=pltpu.HBM(keep.shape, F32),
        compiler_params=pltpu.CompilerParams(vmem_limit_bytes=16 * MB),
        name="total_shares",
    )(keep, got, far, *map(hbm, tokens))


def body(atoms, bonds, triplets, halo_ids, counts, enc_weight, gate_gain, head_weight):
    atom_rows = atoms[0]
    row_count, width = atom_rows.shape
    row_blocks = row_count // BLOCK
    half = lax.axis_size("head") // 2

    count = lax.axis_size("dom")

    gathered = lax.all_gather(head_weight[0], "dom", axis=0, tiled=False)
    own_parts = [(hbm(gathered), 0, [jnp.int32(i) for i in range(count)])]
    far = across(head_weight, half)[0]
    low, high = halo(pick_rows(atom_rows, halo_ids))
    extended = row_count + 2 * low.shape[0]
    codes = ((triplets[0] // LANES) * extended + bonds[0]).reshape(-1)
    pairs = lax.optimization_barrier(bonds[0] * LANES + triplets[0] % LANES).T
    place = lax.axis_index("head").astype(jnp.int32).reshape(1, 1)
    info = jnp.concatenate([counts, place], axis=1)
    own_blocks, mirror_blocks = encode(
        info, codes, atom_rows, low, high, enc_weight, gate_gain[None, :], pairs, half
    )
    near = after(far, hbm(own_blocks), anywhere=True)
    mirror_rows = exchange(after(mirror_blocks, near, hbm(gathered)), half)
    mirror_parts = spread_over_dom(near, mirror_rows)
    own_rows = exchange(after(own_blocks, mirror_rows), half)

    scale = 1.0 / math.sqrt(count * row_count)
    back, send, keep = run_head(mirror_rows, mirror_parts, scale, "head_mirror")
    got = swap(send, 0)
    mirror_keep, mirror_got, sent = sum_over_dom(keep, got)
    mirror_back = exchange(after(back, sent), half)

    back, send, keep = run_head(own_rows, own_parts, scale, "head_own", sent)
    mirror_sum = add(mirror_keep, mirror_got, send)
    far_sum = across(mirror_sum, half)
    own_back = exchange(after(back, mirror_sum), half)
    own_keep, own_got, _ = sum_over_dom(keep, swap(send, 0), mirror_sum)
    row_part = place_rows(info, own_back, mirror_back, row_blocks)
    head_part = total(own_keep, own_got, far_sum, row_part)
    return row_part.reshape(1, row_count, width), head_part[None]


def solution(mesh):
    return jax.shard_map(
        body,
        mesh=mesh,
        in_specs=(
            P("dom", "head", None),
            P("dom", None, "head"),
            P("dom", None, "head"),
            P("dom", "head"),
            P("dom", "head"),
            P(),
            P(),
            P("head", None, "dom", None),
        ),
        out_specs=(P("dom", "head", None), P("head", None, "dom", None)),
        check_vma=False,
    )
```

```python
import functools
import math

import jax
import jax.numpy as jnp
from jax import lax
from jax.experimental import pallas as pl
from jax.experimental.pallas import tpu as pltpu
from jax.sharding import PartitionSpec as P

BLOCK = 128
LANES = 128
MB = 1 << 20
VMEM = 58 * MB
F32 = jnp.float32
BF16 = jnp.bfloat16
ANY = pl.BlockSpec(memory_space=pl.ANY)
IN_VMEM = pl.BlockSpec(memory_space=pltpu.VMEM)


def sigmoid(x):
    return 0.5 + 0.5 * jnp.tanh(0.5 * x)


def hbm(array):
    return pltpu.with_memory_space_constraint(array, pltpu.HBM)


def vmem(array):
    return pltpu.with_memory_space_constraint(array, pltpu.VMEM)


def resident(shape):
    return pl.BlockSpec(shape, lambda *_: (0,) * len(shape))


def pick_kernel(ids_ref, rows_ref, out_ref):
    count, total = out_ref.shape[0], rows_ref.shape[0]
    places = lax.broadcasted_iota(jnp.int32, (total, count), 0)
    ones = jnp.where(places == ids_ref[...], 1.0, 0.0).astype(BF16)
    out_ref[...] = lax.dot_general(
        ones, rows_ref[...], (((0,), (0,)), ((), ())), preferred_element_type=F32
    ).astype(BF16)


def pick_rows(rows, ids):
    return pl.pallas_call(
        pick_kernel,
        in_specs=[IN_VMEM, IN_VMEM],
        out_specs=IN_VMEM,
        out_shape=jax.ShapeDtypeStruct((ids.shape[1], rows.shape[1]), rows.dtype),
        compiler_params=pltpu.CompilerParams(vmem_limit_bytes=16 * MB),
        name="pick_rows",
    )(ids, rows)


def block_place(info_ref, block):
    sets = info_ref.shape[1] - 1
    start, dataset, rank = jnp.int32(0), jnp.int32(0), jnp.int32(0)
    for candidate in range(sets):
        blocks = info_ref[0, candidate] // BLOCK
        inside = jnp.logical_and(block >= start, block < start + blocks)
        dataset = jnp.where(inside, candidate, dataset)
        rank = jnp.where(inside, block - start, rank)
        start = start + blocks
    return dataset, rank, info_ref[0, sets]


def encode_kernel(
    half, batch, info_ref, codes_ref, atoms_ref, low_ref, high_ref, weight_ref, gain_ref,
    pairs_ref, own_ref, mirror_ref, gained, scores, partial, wanted, gates, gate_rows, staged,
    zeros, weight, sems, weight_sem,
):
    rows, width = atoms_ref.shape
    depth = low_ref.shape[0]
    bond_count = pairs_ref.shape[1]
    sets = 2 * half
    weight_in = pltpu.make_async_copy(weight_ref, weight, weight_sem)
    weight_in.start()
    home = info_ref[0, sets] // half * half
    tile = batch * BLOCK

    def leave(source, slot, act):
        def one(ref, at):
            act(pltpu.make_async_copy(source, ref.at[at], sems.at[slot]))

        pl.when(slot < sets)(lambda: one(own_ref, slot))
        pl.when(slot >= sets)(lambda: one(mirror_ref, slot - sets))

    zeros[...] = jnp.zeros_like(zeros)

    def blank(slot, carry):
        dataset = lax.rem(home + slot // 2, sets)
        empty = info_ref[0, dataset] // BLOCK <= lax.rem(slot, 2)
        pl.when(empty)(lambda: leave(zeros, slot, lambda copy: copy.start()))
        return carry

    lax.fori_loop(0, 2 * sets, blank, 0)

    extended = rows + 2 * depth
    parts = ((atoms_ref, 0), (low_ref, rows), (high_ref, rows + depth))
    for ref, at in parts:
        gained[at : at + ref.shape[0], :] = (ref[...].astype(F32) * gain_ref[...]).astype(BF16)
    for ref, base in parts:
        step = min(ref.shape[0], 2 * LANES)
        for at in range(0, ref.shape[0], step):
            value = lax.dot_general(
                gained[...], ref[at : at + step, :], (((1,), (1,)), ((), ())),
                preferred_element_type=F32,
            )
            for k in range(0, step, LANES):
                piece = (base + at + k) // LANES
                scores[piece * extended : (piece + 1) * extended, :] = value[:, k : k + LANES]

    def encode_tile(step, carry):
        base = pl.multiple_of(step * tile, tile)

        eight = lax.broadcasted_iota(jnp.int32, (8, LANES), 0)

        def score(group, carry):
            for bond in range(bond_count):
                at = bond * rows + base + group * 8
                place = pl.multiple_of(bond * tile + group * 8, 8)
                found = scores[pl.ds(codes_ref[at], 8, stride=0), :]
                for j in range(1, 8):
                    row = scores[pl.ds(codes_ref[at + j], 8, stride=0), :]
                    found = jnp.where(eight == j, row, found)
                partial[pl.ds(place, 8), :] = found
            return carry

        lax.fori_loop(0, tile // 8, score, 0, unroll=4)
        places = lax.broadcasted_iota(jnp.int32, (BLOCK, LANES), 1)
        for block in range(batch):
            pairs = pairs_ref[pl.ds(base + block * BLOCK, BLOCK), :]
            for bond in range(bond_count):
                at = bond * tile + block * BLOCK
                pair = jnp.broadcast_to(pairs[:, bond : bond + 1], (BLOCK, LANES))
                wanted[bond] = pair // LANES
                picked = places == pair % LANES
                logits = jnp.sum(
                    jnp.where(picked, partial[at : at + BLOCK, :], 0.0), axis=1, keepdims=True
                )
                gate = sigmoid(logits * (1.0 / math.sqrt(width)))
                gates[bond] = jnp.broadcast_to(gate, (BLOCK, LANES))
            for at in range(0, extended, LANES):
                acc = jnp.zeros((BLOCK, LANES), F32)
                for bond in range(bond_count):
                    acc = acc + jnp.where(wanted[bond] == places + at, gates[bond], 0.0)
                gate_rows[block * BLOCK : (block + 1) * BLOCK, at : at + LANES] = acc.astype(BF16)
        message = jnp.dot(gate_rows[:, :rows], atoms_ref[...], preferred_element_type=F32)
        for ref, at in ((low_ref, rows), (high_ref, rows + depth)):
            message += jnp.dot(
                gate_rows[:, at : at + depth], ref[...], preferred_element_type=F32
            )
        pl.when(step == 0)(lambda: weight_in.wait())
        update = jnp.dot(message.astype(BF16), weight[...], preferred_element_type=F32)
        own = atoms_ref[pl.ds(base, tile), :].astype(F32)
        staged[step] = (own + update * sigmoid(update)).astype(BF16).reshape(staged.shape[1:])
        for block in range(batch):
            dataset, rank, _ = block_place(info_ref, step * batch + block)
            slot = lax.rem(dataset - home + sets, sets) * 2 + rank
            leave(staged.at[step, block], slot, lambda copy: copy.start())
        return carry

    lax.fori_loop(0, rows // tile, encode_tile, 0)

    def settle(slot, carry):
        leave(zeros, slot, lambda copy: copy.wait())
        return carry

    lax.fori_loop(0, 2 * sets, settle, 0)


def encode(info, codes, atoms, low, high, weight, gain, pairs, half):
    rows, width = atoms.shape
    extended = rows + 2 * low.shape[0]
    bond_count = pairs.shape[1]
    slots = 4 * half
    row_blocks = rows // BLOCK
    batch = 4 if row_blocks % 4 == 0 else 1
    blocks = pl.pallas_call(
        functools.partial(encode_kernel, half, batch),
        grid_spec=pltpu.PrefetchScalarGridSpec(
            num_scalar_prefetch=2,
            grid=(1,),
            in_specs=[IN_VMEM] * 3 + [ANY] + [IN_VMEM] * 2,
            out_specs=[pl.BlockSpec(memory_space=pltpu.HBM)] * 2,
            scratch_shapes=[
                pltpu.VMEM((extended, width), BF16),
                pltpu.VMEM((extended // LANES * extended, LANES), F32),
                pltpu.VMEM((batch * BLOCK * bond_count, LANES), F32),
                pltpu.VMEM((bond_count, BLOCK, LANES), jnp.int32),
                pltpu.VMEM((bond_count, BLOCK, LANES), F32),
                pltpu.VMEM((batch * BLOCK, extended), BF16),
                pltpu.VMEM((row_blocks // batch, batch, BLOCK, width), BF16),
                pltpu.VMEM((BLOCK, width), BF16),
                pltpu.VMEM((width, width), BF16),
                pltpu.SemaphoreType.DMA((slots,)),
                pltpu.SemaphoreType.DMA(()),
            ],
        ),
        out_shape=[pltpu.HBM((2 * half, BLOCK, width), BF16)] * 2,
        compiler_params=pltpu.CompilerParams(vmem_limit_bytes=44 * MB),
        cost_estimate=pl.CostEstimate(
            flops=3 * rows * width * width,
            bytes_accessed=10 * MB,
            transcendentals=rows * width,
        ),
        name="encode_rows",
    )(info, codes, atoms, low, high, hbm(weight), gain, pairs)
    return [rows.reshape(half, 2, BLOCK, width) for rows in blocks]


def head_kernel(scale, offsets, tokens, table_ref, rows_ref, *refs):
    part_count = len(offsets)
    weight_refs = refs[:part_count]
    (
        back_ref, send_ref, keep_ref, x, weights, act, slope, err, grad, back, shares,
        in_sems, weight_sems, back_sems,
    ) = refs[part_count + tokens :]
    width = x.shape[-1]
    tile = x.shape[1] * x.shape[2]
    count = weights.shape[1]
    chunk = width // 2
    chunks = [slice(at, at + chunk) for at in range(0, width, chunk)]
    transposed = (((1,), (1,)), ((), ()))
    over_rows = (((0,), (0,)), ((), ()))
    bit = table_ref[0]

    def rows_in(rank):
        return pltpu.make_async_copy(rows_ref.at[:, rank], x.at[rank], in_sems.at[rank])

    def weights_in(layer):
        copies = []
        for ref, at in zip(weight_refs, offsets):
            for i in range(ref.shape[0]):
                owner = table_ref[1 + len(copies)]
                place = weights.at[layer, owner, pl.ds(at, ref.shape[2])]
                sem = weight_sems.at[layer, len(copies)]
                copies.append(pltpu.make_async_copy(ref.at[i, layer], place, sem))
        return copies

    def back_out(rank):
        return pltpu.make_async_copy(back.at[rank], back_ref.at[:, rank], back_sems.at[rank])

    def matrix(layer):
        return weights[layer].reshape(width, width)

    def forward(rank, wait):
        inputs = x[rank].reshape(tile, width)
        low = matrix(0)
        for at in chunks:
            z = jnp.dot(inputs, low[:, at], preferred_element_type=F32)
            s = sigmoid(z)
            act[rank * tile : (rank + 1) * tile, at] = (z * s).astype(BF16)
            slope[rank, :, at] = s * (1.0 + z * (1.0 - s))
        if wait:
            for copy in weights_in(1):
                copy.wait()
        acts = act[rank * tile : (rank + 1) * tile, :]
        high = matrix(1)
        for at in chunks:
            value = jnp.dot(acts, high[:, at], preferred_element_type=F32)
            value = value - inputs[:, at].astype(F32)
            err[rank, :, at] = value
            grad[1, rank * tile : (rank + 1) * tile, at] = value.astype(BF16)

    def backward(rank):
        rows = slice(rank * tile, (rank + 1) * tile)
        grads = grad[1, rows, :]
        high = matrix(1)
        for at in chunks:
            up = lax.dot_general(grads, high[at, :], transposed, preferred_element_type=F32)
            grad[0, rows, at] = (up * slope[rank, :, at]).astype(BF16)
        grads = grad[0, rows, :]
        low = matrix(0)
        shape = x.shape[1:3] + (chunk,)
        for at in chunks:
            up = lax.dot_general(grads, low[at, :], transposed, preferred_element_type=F32)
            back[rank, :, :, at] = (up - err[rank, :, at]).astype(BF16).reshape(shape)

    def share(layer, acts, rows):
        value = lax.dot_general(
            acts, grad[layer, :rows, :], over_rows, preferred_element_type=F32
        )
        shares[...] = (value * scale).astype(BF16).reshape(shares.shape)
        for j in range(count // 2):
            keep_ref[layer, j] = shares[2 * j + bit]
            send_ref[layer, j] = shares[2 * j + 1 - bit]

    for rank in range(2):
        rows_in(rank).start()
    for layer in range(2):
        for copy in weights_in(layer):
            copy.start()
    rows_in(0).wait()
    for copy in weights_in(0):
        copy.wait()
    forward(0, True)
    rows_in(1).wait()
    some = jnp.max(jnp.abs(x[1].reshape(tile, width).astype(F32))) > 0
    none = jnp.logical_not(some)
    pl.when(some)(lambda: forward(1, False))
    pl.when(some)(lambda: share(1, act[...], 2 * tile))
    pl.when(none)(lambda: share(1, act[:tile, :], tile))
    backward(0)
    back_out(0).start()
    pl.when(some)(lambda: backward(1))

    @pl.when(none)
    def _():
        back[1] = jnp.zeros(back.shape[1:], BF16)

    back_out(1).start()
    pl.when(some)(lambda: share(0, x[...].reshape(2 * tile, width), 2 * tile))
    pl.when(none)(lambda: share(0, x[0].reshape(tile, width), tile))
    for rank in range(2):
        back_out(rank).wait()


def run_head(rows, parts, scale, name, *tokens):
    sources, ranks, _, width = rows.shape
    count = lax.axis_size("dom")
    arrays, offsets, owners = zip(*parts)
    owners = [owner for group in owners for owner in group]
    depth = width // count
    layers = 2
    tile = sources * BLOCK
    total = ranks * tile
    part = (layers, count // 2, depth, width)
    bit = lax.axis_index("dom").astype(jnp.int32) & 1
    return pl.pallas_call(
        functools.partial(head_kernel, scale, offsets, len(tokens)),
        grid_spec=pltpu.PrefetchScalarGridSpec(
            num_scalar_prefetch=1,
            grid=(1,),
            in_specs=[ANY] * (1 + len(parts) + len(tokens)),
            out_specs=[ANY, IN_VMEM, IN_VMEM],
            scratch_shapes=[
                pltpu.VMEM((ranks, sources, BLOCK, width), BF16),
                pltpu.VMEM((layers, count, depth, width), BF16),
                pltpu.VMEM((total, width), BF16),
                pltpu.VMEM((ranks, tile, width), F32),
                pltpu.VMEM((ranks, tile, width), F32),
                pltpu.VMEM((layers, total, width), BF16),
                pltpu.VMEM((ranks, sources, BLOCK, width), BF16),
                pltpu.VMEM((count, depth, width), BF16),
                pltpu.SemaphoreType.DMA((ranks,)),
                pltpu.SemaphoreType.DMA((layers, len(owners))),
                pltpu.SemaphoreType.DMA((ranks,)),
            ],
        ),
        out_shape=[pltpu.HBM(rows.shape, BF16)] + [pltpu.VMEM(part, BF16)] * 2,
        compiler_params=pltpu.CompilerParams(vmem_limit_bytes=(20 + 28 * tile // 1024) * MB),
        cost_estimate=pl.CostEstimate(
            flops=24 * total * width * width,
            bytes_accessed=5 * total * width * 2 + width * width * 4,
            transcendentals=total * width,
        ),
        name=name,
    )(jnp.stack([bit] + owners), rows, *arrays, *tokens)


def place_kernel(half, info_ref, own_ref, mirror_ref, out_ref, held, sems):
    blocks = out_ref.shape[0]

    def load(block, act):
        dataset, rank, place = block_place(info_ref, block)
        is_own = dataset // half == place // half

        def one(ref):
            source = ref.at[lax.rem(dataset, half), rank]
            act(pltpu.make_async_copy(source, held.at[block], sems.at[0, block]))

        pl.when(is_own)(lambda: one(own_ref))
        pl.when(jnp.logical_not(is_own))(lambda: one(mirror_ref))

    def store(block):
        return pltpu.make_async_copy(held.at[block], out_ref.at[block], sems.at[1, block])

    for block in range(blocks):
        load(block, lambda copy: copy.start())
    for block in range(blocks):
        load(block, lambda copy: copy.wait())
        store(block).start()
    for block in range(blocks):
        store(block).wait()


def place_rows(info, own, mirror, row_blocks):
    width = own.shape[-1]
    shape = (row_blocks, BLOCK, width)
    return pl.pallas_call(
        functools.partial(place_kernel, own.shape[0]),
        grid_spec=pltpu.PrefetchScalarGridSpec(
            num_scalar_prefetch=1,
            grid=(1,),
            in_specs=[ANY, ANY],
            out_specs=ANY,
            scratch_shapes=[pltpu.VMEM(shape, BF16), pltpu.SemaphoreType.DMA((2, row_blocks))],
        ),
        out_shape=pltpu.HBM(shape, BF16),
        compiler_params=pltpu.CompilerParams(vmem_limit_bytes=16 * MB),
        name="place_rows",
    )(info, own, mirror)


def halo(cut_rows):
    count = lax.axis_size("dom")
    forward = [(i, i + 1) for i in range(count - 1)]
    backward = [(target, source) for source, target in forward]
    low = lax.ppermute(cut_rows, "dom", forward)
    high = lax.ppermute(cut_rows, "dom", backward)
    return low, high


def exchange(blocks, half):
    groups = [list(range(half)), list(range(half, 2 * half))]
    return lax.all_to_all(
        blocks, "head", split_axis=0, concat_axis=0, axis_index_groups=groups, tiled=True
    )


def across(array, half):
    return lax.ppermute(array, "head", [(i, (i + half) % (2 * half)) for i in range(2 * half)])


def after(array, *tokens, anywhere=False):
    shape = jax.ShapeDtypeStruct(array.shape, array.dtype)
    return pl.pallas_call(
        lambda *refs: None,
        in_specs=[ANY] * (1 + len(tokens)),
        out_specs=ANY,
        out_shape=shape if anywhere else pltpu.HBM(array.shape, array.dtype),
        input_output_aliases={0: 0},
        compiler_params=pltpu.CompilerParams(vmem_limit_bytes=4 * MB),
        name="after",
    )(array if anywhere else hbm(array), *tokens)


def swap(array, bit):
    count = lax.axis_size("dom")
    return lax.ppermute(array, "dom", [(i, i ^ (1 << bit)) for i in range(count)])


def spread_over_dom(shard, token):
    pieces = [shard]
    owners = [lax.axis_index("dom").astype(jnp.int32)]
    for bit in reversed(range(lax.axis_size("dom").bit_length() - 1)):
        pieces = pieces if bit else [after(piece, token, anywhere=True) for piece in pieces]
        pieces += [swap(piece, bit) for piece in pieces]
        owners += [owner ^ (1 << bit) for owner in owners]
    return [(piece[None], 0, [owner]) for piece, owner in zip(pieces, owners)]


def merge_kernel(tokens, bit_ref, keep_ref, got_ref, *refs):
    send_ref, kept_ref, mark_ref = refs[tokens:]
    bit = bit_ref[0]
    mark_ref[...] = jnp.zeros_like(mark_ref)
    for layer in range(send_ref.shape[0]):
        for j in range(kept_ref.shape[1]):
            for out_ref, at in ((kept_ref, 2 * j + bit), (send_ref, 2 * j + 1 - bit)):
                keep = keep_ref[layer, at].astype(F32)
                out_ref[layer, j] = (keep + got_ref[layer, at].astype(F32)).astype(BF16)


def merge(keep, got, bit, tokens):
    layers, count, depth, width = keep.shape
    mine = (lax.axis_index("dom").astype(jnp.int32) >> bit) & 1
    shape = (layers, count // 2, depth, width)
    return pl.pallas_call(
        functools.partial(merge_kernel, len(tokens)),
        grid_spec=pltpu.PrefetchScalarGridSpec(
            num_scalar_prefetch=1,
            grid=(1,),
            in_specs=[IN_VMEM, IN_VMEM] + [ANY] * len(tokens),
            out_specs=[IN_VMEM] * 3,
        ),
        out_shape=[pltpu.VMEM(shape, BF16)] * 2 + [jax.ShapeDtypeStruct((8, LANES), F32)],
        compiler_params=pltpu.CompilerParams(vmem_limit_bytes=16 * MB),
        name="merge_shares",
    )(mine.reshape(1), vmem(keep), vmem(got), *tokens)


def sum_over_dom(keep, got, *tokens):
    bits = lax.axis_size("dom").bit_length() - 1
    for bit in range(1, bits):
        send, keep, mark = merge(keep, got, bit, tokens)
        got = swap(send, bit)
    return keep[:, 0], got[:, 0], mark


def add_kernel(keep_ref, got_ref, *refs):
    refs[-1][...] = (keep_ref[...].astype(F32) + got_ref[...].astype(F32)).astype(BF16)


def add(keep, got, *tokens):
    return pl.pallas_call(
        add_kernel,
        in_specs=[IN_VMEM, IN_VMEM] + [ANY] * len(tokens),
        out_specs=IN_VMEM,
        out_shape=pltpu.VMEM(keep.shape, BF16),
        compiler_params=pltpu.CompilerParams(vmem_limit_bytes=16 * MB),
        name="add_shares",
    )(keep, got, *tokens)


def total_kernel(keep_ref, got_ref, far_ref, *refs):
    total = keep_ref[...].astype(F32) + got_ref[...].astype(F32) + far_ref[...].astype(F32)
    refs[-1][...] = total


def total(keep, got, far, *tokens):
    layers, depth, width = keep.shape
    block = pl.BlockSpec((1, depth, width), lambda t: (t, 0, 0))
    return pl.pallas_call(
        total_kernel,
        grid=(layers,),
        in_specs=[block] * 3 + [ANY] * len(tokens),
        out_specs=block,
        out_shape=pltpu.HBM(keep.shape, F32),
        compiler_params=pltpu.CompilerParams(vmem_limit_bytes=16 * MB),
        name="total_shares",
    )(keep, got, far, *map(hbm, tokens))


def body(atoms, bonds, triplets, halo_ids, counts, enc_weight, gate_gain, head_weight):
    atom_rows = atoms[0]
    row_count, width = atom_rows.shape
    row_blocks = row_count // BLOCK
    half = lax.axis_size("head") // 2

    count = lax.axis_size("dom")

    gathered = lax.all_gather(head_weight[0], "dom", axis=0, tiled=False)
    own_parts = [(hbm(gathered), 0, [jnp.int32(i) for i in range(count)])]
    far = across(head_weight, half)[0]
    low, high = halo(pick_rows(atom_rows, halo_ids))
    extended = row_count + 2 * low.shape[0]
    codes = ((triplets[0] // LANES) * extended + bonds[0]).reshape(-1)
    pairs = lax.optimization_barrier(bonds[0] * LANES + triplets[0] % LANES).T
    place = lax.axis_index("head").astype(jnp.int32).reshape(1, 1)
    info = jnp.concatenate([counts, place], axis=1)
    own_blocks, mirror_blocks = encode(
        info, codes, atom_rows, low, high, enc_weight, gate_gain[None, :], pairs, half
    )
    near = after(far, hbm(own_blocks), anywhere=True)
    mirror_rows = exchange(after(mirror_blocks, near, hbm(gathered)), half)
    mirror_parts = spread_over_dom(near, mirror_rows)
    own_rows = exchange(after(own_blocks, mirror_rows), half)

    scale = 1.0 / math.sqrt(count * row_count)
    back, send, keep = run_head(mirror_rows, mirror_parts, scale, "head_mirror")
    got = swap(send, 0)
    mirror_keep, mirror_got, sent = sum_over_dom(keep, got)
    mirror_back = exchange(after(back, sent), half)

    back, send, keep = run_head(own_rows, own_parts, scale, "head_own", sent)
    mirror_sum = add(mirror_keep, mirror_got, send)
    far_sum = across(mirror_sum, half)
    own_back = exchange(after(back, mirror_sum), half)
    own_keep, own_got, _ = sum_over_dom(keep, swap(send, 0), mirror_sum)
    row_part = place_rows(info, own_back, mirror_back, row_blocks)
    head_part = total(own_keep, own_got, far_sum, row_part)
    return row_part.reshape(1, row_count, width), head_part[None]


def solution(mesh):
    return jax.shard_map(
        body,
        mesh=mesh,
        in_specs=(
            P("dom", "head", None),
            P("dom", None, "head"),
            P("dom", None, "head"),
            P("dom", "head"),
            P("dom", "head"),
            P(),
            P(),
            P("head", None, "dom", None),
        ),
        out_specs=(P("dom", "head", None), P("head", None, "dom", None)),
        check_vma=False,
    )
```
